32 devices in a mesh: prow: 4 (over z), pcol: 8 (over y, x, core).
Axes of the slice: x: 2, y: 2, z: 4, core: 2. Of those that a mesh axis runs over, the one named last changes fastest.
Arguments:
- slab: float32 [256, 50176], P('pcol', 'prow'), may hold values from -6 to 6
- reflectors: float32 [2, 128, 50176], P(None, 'pcol', 'prow'), may hold values from -6 to 6
- factors: float32 [2, 128, 128], P(None, 'pcol'), as said below
Outputs:
- result: float32 [256, 50176], P('pcol', 'prow')
The draws below stay inside these ranges and needn't reach their ends.
Inputs may be any that keep to these rules, and one draw needn't show every extreme that they name: factors[p] is upper triangular with a positive diagonal.
All inputs are finite; a program needn't handle non-finite values.
Results may differ from the reference program's by a relative error of at most 0.00013.
Values sent between devices are 32-bit elements; how exact they have to be, the bound alone decides.
No kernel may reach another device: no remote copies, remote signals or barrier semaphores. Data moves between devices by JAX's collectives and lax.ppermute only.
A program may use at most 128 MiB of HBM per device.

```python
import math
import jax
import jax.numpy as jnp
from jax import lax

NB = 128
PANELS = 2
ORDER = 50176
SLAB = 256


def draw_factors(key, part):
    first_key, second_key = jax.random.split(jax.random.fold_in(key, 17))
    unit = 0.3 / math.sqrt(NB * ORDER)
    diagonal = jax.random.uniform(first_key, (PANELS, NB), jnp.float32, 1.0, 2.0)
    upper = jax.random.normal(second_key, (PANELS, NB, NB), jnp.float32) * 0.1
    whole = jnp.triu(upper, 1) + diagonal[:, :, None] * jnp.eye(NB, dtype=jnp.float32)[None, :, :]
    return whole * unit


def levels(own_key, shape, cuts, smallest, high):
    factor_of, own = 1.0, jax.random.fold_in(own_key, 6)
    for axis_at, shards_of in cuts:
        heights = jnp.exp(jax.random.uniform(jax.random.fold_in(own, axis_at), (shards_of,), jnp.float32, smallest / len(cuts), high / len(cuts)))
        factor_of = factor_of * jnp.repeat(heights, shape[axis_at] // shards_of).reshape([-1 if axis == axis_at else 1 for axis in range(len(shape))])
    return factor_of


def scatter_about(own_key, shape, scale, limit, pieces=(), kind=jnp.bfloat16):
    loudness = levels(own_key, shape, pieces, -0.22, 0.18) if pieces else 1.0
    drawn = jax.random.normal(own_key, shape, jnp.float32) * scale * loudness
    return jnp.minimum(jnp.maximum(drawn, -limit), limit).astype(kind)


def setup_inputs(seed: int = 0) -> dict:
    splits = jax.random.split(jax.random.key(seed), 4)
    slab = scatter_about(splits[0], (SLAB, ORDER), 1.0, 6.0, ((0, 8), (1, 4)), jnp.float32)
    reflectors = scatter_about(splits[1], (PANELS, NB, ORDER), 1.0, 6.0, ((1, 8), (2, 4)), jnp.float32)
    factors = draw_factors(jax.random.fold_in(splits[3], 71), 0)
    return dict(slab=slab, reflectors=reflectors, factors=factors)


def reference(slab, reflectors, factors):
    current = slab
    for panel_index in range(PANELS):
        vectors = reflectors[panel_index]
        inner = jnp.dot(current, vectors.T, precision=lax.Precision.HIGHEST, preferred_element_type=jnp.float32)
        scaled = jnp.dot(inner, factors[panel_index].T, precision=lax.Precision.HIGHEST, preferred_element_type=jnp.float32)
        current = current - jnp.dot(scaled, vectors, precision=lax.Precision.HIGHEST, preferred_element_type=jnp.float32)
    return current
```

```python
import functools

import jax
import jax.numpy as jnp
from jax import lax
from jax.experimental import pallas as pl
from jax.experimental.pallas import tpu as pltpu
from jax.sharding import PartitionSpec as P

TILE_LIMIT = 2048
VMEM_LIMIT = 48 * 1024 * 1024
ROWS = (((1,), (1,)), ((), ()))
PLAIN = (((1,), (0,)), ((), ()))


def tile_of(width):
    best = width
    for unit in (256, 128):
        fits = [t for t in range(unit, TILE_LIMIT + 1, unit) if width % t == 0]
        if fits:
            best = max(fits)
            break
    return best


def split(value):
    high = value.astype(jnp.bfloat16)
    return high, (value - high.astype(jnp.float32)).astype(jnp.bfloat16)


def dot3(left, right, dims):
    (lh, ll), (rh, rl) = left, right
    dot = functools.partial(lax.dot_general, dimension_numbers=dims, preferred_element_type=jnp.float32)
    return dot(lh, rh) + (dot(lh, rl) + dot(ll, rh))


def exact(left, right, dims):
    return lax.dot_general(left, right, dims, precision=lax.Precision.HIGHEST, preferred_element_type=jnp.float32)


def panel_rows(layout, refs, panel):
    return jnp.concatenate([refs[entry[panel][0]][entry[panel][1]] for entry in layout], axis=0)


def inner_kernel(layout, slab_ref, *refs):
    vector_refs, out_ref = refs[:-1], refs[-1]
    first, second = (panel_rows(layout, vector_refs, p) for p in range(2))
    nb = first.shape[0]
    rows = slab_ref.shape[0]
    left = split(jnp.concatenate([slab_ref[...], first], axis=0))
    right = split(jnp.concatenate([first, second], axis=0))
    both = dot3(left, right, ROWS)
    packed = jnp.concatenate([both[:rows, :nb], both[:, nb:]], axis=0)

    @pl.when(pl.program_id(0) == 0)
    def _():
        out_ref[...] = packed

    @pl.when(pl.program_id(0) > 0)
    def _():
        out_ref[...] += packed


def inner_products(layout, slab, vectors, width, start, tile):
    rows, nb = slab.shape[0], sum(vectors[e[0][0]][0].shape[1] for e in layout)
    specs = [pl.BlockSpec((rows, tile), lambda i: (0, start + i))]
    for array, offset in vectors:
        specs.append(pl.BlockSpec((array.shape[0], array.shape[1], tile), functools.partial(lambda o, i: (0, 0, o + i), offset)))
    return pl.pallas_call(
        functools.partial(inner_kernel, layout),
        grid=(width // tile,),
        in_specs=specs,
        out_specs=pl.BlockSpec((2 * rows + nb, nb), lambda i: (0, 0)),
        out_shape=jax.ShapeDtypeStruct((2 * rows + nb, nb), jnp.float32),
        compiler_params=pltpu.CompilerParams(vmem_limit_bytes=VMEM_LIMIT),
        cost_estimate=pl.CostEstimate(flops=6 * (rows + nb) * 2 * nb * width, bytes_accessed=4 * (rows + 2 * nb) * width, transcendentals=0),
    )(slab, *[array for array, _ in vectors])


def update_kernel(layouts, counts, steps, *refs):
    mine_ref, other_ref, factors_ref, slab_ref = refs[:4]
    vector_refs, out_ref, high_ref, low_ref = refs[4:-3], refs[-3], refs[-2], refs[-1]
    rows = slab_ref.shape[0]
    step = pl.program_id(0)

    @pl.when(step == 0)
    def _():
        total = mine_ref[...] + other_ref[...]
        scaled = exact(total[:rows], factors_ref[0], ROWS)
        inner = total[rows : 2 * rows] - exact(scaled, total[2 * rows :], PLAIN)
        later = exact(inner, factors_ref[1], ROWS)
        high_ref[...], low_ref[...] = split(jnp.concatenate([scaled, later], axis=1))

    position = 0
    for layout, (begin, end), count in zip(layouts, steps, counts):
        part = vector_refs[position : position + count]
        position += count

        @pl.when((step >= begin) & (step < end))
        def _():
            vectors = jnp.concatenate([panel_rows(layout, part, p) for p in range(2)], axis=0)
            out_ref[...] = slab_ref[...] - dot3((high_ref[...], low_ref[...]), split(vectors), PLAIN)


def update(layouts, mine, other, factors, slab, chunks, steps, tile):
    rows, width = slab.shape
    nb = factors.shape[1]
    specs = [
        pl.BlockSpec(mine.shape, lambda i: (0, 0)),
        pl.BlockSpec(mine.shape, lambda i: (0, 0)),
        pl.BlockSpec(factors.shape, lambda i: (0, 0, 0)),
        pl.BlockSpec((rows, tile), lambda i: (0, i)),
    ]
    arrays = []
    for vectors, (begin, end) in zip(chunks, steps):
        for array, offset in vectors:
            index = functools.partial(lambda o, b, e, i: (0, 0, o + jnp.clip(i, b, e - 1) - b), offset, begin, end)
            specs.append(pl.BlockSpec((array.shape[0], array.shape[1], tile), index))
            arrays.append(array)
    return pl.pallas_call(
        functools.partial(update_kernel, layouts, [len(c) for c in chunks], steps),
        grid=(width // tile,),
        in_specs=specs,
        out_specs=pl.BlockSpec((rows, tile), lambda i: (0, i)),
        out_shape=jax.ShapeDtypeStruct(slab.shape, jnp.float32),
        scratch_shapes=[pltpu.VMEM((rows, 2 * nb), jnp.bfloat16)] * 2,
        compiler_params=pltpu.CompilerParams(vmem_limit_bytes=VMEM_LIMIT),
        cost_estimate=pl.CostEstimate(flops=6 * rows * 2 * nb * width, bytes_accessed=4 * (2 * rows + 2 * nb) * width, transcendentals=0),
    )(mine, other, factors, slab, *arrays)


def exchange(array, bit, size, axis):
    return lax.ppermute(array, axis, [(i, i ^ bit) for i in range(size)])


def gather_factors(factors, size):
    blocks = factors[:, None]
    bit = size // 2
    held = [factors]
    blocks = {0: factors}
    while bit:
        got = exchange(jnp.stack([blocks[r] for r in sorted(blocks)]), bit, size, "pcol")
        for place, r in enumerate(sorted(blocks)):
            blocks = {**blocks, r ^ bit: got[place]}
        bit //= 2
    rows = jnp.concatenate([blocks[r] for r in range(size)], axis=1)
    panels, nb, _ = rows.shape
    columns = rows.reshape(panels, nb, size, nb // size)
    me = lax.axis_index("pcol")
    bit = 1
    while bit < size:
        pairs = columns.reshape(panels, nb, size // (2 * bit), 2, bit, nb // size)
        swapped = pairs[:, :, :, ::-1].reshape(columns.shape)
        columns = jnp.where((me & bit) != 0, swapped, columns)
        bit *= 2
    return columns.reshape(rows.shape)


def gather_chunk(own, size):
    parts = {0: ((own, 0), (own, 1))}
    top, next_top = size // 2, size // 4
    if next_top >= 1:
        by_next = exchange(own, next_top, size, "pcol")
        by_top = exchange(own, top, size, "pcol")
        corner_first = exchange(by_top[:1], next_top, size, "pcol")
        corner_second = exchange(by_next[1:], top, size, "pcol")
        parts[next_top] = ((by_next, 0), (by_next, 1))
        parts[top] = ((by_top, 0), (by_top, 1))
        parts[top | next_top] = ((corner_first, 0), (corner_second, 0))
        bit = next_top // 2
    else:
        bit = top
    while bit:
        moved = {}
        for r in list(parts):
            entry = []
            for array, index in parts[r]:
                if id(array) not in moved:
                    moved[id(array)] = exchange(array, bit, size, "pcol")
                entry.append((moved[id(array)], index))
            parts[r | bit] = tuple(entry)
        bit //= 2
    return parts


def indexed(parts, size):
    arrays, places, layout = [], {}, []
    for r in range(size):
        entry = []
        for array, index in parts[r]:
            if id(array) not in places:
                places[id(array)] = len(arrays)
                arrays.append(array)
            entry.append((places[id(array)], index))
        layout.append(tuple(entry))
    return arrays, layout


def body(sizes, slab, reflectors, factors):
    size, depth = sizes["pcol"], sizes["prow"]
    width = slab.shape[1]
    tile = tile_of(width)
    tiles = width // tile
    cut = (tiles + 1) // 2
    steps = [(0, cut), (cut, tiles)] if tiles > 1 else [(0, tiles)]
    triangles = gather_factors(factors, size)
    chunks, layouts, total = [], [], None
    for begin, end in steps:
        own = reflectors[:, :, begin * tile : end * tile]
        arrays, layout = indexed(gather_chunk(own, size), size)
        chunks.append([(array, 0) for array in arrays])
        layouts.append(layout)
    for (begin, end), vectors, layout in zip(steps, chunks, layouts):
        part = inner_products(layout, slab, vectors, (end - begin) * tile, begin, tile)
        total = part if total is None else total + part
    other = jnp.zeros_like(total)
    bit = 1
    while bit < depth:
        if bit > 1:
            total = total + other
        other = exchange(total, bit, depth, "prow")
        bit *= 2
    return update(layouts, total, other, triangles, slab, chunks, steps, tile)


def solution(mesh):
    in_specs = (P("pcol", "prow"), P(None, "pcol", "prow"), P(None, "pcol", None))
    out_specs = P("pcol", "prow")
    return jax.shard_map(functools.partial(body, dict(mesh.shape)), mesh=mesh, in_specs=in_specs, out_specs=out_specs, check_vma=False)
```

```python
import functools

import jax
import jax.numpy as jnp
from jax import lax
from jax.experimental import pallas as pl
from jax.experimental.pallas import tpu as pltpu
from jax.sharding import PartitionSpec as P

TILE_LIMIT = 2048
VMEM_LIMIT = 56 * 1024 * 1024
LATE_TILES = 2
PANELS = 2
ROWS = (((1,), (1,)), ((), ()))
PLAIN = (((1,), (0,)), ((), ()))


def tile_of(width):
    for unit in (256, 128):
        fits = [t for t in range(unit, TILE_LIMIT + 1, unit) if width % t == 0]
        if fits:
            return max(fits)
    return width


def in_hbm(array):
    return pltpu.with_memory_space_constraint(array, pltpu.HBM)


def split(value):
    high = value.astype(jnp.bfloat16)
    return high, (value - high.astype(jnp.float32)).astype(jnp.bfloat16)


def dot(left, right, dims):
    return lax.dot_general(left, right, dims, preferred_element_type=jnp.float32)


def exact(left, right, dims):
    return lax.dot_general(left, right, dims, precision=lax.Precision.HIGHEST, preferred_element_type=jnp.float32)


def stacked(refs):
    return jnp.concatenate([ref[...] for ref in refs], axis=0)


def pack_kernel(reflectors_ref, factors_ref, *refs):
    outs, sems = refs[:PANELS], refs[PANELS]
    width, nb = reflectors_ref.shape[2], factors_ref.shape[2]
    copies = []
    for p in range(PANELS):
        copies.append(pltpu.make_async_copy(reflectors_ref.at[p], outs[p].at[:, pl.ds(0, width)], sems.at[2 * p]))
        copies.append(pltpu.make_async_copy(factors_ref.at[p], outs[p].at[:, pl.ds(width, nb)], sems.at[2 * p + 1]))
    for copy in copies:
        copy.start()
    for copy in copies:
        copy.wait()


def pack(reflectors, factors):
    _, block, width = reflectors.shape
    nb = factors.shape[2]
    return pl.pallas_call(
        pack_kernel,
        in_specs=[pl.BlockSpec(memory_space=pltpu.HBM)] * 2,
        out_specs=[pl.BlockSpec(memory_space=pltpu.HBM)] * PANELS,
        out_shape=[jax.ShapeDtypeStruct((block, width + nb), jnp.float32)] * PANELS,
        scratch_shapes=[pltpu.SemaphoreType.DMA((2 * PANELS,))],
        cost_estimate=pl.CostEstimate(flops=0, bytes_accessed=16 * PANELS * block * width, transcendentals=0),
    )(reflectors, factors)


def inner_step(size, slab_ref, vector_refs):
    (fh, fl), (sh, sl) = (split(stacked(vector_refs[p * size : (p + 1) * size])) for p in range(PANELS))
    ch, cl = split(slab_ref[...])
    rows, nb = ch.shape[0], fh.shape[0]
    main = dot(jnp.concatenate([ch, cl, fh, fl], axis=0), jnp.concatenate([fh, sh], axis=0), ROWS)
    rest = dot(jnp.concatenate([ch, fh], axis=0), jnp.concatenate([fl, sl], axis=0), ROWS)
    inner = main[:rows] + main[rows : 2 * rows] + rest[:rows]
    between = main[2 * rows : 2 * rows + nb, nb:] + main[2 * rows + nb :, nb:] + rest[rows:, nb:]
    return jnp.concatenate([inner[:, :nb], inner[:, nb:], between], axis=0)


def early_kernel(size, *refs):
    slab_ref, order_ref = refs[:2]
    vector_refs = refs[2 : 2 + PANELS * size]
    factor_refs = refs[2 + PANELS * size : 2 + 2 * PANELS * size]
    out_ref, triangles_ref = refs[-2:]
    step = pl.program_id(0)
    part = inner_step(size, slab_ref, vector_refs)

    @pl.when(step == 0)
    def _():
        out_ref[...] = part
        for p in range(PANELS):
            triangles_ref[p] = exact(stacked(factor_refs[p * size : (p + 1) * size]), order_ref[...], PLAIN)

    @pl.when(step > 0)
    def _():
        out_ref[...] += part


def late_kernel(size, *refs):
    slab_ref, before_ref, out_ref = refs[0], refs[1], refs[-1]
    part = inner_step(size, slab_ref, refs[2 : 2 + PANELS * size])

    @pl.when(pl.program_id(0) == 0)
    def _():
        out_ref[...] = before_ref[...] + part

    @pl.when(pl.program_id(0) > 0)
    def _():
        out_ref[...] += part


def moving(block, tile, offset):
    return pl.BlockSpec((block, tile), lambda i: (0, offset + i))


def fixed(shape, *place):
    place = place or (0,) * len(shape)
    return pl.BlockSpec(shape, lambda i: place)


def inner_cost(rows, nb, width):
    return pl.CostEstimate(flops=6 * (rows + nb) * 2 * nb * width, bytes_accessed=4 * (rows + 2 * nb) * width, transcendentals=0)


def early_products(size, slab, order, chunk, steps, tile):
    rows, nb = slab.shape[0], order.shape[0]
    begin, end = steps
    block = chunk[0][0].shape[0]
    arrays = [in_hbm(array) for array, _ in chunk]
    specs = [moving(rows, tile, begin), fixed((nb, nb))]
    specs += [moving(block, tile, begin - base) for _, base in chunk]
    specs += [fixed((block, nb), 0, array.shape[1] // nb - 1) for array, _ in chunk]
    return pl.pallas_call(
        functools.partial(early_kernel, size),
        grid=(end - begin,),
        in_specs=specs,
        out_specs=[fixed((2 * rows + nb, nb)), fixed((PANELS, nb, nb))],
        out_shape=[jax.ShapeDtypeStruct((2 * rows + nb, nb), jnp.float32), jax.ShapeDtypeStruct((PANELS, nb, nb), jnp.float32)],
        compiler_params=pltpu.CompilerParams(vmem_limit_bytes=VMEM_LIMIT),
        cost_estimate=inner_cost(rows, nb, (end - begin) * tile),
    )(slab, order, *arrays, *arrays)


def late_products(size, slab, before, chunk, steps, tile):
    rows, nb = slab.shape[0], before.shape[1]
    begin, end = steps
    block = chunk[0][0].shape[0]
    specs = [moving(rows, tile, begin), fixed(before.shape)]
    specs += [moving(block, tile, begin - base) for _, base in chunk]
    return pl.pallas_call(
        functools.partial(late_kernel, size),
        grid=(end - begin,),
        in_specs=specs,
        out_specs=fixed(before.shape),
        out_shape=jax.ShapeDtypeStruct(before.shape, jnp.float32),
        compiler_params=pltpu.CompilerParams(vmem_limit_bytes=VMEM_LIMIT),
        cost_estimate=inner_cost(rows, nb, (end - begin) * tile),
    )(slab, before, *[in_hbm(array) for array, _ in chunk])


def update_kernel(size, terms, layouts, *refs):
    term_refs, triangles_ref, slab_ref = refs[:terms], refs[terms], refs[terms + 1]
    vector_refs, out_ref, both_ref = refs[terms + 2 : -2], refs[-2], refs[-1]
    rows = slab_ref.shape[0]
    step = pl.program_id(0)

    @pl.when(step == 0)
    def _():
        total = term_refs[0][...]
        for ref in term_refs[1:]:
            total += ref[...]
        scaled = exact(total[:rows], triangles_ref[0], ROWS)
        inner = total[rows : 2 * rows] - exact(scaled, total[2 * rows :], PLAIN)
        later = exact(inner, triangles_ref[1], ROWS)
        high, low = split(jnp.concatenate([scaled, later], axis=1))
        both_ref[...] = jnp.concatenate([high, low], axis=0)

    for (begin, end), places in layouts:

        @pl.when((step >= begin) & (step < end))
        def _():
            high, low = split(stacked([vector_refs[place] for place in places]))
            main = dot(both_ref[...], high, PLAIN)
            rest = dot(both_ref[:rows], low, PLAIN)
            out_ref[...] = slab_ref[...] - (main[:rows] + main[rows:] + rest)


def update(size, terms, triangles, slab, chunks, tile):
    rows, width = slab.shape
    nb = triangles.shape[1]
    specs = [fixed(term.shape) for term in terms]
    specs += [fixed(triangles.shape), moving(rows, tile, 0)]
    arrays, layouts, known = [], [], {}
    for chunk, (begin, end) in chunks:
        places = []
        for array, base in chunk:
            if id(array) not in known:
                known[id(array)] = len(arrays)
                arrays.append(array)
                last = base + array.shape[1] // tile - 1
                index = functools.partial(lambda low, high, i: (0, jnp.clip(i, low, high) - low), base, last)
                specs.append(pl.BlockSpec((array.shape[0], tile), index))
            places.append(known[id(array)])
        layouts.append(((begin, end), places))
    return pl.pallas_call(
        functools.partial(update_kernel, size, len(terms), layouts),
        grid=(width // tile,),
        in_specs=specs,
        out_specs=moving(rows, tile, 0),
        out_shape=jax.ShapeDtypeStruct(slab.shape, jnp.float32),
        scratch_shapes=[pltpu.VMEM((2 * rows, PANELS * nb), jnp.bfloat16)],
        compiler_params=pltpu.CompilerParams(vmem_limit_bytes=VMEM_LIMIT),
        cost_estimate=pl.CostEstimate(flops=6 * rows * 2 * nb * width, bytes_accessed=4 * (2 * rows + 2 * nb) * width, transcendentals=0),
    )(*terms, triangles, slab, *[in_hbm(array) for array in arrays])


def exchange(array, bit, size, axis):
    return lax.ppermute(array, axis, [(i, i ^ bit) for i in range(size)])


def gather(own, size, cut):
    column, first_tile = cut
    across = functools.partial(exchange, size=size, axis="pcol")
    early = [{0: (own[p], 0)} for p in range(PANELS)]
    late = [{0: (own[p], 0)} for p in range(PANELS)]
    bits = [1 << k for k in range(size.bit_length() - 1)]
    if len(bits) >= 2:
        high, low = bits.pop(), bits.pop()
        order = [(0, high, low), (1, low, high)]
        came = {}
        for p, direct, other in order:
            came[p, direct] = across(own[p], direct)
        for p, direct, other in order:
            came[p, other] = across(own[p], other)
        for p, direct, other in order:
            for bit in (direct, other):
                early[p][bit] = late[p][bit] = (came[p, bit], 0)
        for p, direct, other in order:
            early[p][high | low] = (across(came[p, direct][:, column:], other), first_tile)
        for p, direct, other in order:
            late[p][high | low] = (across(came[p, direct][:, :column], other), 0)
    for bit in reversed(bits):
        moved = {}
        for part in early + late:
            for r in list(part):
                array, base = part[r]
                if id(array) not in moved:
                    moved[id(array)] = (array, across(array, bit))
                part[r | bit] = (moved[id(array)][1], base)
    flat = lambda parts: [parts[p][r] for p in range(PANELS) for r in range(size)]
    return flat(early), flat(late)


def body(sizes, slab, reflectors, factors):
    size, depth = sizes["pcol"], sizes["prow"]
    block, width = reflectors.shape[1:]
    nb = factors.shape[2]
    tile = tile_of(width)
    tiles = width // tile
    cut = min(LATE_TILES, tiles - 1)
    me = lax.axis_index("pcol")
    place = jnp.arange(nb)
    moved_to = ((place // block) ^ me) * block + place % block
    order = (place[:, None] == moved_to[None, :]).astype(jnp.float32)
    own = pack(reflectors, factors)
    early, late = gather(own, size, (cut * tile, cut))
    total, triangles = early_products(size, slab, order, early, (cut, tiles), tile)
    chunks = [(early, (cut, tiles))]
    if cut:
        total = late_products(size, slab, total, late, (0, cut), tile)
        chunks.append((late, (0, cut)))
    terms, reach = [total], 1
    while reach < depth:
        if reach > 1:
            terms = [sum(terms[1:], terms[0])]
        span = min(4, depth // reach)
        terms = terms + [exchange(terms[0], k * reach, depth, "prow") for k in range(1, span)]
        reach *= span
    return update(size, terms, triangles, slab, chunks, tile)


def solution(mesh):
    in_specs = (P("pcol", "prow"), P(None, "pcol", "prow"), P(None, "pcol", None))
    out_specs = P("pcol", "prow")
    return jax.shard_map(functools.partial(body, dict(mesh.shape)), mesh=mesh, in_specs=in_specs, out_specs=out_specs, check_vma=False)
```

```python
import functools

import jax
import jax.numpy as jnp
from jax import lax
from jax.experimental import pallas as pl
from jax.experimental.pallas import tpu as pltpu
from jax.sharding import PartitionSpec as P


TILE_LIMIT = 8192
SUBTILE_LIMIT = 1024
VMEM_LIMIT = 60 * 1024 * 1024
PANELS = 2
ROWS = (((1,), (1,)), ((), ()))
PLAIN = (((1,), (0,)), ((), ()))


def divisor(width, limit):
    for unit in (128, 1):
        fits = [t for t in range(unit, min(limit, width) + 1, unit) if width % t == 0]
        if fits:
            return max(fits)
    return width


def split(value):
    high = value.astype(jnp.bfloat16)
    return high, (value - high.astype(jnp.float32)).astype(jnp.bfloat16)


def dot(left, right, dims):
    return lax.dot_general(left, right, dims, preferred_element_type=jnp.float32)


def exact(left, right, dims):
    return lax.dot_general(left, right, dims, precision=lax.Precision.HIGHEST, preferred_element_type=jnp.float32)


def over_columns(width, part):
    sub = divisor(width, SUBTILE_LIMIT)
    total = part(pl.ds(0, sub))

    def step(at, total):
        return total + part(pl.ds(pl.multiple_of(at * sub, sub), sub))

    return lax.fori_loop(1, width // sub, step, total)


def stacked(refs, places, columns):
    blocks = [refs[ref][:, columns] if panel is None else refs[ref][panel, :, columns] for ref, panel in places]
    return jnp.concatenate(blocks, axis=0)


def add_up(out_ref, value):
    @pl.when(pl.program_id(0) == 0)
    def _():
        out_ref[...] = value

    @pl.when(pl.program_id(0) > 0)
    def _():
        out_ref[...] += value


def near_kernel(layout, size, slab_ref, factors_ref, order_ref, *refs):
    vector_refs, inner_ref, share_ref, factors_out_ref = refs[:-3], *refs[-3:]
    rows, width = slab_ref.shape
    nb = order_ref.shape[0]
    block = nb // size
    near, corner = nb - nb // 4, nb // 4

    def part(columns):
        (fh, fl), (sh, sl) = (split(stacked(vector_refs, layout[p], columns)) for p in range(PANELS))
        ch, cl = split(slab_ref[:, columns])
        via = size // 4 * block
        left_high = [ch, fh[:block], fh[via : via + block]]
        left_low = [cl, fl[:block], fl[via : via + block]]
        second = dot(jnp.concatenate(left_high + left_low, axis=0), sh, ROWS)
        second = second[: second.shape[0] // 2] + second[second.shape[0] // 2 :]
        second += dot(jnp.concatenate(left_high, axis=0), sl, ROWS)
        first = dot(jnp.concatenate([ch, cl], axis=0), fh, ROWS)
        first = first[:rows] + first[rows:] + dot(ch, fl, ROWS)
        return jnp.concatenate([first, second], axis=0)

    found = over_columns(width, part)
    empty = jnp.zeros((2 * rows, corner), jnp.float32)
    add_up(inner_ref, jnp.concatenate([found[: 2 * rows], empty], axis=1))
    own, via = found[2 * rows : 2 * rows + block], found[2 * rows + block :]
    add_up(share_ref, jnp.concatenate([own, via[:, near - corner :]], axis=1))

    @pl.when(pl.program_id(0) == 0)
    def _():
        for p in range(PANELS):
            factors_out_ref[p * block : (p + 1) * block] = exact(factors_ref[p], order_ref[...], PLAIN)


def corner_kernel(layout, slab_ref, near_ref, *refs):
    vector_refs, out_ref = refs[:-1], refs[-1]
    rows, width = slab_ref.shape
    corner = near_ref.shape[1] // 4

    def part(columns):
        high, low = split(jnp.concatenate([stacked(vector_refs, layout[p], columns) for p in range(PANELS)], axis=0))
        ch, cl = split(slab_ref[:, columns])
        main = dot(jnp.concatenate([ch, cl], axis=0), high, ROWS)
        return main[:rows] + main[rows:] + dot(ch, low, ROWS)

    found = over_columns(width, part)
    found = jnp.concatenate([found[:, :corner], found[:, corner:]], axis=0)
    empty = jnp.zeros((2 * rows, near_ref.shape[1] - corner), jnp.float32)
    found = jnp.concatenate([empty, found], axis=1)

    @pl.when(pl.program_id(0) == 0)
    def _():
        out_ref[...] = near_ref[...] + found

    @pl.when(pl.program_id(0) > 0)
    def _():
        out_ref[...] += found


def share_kernel(*refs):
    share_refs, factors_ref, out_ref = refs[:-2], refs[-2], refs[-1]
    block = share_refs[0].shape[0]
    total = share_refs[0][...]
    for ref in share_refs[1:]:
        total += ref[...]
    out_ref[:block] = total
    out_ref[block:] = factors_ref[...]


def from_place(value, q, block, lane):
    width = value.shape[1]
    bit = 1
    while bit * block < width:
        if q & bit:
            shift = bit * block
            ahead, behind = pltpu.roll(value, width - shift, 1), pltpu.roll(value, shift, 1)
            value = jnp.where((lane // shift) % 2 == 0, ahead, behind)
        bit *= 2
    return value


def update_kernel(layout, size, terms, *refs):
    term_refs, share_refs, slab_ref = refs[:terms], refs[terms : terms + size], refs[terms + size]
    vector_refs, out_ref, both_ref = refs[terms + size + 1 : -2], refs[-2], refs[-1]
    rows, width = slab_ref.shape
    nb = term_refs[0].shape[1]
    block = nb // size

    @pl.when(pl.program_id(0) == 0)
    def _():
        total = term_refs[0][...]
        for ref in term_refs[1:]:
            total += ref[...]
        lane = lax.broadcasted_iota(jnp.int32, (1, nb), 1)
        between, triangles = [], [[] for _ in range(PANELS)]
        for q in range(size):
            held = from_place(share_refs[q][...], q, block, lane)
            other = from_place(share_refs[q ^ (size // 4)][:block], q, block, lane)
            far = ((lane // block) ^ q) >= size - size // 4
            between.append(jnp.where(far, other, held[:block]))
            for p in range(PANELS):
                triangles[p].append(held[(1 + p) * block : (2 + p) * block])
        between, first, second = (jnp.concatenate(parts, axis=0) for parts in (between, *triangles))
        scaled = exact(total[:rows], first, ROWS)
        inner = total[rows:] - exact(scaled, between, PLAIN)
        later = exact(inner, second, ROWS)
        high, low = split(jnp.concatenate([scaled, later], axis=1))
        both_ref[...] = jnp.concatenate([high, low], axis=0)

    sub = divisor(width, SUBTILE_LIMIT)

    @pl.loop(0, width // sub)
    def _(at):
        columns = pl.ds(pl.multiple_of(at * sub, sub), sub)
        high, low = split(jnp.concatenate([stacked(vector_refs, layout[p], columns) for p in range(PANELS)], axis=0))
        main = dot(both_ref[...], high, PLAIN)
        rest = dot(both_ref[:rows], low, PLAIN)
        out_ref[:, columns] = slab_ref[:, columns] - (main[:rows] + main[rows:] + rest)


def moving(array, tile):
    lead = array.shape[:-1]
    return pl.BlockSpec((*lead, tile), lambda i: (*(0 for _ in lead), i))


def fixed(shape):
    return pl.BlockSpec(shape, lambda i: tuple(0 for _ in shape))


def call(kernel, tile, whole, streamed, outs, streamed_out=False, scratch=(), flops=0):
    width = streamed[0].shape[-1]
    shapes = [jax.ShapeDtypeStruct(shape, jnp.float32) for shape in outs]
    arrays = [*whole[0], streamed[0], *whole[1], *streamed[1:]]
    specs = [fixed(a.shape) for a in whole[0]] + [moving(streamed[0], tile)]
    specs += [fixed(a.shape) for a in whole[1]] + [moving(a, tile) for a in streamed[1:]]
    return pl.pallas_call(
        kernel,
        grid=(width // tile,),
        in_specs=specs,
        out_specs=[moving(s, tile) if streamed_out else fixed(s.shape) for s in shapes],
        out_shape=shapes,
        scratch_shapes=list(scratch),
        compiler_params=pltpu.CompilerParams(vmem_limit_bytes=VMEM_LIMIT),
        cost_estimate=pl.CostEstimate(
            flops=flops, bytes_accessed=4 * sum(a.size for a in (*arrays, *shapes)), transcendentals=0
        ),
    )(*arrays)


def exchange(array, bit, size, axis):
    return lax.ppermute(array, axis, [(i, i ^ bit) for i in range(size)])


def summed_terms(value, depth):
    terms, reach = [value], 1
    while reach < depth:
        if reach > 1:
            terms = [sum(terms[1:], terms[0])]
        span = min(4, depth // reach)
        terms = terms + [exchange(terms[0], k * reach, depth, "prow") for k in range(1, span)]
        reach *= span
    return terms


def over_rest(arrays, layout, bit, across):
    while bit:
        count = len(arrays)
        arrays += [across(array, bit) for array in arrays]
        for part in layout:
            part.update({q | bit: (at + count, index) for q, (at, index) in part.items()})
        bit //= 2


def body(sizes, slab, reflectors, factors):
    size, depth = sizes["pcol"], sizes["prow"]
    rows, width = slab.shape
    block, nb = factors.shape[1:]
    high, low = size // 2, size // 4
    across = functools.partial(exchange, size=size, axis="pcol")
    me = lax.axis_index("pcol")
    place = jnp.arange(nb)
    order = (place[:, None] == ((place // block) ^ me) * block + place % block).astype(jnp.float32)

    own = [reflectors[p] for p in range(PANELS)]
    by_high, by_low = [], []
    for p in range(PANELS):
        by_high.append(across(own[p], high))
        by_low.append(across(own[p], low))
    corner = [across(by_high[0], low), across(by_low[1], high)]

    near_arrays = [reflectors, *by_low, *by_high]
    near = [{0: (0, p), low: (1 + p, None), high: (3 + p, None)} for p in range(PANELS)]
    far_arrays, far = list(corner), [{high | low: (p, None)} for p in range(PANELS)]
    over_rest(near_arrays, near, low // 2, across)
    near = [[part[q] for q in sorted(part)] for part in near]

    tile = divisor(width, TILE_LIMIT)
    inner, share, turned = call(
        functools.partial(near_kernel, near, size),
        tile,
        ([], [factors, order]),
        [slab, *near_arrays],
        [(2 * rows, nb), (block, nb), (PANELS * block, nb)],
        flops=6 * (2 * rows + 2 * block) * nb * width,
    )
    shares = summed_terms(share, depth)
    share = pl.pallas_call(share_kernel, out_shape=jax.ShapeDtypeStruct((3 * block, nb), jnp.float32))(*shares, turned)
    share, far_arrays = lax.optimization_barrier((share, corner))
    far = [{high | low: (p, None)} for p in range(PANELS)]
    over_rest(far_arrays, far, low // 2, across)
    far = [[part[q] for q in sorted(part)] for part in far]
    everything = [n + [(at + len(near_arrays), index) for at, index in f] for n, f in zip(near, far)]
    shares = [share] + [across(share, q) for q in range(1, size)]
    (inner,) = call(
        functools.partial(corner_kernel, far),
        tile,
        ([], [inner]),
        [slab, *far_arrays],
        [(2 * rows, nb)],
        flops=6 * 2 * rows * nb * width // 4,
    )
    terms = summed_terms(inner, depth)
    (result,) = call(
        functools.partial(update_kernel, everything, size, len(terms)),
        tile,
        ([*terms, *shares], []),
        [slab, *near_arrays, *far_arrays],
        [slab.shape],
        streamed_out=True,
        scratch=[pltpu.VMEM((2 * rows, PANELS * nb), jnp.bfloat16)],
        flops=6 * rows * 2 * nb * width,
    )
    return result


def solution(mesh):
    in_specs = (P("pcol", "prow"), P(None, "pcol", "prow"), P(None, "pcol", None))
    out_specs = P("pcol", "prow")
    return jax.shard_map(functools.partial(body, dict(mesh.shape)), mesh=mesh, in_specs=in_specs, out_specs=out_specs, check_vma=False)
```

```python
import functools

import jax
import jax.numpy as jnp
from jax import lax
from jax.experimental import pallas as pl
from jax.experimental.pallas import tpu as pltpu
from jax.sharding import PartitionSpec as P


TILE_LIMIT = 8192
UPDATE_LIMIT = 2048
VMEM_LIMIT = 48 * 1024 * 1024
COST = pl.CostEstimate(flops=1, bytes_accessed=1, transcendentals=0)
PANELS = 2
ROWS = (((1,), (1,)), ((), ()))
PLAIN = (((1,), (0,)), ((), ()))


def divisor(width, limit):
    for unit in (128, 1):
        fits = [t for t in range(unit, min(limit, width) + 1, unit) if width % t == 0]
        if fits:
            return max(fits)
    return width


def split(value):
    high = value.astype(jnp.bfloat16)
    return high, (value - high.astype(jnp.float32)).astype(jnp.bfloat16)


def dot(left, right, dims):
    return lax.dot_general(left, right, dims, preferred_element_type=jnp.float32)


def exact(left, right, dims):
    return lax.dot_general(left, right, dims, precision=lax.Precision.HIGHEST, preferred_element_type=jnp.float32)


def rows_of(refs):
    return jnp.concatenate([ref[...] for ref in refs], axis=0)


def add_up(out_ref, value, start_ref=None):
    @pl.when(pl.program_id(0) == 0)
    def _():
        out_ref[...] = value if start_ref is None else start_ref[...] + value

    @pl.when(pl.program_id(0) > 0)
    def _():
        out_ref[...] += value


def first_kernel(factors_ref, order_ref, slab_ref, *refs):
    vector_refs, inner_ref, turned_ref = refs[:-2], *refs[-2:]
    rows, nb, block = slab_ref.shape[0], order_ref.shape[0], factors_ref.shape[1]
    (vh, vl), (ch, cl) = split(rows_of(vector_refs)), split(slab_ref[...])
    found = dot(jnp.concatenate([ch, cl], axis=0), vh, ROWS)
    found = found[:rows] + found[rows:] + dot(ch, vl, ROWS)
    add_up(inner_ref, jnp.concatenate([found, jnp.zeros((rows, nb // 4), jnp.float32)], axis=1))

    @pl.when(pl.program_id(0) == 0)
    def _():
        for p in range(PANELS):
            turned_ref[p * block : (p + 1) * block] = exact(factors_ref[p], order_ref[...], PLAIN)


def second_kernel(slab_ref, own_ref, via_ref, *refs):
    vector_refs, inner_ref, share_ref = refs[:-2], *refs[-2:]
    rows, block, nb = slab_ref.shape[0], own_ref.shape[0], share_ref.shape[1]
    vh, vl = split(rows_of(vector_refs))
    high, low = split(rows_of([slab_ref, own_ref, via_ref]))
    count = high.shape[0]
    found = dot(jnp.concatenate([high, low], axis=0), vh, ROWS)
    found = found[:count] + found[count:] + dot(high, vl, ROWS)
    inner, own, via = found[:rows], found[rows : rows + block], found[rows + block :]
    add_up(inner_ref, jnp.concatenate([inner, jnp.zeros((rows, nb // 4), jnp.float32)], axis=1))
    add_up(share_ref, jnp.concatenate([own, via[:, nb // 2 :]], axis=1))


def corner_kernel(first_ref, second_ref, slab_ref, *refs):
    vector_refs, out_ref = refs[:-1], refs[-1]
    rows, nb = first_ref.shape
    (vh, vl), (ch, cl) = split(rows_of(vector_refs)), split(slab_ref[...])
    found = dot(jnp.concatenate([ch, cl], axis=0), vh, ROWS)
    found = found[:rows] + found[rows:] + dot(ch, vl, ROWS)
    found = jnp.concatenate([found[:, : nb // 4], found[:, nb // 4 :]], axis=0)
    found = jnp.concatenate([jnp.zeros((2 * rows, nb - nb // 4), jnp.float32), found], axis=1)

    @pl.when(pl.program_id(0) == 0)
    def _():
        out_ref[...] = jnp.concatenate([first_ref[...], second_ref[...]], axis=0) + found

    @pl.when(pl.program_id(0) > 0)
    def _():
        out_ref[...] += found


def share_kernel(*refs):
    share_refs, factors_ref, out_ref = refs[:-2], refs[-2], refs[-1]
    block = share_refs[0].shape[0]
    total = share_refs[0][...]
    for ref in share_refs[1:]:
        total += ref[...]
    out_ref[:block] = total
    out_ref[block:] = factors_ref[...]


def from_place(value, q, block, lane):
    width = value.shape[1]
    bit = 1
    while bit * block < width:
        if q & bit:
            shift = bit * block
            ahead, behind = pltpu.roll(value, width - shift, 1), pltpu.roll(value, shift, 1)
            value = jnp.where((lane // shift) % 2 == 0, ahead, behind)
        bit *= 2
    return value


def cut_columns(width):
    sub = divisor(width, UPDATE_LIMIT)
    count = width // sub
    firsts = [0, *range(1, count, 2)] if count % 2 else list(range(0, count, 2))
    return [(begin * sub, (end - begin) * sub) for begin, end in zip(firsts, [*firsts[1:], count])]


def update_kernel(panels, size, terms, *refs):
    term_refs, share_refs = refs[:terms], refs[terms : terms + size]
    slab_ref, *vector_refs = refs[terms + size : -5]
    out_ref, vectors, before, after, sems = refs[-5:]
    rows, width = slab_ref.shape
    nb = term_refs[0].shape[1]
    block = nb // size
    parts = cut_columns(width)

    for at, (begin, count) in enumerate(parts):
        columns = pl.ds(begin, count)
        pltpu.make_async_copy(slab_ref.at[:, columns], before.at[:, columns], sems.at[1, at]).start()
        for place, (ref, panel) in enumerate(zip(vector_refs, panels)):
            source = ref.at[:, columns] if panel is None else ref.at[panel, :, columns]
            target = vectors.at[pl.ds(place * block, block), columns]
            pltpu.make_async_copy(source, target, sems.at[0, at]).start()

    total = term_refs[0][...]
    for ref in term_refs[1:]:
        total += ref[...]
    lane = lax.broadcasted_iota(jnp.int32, (1, nb), 1)
    between, triangles = [], [[] for _ in range(PANELS)]
    for q in range(size):
        held = from_place(share_refs[q][...], q, block, lane)
        other = from_place(share_refs[q ^ (size // 4)][:block], q, block, lane)
        far = ((lane // block) ^ q) >= size - size // 4
        between.append(jnp.where(far, other, held[:block]))
        for p in range(PANELS):
            triangles[p].append(held[(1 + p) * block : (2 + p) * block])
    between, first, second = (jnp.concatenate(pieces, axis=0) for pieces in (between, *triangles))
    scaled = exact(total[:rows], first, ROWS)
    inner = total[rows:] - exact(scaled, between, PLAIN)
    later = exact(inner, second, ROWS)
    both = jnp.concatenate(split(jnp.concatenate([scaled, later], axis=1)), axis=0)

    for at, (begin, count) in enumerate(parts):
        columns = pl.ds(begin, count)
        held = vectors.at[:, columns]
        pltpu.make_async_copy(held, held, sems.at[0, at]).wait()
        pltpu.make_async_copy(slab_ref.at[:, columns], before.at[:, columns], sems.at[1, at]).wait()
        high, low = split(vectors[:, columns])
        main = dot(both, high, PLAIN)
        rest = dot(both[:rows], low, PLAIN)
        after[:, columns] = before[:, columns] - (main[:rows] + main[rows:] + rest)
        pltpu.make_async_copy(after.at[:, columns], out_ref.at[:, columns], sems.at[2, at]).start()
    for at, (begin, count) in enumerate(parts):
        columns = pl.ds(begin, count)
        pltpu.make_async_copy(after.at[:, columns], out_ref.at[:, columns], sems.at[2, at]).wait()


def fixed(shape):
    return pl.BlockSpec(shape, lambda i: tuple(0 for _ in shape))


def moving(array, panel, tile):
    if panel is None:
        return pl.BlockSpec((array.shape[0], tile), lambda i: (0, i))
    return pl.BlockSpec((None, array.shape[1], tile), lambda i: (panel, 0, i))


def products(kernel, whole, streamed, outs):
    width = streamed[0][0].shape[-1]
    tile = divisor(width, TILE_LIMIT)
    return pl.pallas_call(
        kernel,
        grid=(width // tile,),
        in_specs=[fixed(a.shape) for a in whole] + [moving(a, p, tile) for a, p in streamed],
        out_specs=[fixed(shape) for shape in outs],
        out_shape=[jax.ShapeDtypeStruct(shape, jnp.float32) for shape in outs],
        compiler_params=pltpu.CompilerParams(vmem_limit_bytes=VMEM_LIMIT),
        cost_estimate=COST,
    )(*whole, *[a for a, _ in streamed])


def update(terms, shares, slab, pieces):
    rows, width = slab.shape
    size, nb = len(shares), terms[0].shape[1]
    count = len(cut_columns(width))
    whole = [*terms, *shares]
    return pl.pallas_call(
        functools.partial(update_kernel, [panel for _, panel in pieces], size, len(terms)),
        in_specs=[pl.BlockSpec(memory_space=pltpu.VMEM)] * len(whole) + [pl.BlockSpec(memory_space=pl.ANY)] * (1 + len(pieces)),
        out_specs=pl.BlockSpec(memory_space=pl.ANY),
        out_shape=jax.ShapeDtypeStruct(slab.shape, jnp.float32),
        scratch_shapes=[
            pltpu.VMEM((PANELS * nb, width), jnp.float32),
            pltpu.VMEM((rows, width), jnp.float32),
            pltpu.VMEM((rows, width), jnp.float32),
            pltpu.SemaphoreType.DMA((3, count)),
        ],
        compiler_params=pltpu.CompilerParams(vmem_limit_bytes=VMEM_LIMIT),
        cost_estimate=COST,
    )(*whole, slab, *[array for array, _ in pieces])


def exchange(array, bit, size, axis):
    return lax.ppermute(array, axis, [(i, i ^ bit) for i in range(size)])


def summed_terms(value, depth):
    terms, reach = [value], 1
    while reach < depth:
        if reach > 1:
            terms = [sum(terms[1:], terms[0])]
        span = min(4, depth // reach)
        terms = terms + [exchange(terms[0], k * reach, depth, "prow") for k in range(1, span)]
        reach *= span
    return terms


def over_rest(held, bit, across):
    while bit:
        moved = {}
        for q, (array, panel) in list(held.items()):
            if id(array) not in moved:
                moved[id(array)] = across(array, bit)
            held[q | bit] = (moved[id(array)], panel)
        bit //= 2


def in_order(held):
    return [held[q] for q in sorted(held)]


def body(sizes, slab, reflectors, factors):
    size, depth = sizes["pcol"], sizes["prow"]
    rows = slab.shape[0]
    block, nb = factors.shape[1:]
    high, low = size // 2, size // 4
    across = functools.partial(exchange, size=size, axis="pcol")
    me = lax.axis_index("pcol")
    place = jnp.arange(nb)
    order = (place[:, None] == ((place // block) ^ me) * block + place % block).astype(jnp.float32)

    by_high = [across(reflectors[p], high) for p in range(PANELS)]
    by_low = [across(reflectors[p], low) for p in range(PANELS)]
    corner = [across(by_high[0], low), None]
    own = {0: (reflectors, 0)}
    over_rest(own, low // 2, across)

    near = [{q: (array, p) for q, (array, _) in own.items()} for p in range(PANELS)]
    held = {low: (by_low[0], None), high: (by_high[0], None)}
    over_rest(held, low // 2, across)
    near[0].update(held)
    inner, turned = products(first_kernel, [factors, order], [(slab, None), *in_order(near[0])], [(rows, nb), (PANELS * block, nb)])

    inner, by_low[1], by_high[1] = lax.optimization_barrier((inner, by_low[1], by_high[1]))
    corner[1] = across(by_low[1], high)
    held = {low: (by_low[1], None), high: (by_high[1], None)}
    over_rest(held, low // 2, across)
    near[1].update(held)
    later, share = products(
        second_kernel, [], [(slab, None), near[0][0], near[0][low], *in_order(near[1])], [(rows, nb), (block, nb)]
    )

    later, corner = lax.optimization_barrier((later, corner))
    far = [{high | low: (corner[p], None)} for p in range(PANELS)]
    for p in range(PANELS):
        over_rest(far[p], low // 2, across)
    far = [in_order(far[p]) for p in range(PANELS)]
    shares = summed_terms(share, depth)
    share = pl.pallas_call(
        share_kernel, out_shape=jax.ShapeDtypeStruct(((1 + PANELS) * block, nb), jnp.float32), cost_estimate=COST
    )(*shares, turned)
    shares = [share] + [across(share, q) for q in range(1, size)]
    (inner,) = products(corner_kernel, [inner, later], [(slab, None), *far[0], *far[1]], [(2 * rows, nb)])
    terms = summed_terms(inner, depth)
    return update(terms, shares, slab, [piece for p in range(PANELS) for piece in (*in_order(near[p]), *far[p])])


def solution(mesh):
    in_specs = (P("pcol", "prow"), P(None, "pcol", "prow"), P(None, "pcol", None))
    out_specs = P("pcol", "prow")
    return jax.shard_map(functools.partial(body, dict(mesh.shape)), mesh=mesh, in_specs=in_specs, out_specs=out_specs, check_vma=False)
```

```python
import functools

import jax
import jax.numpy as jnp
from jax import lax
from jax.experimental import pallas as pl
from jax.experimental.pallas import tpu as pltpu
from jax.sharding import PartitionSpec as P


TILE_LIMIT = 8192
UPDATE_LIMIT = 2048
VMEM_LIMIT = 48 * 1024 * 1024
SMALL_LIMIT = 8 * 1024 * 1024
COST = pl.CostEstimate(flops=1, bytes_accessed=1, transcendentals=0)
PANELS = 2
ROWS = (((1,), (1,)), ((), ()))
PLAIN = (((1,), (0,)), ((), ()))


def divisor(width, limit):
    for unit in (128, 1):
        fits = [t for t in range(unit, min(limit, width) + 1, unit) if width % t == 0]
        if fits:
            return max(fits)
    return width


def split(value):
    high = value.astype(jnp.bfloat16)
    return high, (value - high.astype(jnp.float32)).astype(jnp.bfloat16)


def dot(left, right, dims):
    return lax.dot_general(left, right, dims, preferred_element_type=jnp.float32)


def exact(left, right, dims):
    return lax.dot_general(left, right, dims, precision=lax.Precision.HIGHEST, preferred_element_type=jnp.float32)


def panel_rows(refs, panel):
    return jnp.concatenate([ref[panel] for ref in refs], axis=0)


def add_up(out_ref, value):
    @pl.when(pl.program_id(0) == 0)
    def _():
        out_ref[...] = value

    @pl.when(pl.program_id(0) > 0)
    def _():
        out_ref[...] += value


def near_kernel(slab_ref, *refs):
    vector_refs, inner_ref, share_ref = refs[:-2], *refs[-2:]
    (rows, _), (group, nb) = slab_ref.shape, share_ref.shape
    (fh, fl), (sh, sl) = (split(panel_rows(vector_refs, p)) for p in range(PANELS))
    ch, cl = split(slab_ref[...])
    first = dot(jnp.concatenate([ch, cl], axis=0), fh, ROWS)
    first = first[:rows] + first[rows:] + dot(ch, fl, ROWS)
    high = jnp.concatenate([ch, fh[: 2 * group]], axis=0)
    low = jnp.concatenate([cl, fl[: 2 * group]], axis=0)
    second = dot(jnp.concatenate([high, low], axis=0), sh, ROWS)
    second = second[: high.shape[0]] + second[high.shape[0] :] + dot(high, sl, ROWS)
    inner, own, via = second[:rows], second[rows : rows + group], second[rows + group :]
    inner = jnp.concatenate([first, inner], axis=0)
    add_up(inner_ref, jnp.concatenate([inner, jnp.zeros((2 * rows, nb // 4), jnp.float32)], axis=1))
    add_up(share_ref, jnp.concatenate([own, via[:, nb // 2 :]], axis=1))


def corner_kernel(near_ref, slab_ref, *refs):
    vector_refs, out_ref = refs[:-1], refs[-1]
    rows, nb = slab_ref.shape[0], near_ref.shape[1]
    (vh, vl), (ch, cl) = split(jnp.concatenate([ref[...] for ref in vector_refs], axis=0)), split(slab_ref[...])
    found = dot(jnp.concatenate([ch, cl], axis=0), vh, ROWS)
    found = found[:rows] + found[rows:] + dot(ch, vl, ROWS)
    found = jnp.concatenate([found[:, : nb // 4], found[:, nb // 4 :]], axis=0)
    found = jnp.concatenate([jnp.zeros((2 * rows, nb - nb // 4), jnp.float32), found], axis=1)

    @pl.when(pl.program_id(0) == 0)
    def _():
        out_ref[...] = near_ref[...] + found

    @pl.when(pl.program_id(0) > 0)
    def _():
        out_ref[...] += found


def turn_kernel(factors_ref, order_ref, out_ref):
    for p in range(PANELS):
        out_ref[p] = exact(factors_ref[p], order_ref[...], PLAIN)


def share_kernel(terms, *refs):
    share_refs, turned_refs, out_ref = refs[:terms], refs[terms:-1], refs[-1]
    group, nb = share_refs[0].shape
    block = group // len(turned_refs)
    total = share_refs[0][...]
    for ref in share_refs[1:]:
        total += ref[...]
    out_ref[:group] = total
    lane = lax.broadcasted_iota(jnp.int32, (1, nb), 1)
    turned = [[from_place(ref[p], q, block, lane) for q, ref in enumerate(turned_refs)] for p in range(PANELS)]
    out_ref[group:] = jnp.concatenate([rows for part in turned for rows in part], axis=0)


def from_place(value, q, block, lane):
    width = value.shape[1]
    bit = 1
    while bit * block < width:
        if q & bit:
            shift = bit * block
            ahead, behind = pltpu.roll(value, width - shift, 1), pltpu.roll(value, shift, 1)
            value = jnp.where((lane // shift) % 2 == 0, ahead, behind)
        bit *= 2
    return value


def cut_columns(width):
    sub = divisor(width, UPDATE_LIMIT)
    count = width // sub
    firsts = [0, *range(1, count, 2)] if count % 2 else list(range(0, count, 2))
    return [(begin * sub, (end - begin) * sub) for begin, end in zip(firsts, [*firsts[1:], count])]


def update_kernel(panels, terms, *refs):
    term_refs, share_refs = refs[:terms], refs[terms : terms + 4]
    slab_ref, *vector_refs = refs[terms + 4 : -5]
    out_ref, vectors, before, after, sems = refs[-5:]
    rows, width = slab_ref.shape
    nb = term_refs[0].shape[1]
    block = PANELS * nb // len(panels)
    group = nb // 4
    parts = cut_columns(width)

    for at, (begin, count) in enumerate(parts):
        columns = pl.ds(begin, count)
        pltpu.make_async_copy(slab_ref.at[:, columns], before.at[:, columns], sems.at[1, at]).start()
        for place, (ref, panel) in enumerate(zip(vector_refs, panels)):
            source = ref.at[:, columns] if panel is None else ref.at[panel, :, columns]
            target = vectors.at[pl.ds(place * block, block), columns]
            pltpu.make_async_copy(source, target, sems.at[0, at]).start()

    total = term_refs[0][...]
    for ref in term_refs[1:]:
        total += ref[...]
    lane = lax.broadcasted_iota(jnp.int32, (1, nb), 1)
    between, triangles = [], [[] for _ in range(PANELS)]
    for side in range(4):
        held = from_place(share_refs[side][...], side, group, lane)
        other = from_place(share_refs[side ^ 1][:group], side, group, lane)
        far = ((lane // group) ^ side) == 3
        between.append(jnp.where(far, other, held[:group]))
        for p in range(PANELS):
            triangles[p].append(held[(1 + p) * group : (2 + p) * group])
    between, first, second = (jnp.concatenate(pieces, axis=0) for pieces in (between, *triangles))
    scaled = exact(total[:rows], first, ROWS)
    inner = total[rows:] - exact(scaled, between, PLAIN)
    later = exact(inner, second, ROWS)
    both = jnp.concatenate(split(jnp.concatenate([scaled, later], axis=1)), axis=0)

    for at, (begin, count) in enumerate(parts):
        columns = pl.ds(begin, count)
        held = vectors.at[:, columns]
        pltpu.make_async_copy(held, held, sems.at[0, at]).wait()
        pltpu.make_async_copy(slab_ref.at[:, columns], before.at[:, columns], sems.at[1, at]).wait()
        high, low = split(vectors[:, columns])
        main = dot(both, high, PLAIN)
        rest = dot(both[:rows], low, PLAIN)
        after[:, columns] = before[:, columns] - (main[:rows] + main[rows:] + rest)
        pltpu.make_async_copy(after.at[:, columns], out_ref.at[:, columns], sems.at[2, at]).start()
    for at, (begin, count) in enumerate(parts):
        columns = pl.ds(begin, count)
        pltpu.make_async_copy(after.at[:, columns], out_ref.at[:, columns], sems.at[2, at]).wait()


def fixed(shape):
    return pl.BlockSpec(shape, lambda i: tuple(0 for _ in shape))


def moving(array, tile):
    lead = array.shape[:-1]
    return pl.BlockSpec((*lead, tile), lambda i: (*(0 for _ in lead), i))


def products(kernel, whole, streamed, outs):
    width = streamed[0].shape[-1]
    tile = divisor(width, TILE_LIMIT)
    return pl.pallas_call(
        kernel,
        grid=(width // tile,),
        in_specs=[fixed(a.shape) for a in whole] + [moving(a, tile) for a in streamed],
        out_specs=[fixed(shape) for shape in outs],
        out_shape=[jax.ShapeDtypeStruct(shape, jnp.float32) for shape in outs],
        compiler_params=pltpu.CompilerParams(vmem_limit_bytes=VMEM_LIMIT),
        cost_estimate=COST,
    )(*whole, *streamed)


def small(kernel, shape, *arrays):
    return pl.pallas_call(
        kernel,
        out_shape=jax.ShapeDtypeStruct(shape, jnp.float32),
        compiler_params=pltpu.CompilerParams(vmem_limit_bytes=SMALL_LIMIT),
        cost_estimate=COST,
    )(*arrays)


def update(terms, shares, slab, pieces):
    rows, width = slab.shape
    nb = terms[0].shape[1]
    count = len(cut_columns(width))
    whole = [*terms, *shares]
    return pl.pallas_call(
        functools.partial(update_kernel, [panel for _, panel in pieces], len(terms)),
        in_specs=[pl.BlockSpec(memory_space=pltpu.VMEM)] * len(whole) + [pl.BlockSpec(memory_space=pl.ANY)] * (1 + len(pieces)),
        out_specs=pl.BlockSpec(memory_space=pl.ANY),
        out_shape=jax.ShapeDtypeStruct(slab.shape, jnp.float32),
        scratch_shapes=[
            pltpu.VMEM((PANELS * nb, width), jnp.float32),
            pltpu.VMEM((rows, width), jnp.float32),
            pltpu.VMEM((rows, width), jnp.float32),
            pltpu.SemaphoreType.DMA((3, count)),
        ],
        compiler_params=pltpu.CompilerParams(vmem_limit_bytes=VMEM_LIMIT),
        cost_estimate=COST,
    )(*whole, slab, *[array for array, _ in pieces])


def exchange(array, bit, size, axis):
    return lax.ppermute(array, axis, [(i, i ^ bit) for i in range(size)])


def summed_terms(value, depth):
    terms, reach = [value], 1
    while reach < depth:
        if reach > 1:
            terms = [sum(terms[1:], terms[0])]
        span = min(4, depth // reach)
        terms = terms + [exchange(terms[0], k * reach, depth, "prow") for k in range(1, span)]
        reach *= span
    return terms


def over_rest(arrays, bit, across):
    lower, arrays = 1, list(arrays)
    while lower <= bit:
        arrays += [across(array, lower) for array in arrays]
        lower *= 2
    return arrays


def body(sizes, slab, reflectors, factors):
    size, depth = sizes["pcol"], sizes["prow"]
    rows = slab.shape[0]
    block, nb = factors.shape[1:]
    high, low = size // 2, size // 4
    across = functools.partial(exchange, size=size, axis="pcol")
    me = lax.axis_index("pcol")
    place = jnp.arange(nb)
    order = (place[:, None] == ((place // block) ^ me) * block + place % block).astype(jnp.float32)

    by_high, by_low = across(reflectors, high), across(reflectors, low)
    corner = [across(by_high[0], low), across(by_low[1], high)]
    near = [array for held in (reflectors, by_low, by_high) for array in over_rest([held], low // 2, across)]
    turned = small(turn_kernel, factors.shape, factors, order)
    turned = over_rest([turned], low // 2, across)
    near, turned = lax.optimization_barrier((near, turned))
    inner, share = products(near_kernel, [], [slab, *near], [(2 * rows, nb), (nb // 4, nb)])
    shares = summed_terms(share, depth)
    shares, corner = lax.optimization_barrier((shares, corner))
    far = [over_rest([corner[p]], low // 2, across) for p in range(PANELS)]
    share = small(functools.partial(share_kernel, len(shares)), ((1 + PANELS) * nb // 4, nb), *shares, *turned)
    shares = [share] + [across(share, side * low) for side in range(1, 4)]
    (inner,) = products(corner_kernel, [inner], [slab, *far[0], *far[1]], [(2 * rows, nb)])
    terms = summed_terms(inner, depth)
    pieces = [piece for p in range(PANELS) for piece in (*((array, p) for array in near), *((array, None) for array in far[p]))]
    return update(terms, shares, slab, pieces)


def solution(mesh):
    in_specs = (P("pcol", "prow"), P(None, "pcol", "prow"), P(None, "pcol", None))
    out_specs = P("pcol", "prow")
    return jax.shard_map(functools.partial(body, dict(mesh.shape)), mesh=mesh, in_specs=in_specs, out_specs=out_specs, check_vma=False)
```

```python
import functools

import jax
import jax.numpy as jnp
from jax import lax
from jax.experimental import pallas as pl
from jax.experimental.pallas import tpu as pltpu
from jax.sharding import PartitionSpec as P


UNIT_LIMIT = 2048
TILE_LIMIT = 8192
VMEM_LIMIT = 48 * 1024 * 1024
SMALL_LIMIT = 8 * 1024 * 1024
COST = pl.CostEstimate(flops=1, bytes_accessed=1, transcendentals=0)
PANELS = 2
ROWS = (((1,), (1,)), ((), ()))
PLAIN = (((1,), (0,)), ((), ()))


def divisor(width, limit):
    for unit in (128, 1):
        fits = [t for t in range(unit, min(limit, width) + 1, unit) if width % t == 0]
        if fits:
            return max(fits)
    return width


def split(value):
    high = value.astype(jnp.bfloat16)
    return high, (value - high.astype(jnp.float32)).astype(jnp.bfloat16)


def dot(left, right, dims):
    return lax.dot_general(left, right, dims, preferred_element_type=jnp.float32)


def exact(left, right, dims):
    return lax.dot_general(left, right, dims, precision=lax.Precision.HIGHEST, preferred_element_type=jnp.float32)


def panel_rows(refs, panel):
    return jnp.concatenate([ref[panel] for ref in refs], axis=0)


def add_up(out_ref, value):
    @pl.when(pl.program_id(0) == 0)
    def _():
        out_ref[...] = value

    @pl.when(pl.program_id(0) > 0)
    def _():
        out_ref[...] += value


def near_kernel(slab_ref, *refs):
    vector_refs, out_ref, high_ref, low_ref = refs[:-3], *refs[-3:]
    rows, nb = slab_ref.shape[0], out_ref.shape[1]
    group = nb // 4
    (fh, fl), (sh, sl) = (split(panel_rows(vector_refs, p)) for p in range(PANELS))
    high_ref[...] = jnp.concatenate([fh, sh], axis=0)
    low_ref[...] = jnp.concatenate([fl, sl], axis=0)
    ch, cl = split(slab_ref[...])
    first = dot(jnp.concatenate([ch, cl], axis=0), fh, ROWS)
    first = first[:rows] + first[rows:] + dot(ch, fl, ROWS)
    high = jnp.concatenate([ch, fh[: 2 * group]], axis=0)
    low = jnp.concatenate([cl, fl[: 2 * group]], axis=0)
    second = dot(jnp.concatenate([high, low], axis=0), sh, ROWS)
    second = second[: high.shape[0]] + second[high.shape[0] :] + dot(high, sl, ROWS)
    inner, own, via = second[:rows], second[rows : rows + group], second[rows + group :]
    inner = jnp.concatenate([first, inner], axis=0)
    inner = jnp.concatenate([inner, jnp.zeros((2 * rows, group), jnp.float32)], axis=1)
    share = jnp.concatenate([own, via[:, 2 * group :]], axis=1)
    add_up(out_ref, jnp.concatenate([inner, share], axis=0))


def corner_kernel(slab_ref, *refs):
    vector_refs, out_ref = refs[:-1], refs[-1]
    rows, (part, nb) = slab_ref.shape[0], out_ref.shape
    (vh, vl), (ch, cl) = split(jnp.concatenate([ref[...] for ref in vector_refs], axis=0)), split(slab_ref[...])
    found = dot(jnp.concatenate([ch, cl], axis=0), vh, ROWS)
    found = found[:rows] + found[rows:] + dot(ch, vl, ROWS)
    found = jnp.concatenate([found[:, : nb // 4], found[:, nb // 4 :]], axis=0)
    add_up(out_ref, jnp.concatenate([found[k * part : (k + 1) * part] for k in range(4)], axis=1))


def turn_kernel(factors_ref, order_ref, out_ref):
    for p in range(PANELS):
        out_ref[p] = exact(factors_ref[p], order_ref[...], PLAIN)


def share_kernel(terms, *refs):
    term_refs, turned_refs, inner_ref, share_ref = refs[:terms], refs[terms:-2], *refs[-2:]
    group = share_ref.shape[0] // (1 + PANELS)
    nb = share_ref.shape[1]
    block = group // len(turned_refs)
    total = term_refs[0][...]
    for ref in term_refs[1:]:
        total += ref[...]
    inner_ref[...] = total[:-group]
    share_ref[:group] = total[-group:]
    lane = lax.broadcasted_iota(jnp.int32, (1, nb), 1)
    turned = [[from_place(ref[p], q, block, lane) for q, ref in enumerate(turned_refs)] for p in range(PANELS)]
    share_ref[group:] = jnp.concatenate([rows for part in turned for rows in part], axis=0)


def from_place(value, q, block, lane):
    width = value.shape[1]
    bit = 1
    while bit * block < width:
        if q & bit:
            shift = bit * block
            ahead, behind = pltpu.roll(value, width - shift, 1), pltpu.roll(value, shift, 1)
            value = jnp.where((lane // shift) % 2 == 0, ahead, behind)
        bit *= 2
    return value


def cut_columns(width):
    sub = divisor(width, UNIT_LIMIT)
    count = width // sub
    firsts = [0, *range(1, count, 2)] if count % 2 else list(range(0, count, 2))
    return [(begin * sub, (end - begin) * sub) for begin, end in zip(firsts, [*firsts[1:], count])]


def update_kernel(terms, *refs):
    near_ref, term_refs, share_refs = refs[0], refs[1 : 1 + terms], refs[1 + terms : 5 + terms]
    slab_ref, high_ref, low_ref, *corner_refs = refs[5 + terms : -7]
    out_ref, high, low, corner, before, after, sems = refs[-7:]
    rows, nb = near_ref.shape[0] // PANELS, near_ref.shape[1]
    group = nb // 4
    block = corner_refs[0].shape[0]
    parts = cut_columns(slab_ref.shape[1])

    def copies(at, begin, count):
        columns = pl.ds(begin, count)
        for ref, held, sem in ((slab_ref, before, 0), (high_ref, high, 1), (low_ref, low, 2)):
            yield pltpu.make_async_copy(ref.at[:, columns], held.at[:, columns], sems.at[sem, at])
        for place, ref in enumerate(corner_refs):
            target = corner.at[pl.ds(place * block, block), columns]
            yield pltpu.make_async_copy(ref.at[:, columns], target, sems.at[4 + place, at])

    for at, (begin, count) in enumerate(parts):
        for copy in copies(at, begin, count):
            copy.start()

    total = term_refs[0][...]
    for ref in term_refs[1:]:
        total += ref[...]
    total = jnp.concatenate([total[:, k * group : (k + 1) * group] for k in range(4)], axis=0)
    total = near_ref[...] + jnp.concatenate([jnp.zeros((PANELS * rows, nb - group), jnp.float32), total], axis=1)
    lane = lax.broadcasted_iota(jnp.int32, (1, nb), 1)
    between, triangles = [], [[] for _ in range(PANELS)]
    for side in range(4):
        held = from_place(share_refs[side][...], side, group, lane)
        other = from_place(share_refs[side ^ 1][:group], side, group, lane)
        far = ((lane // group) ^ side) == 3
        between.append(jnp.where(far, other, held[:group]))
        for p in range(PANELS):
            triangles[p].append(held[(1 + p) * group : (2 + p) * group])
    between, first, second = (jnp.concatenate(pieces, axis=0) for pieces in (between, *triangles))
    scaled = exact(total[:rows], first, ROWS)
    inner = total[rows:] - exact(scaled, between, PLAIN)
    later = exact(inner, second, ROWS)
    near = nb - group
    scaled = jnp.concatenate([scaled[:, :near], later[:, :near], scaled[:, near:], later[:, near:]], axis=1)
    both = jnp.concatenate(split(scaled), axis=0)

    for at, (begin, count) in enumerate(parts):
        columns = pl.ds(begin, count)
        for copy in copies(at, begin, count):
            copy.wait()
        corner_high, corner_low = split(corner[:, columns])
        main = dot(both, jnp.concatenate([high[:, columns], corner_high], axis=0), PLAIN)
        rest = dot(both[:rows], jnp.concatenate([low[:, columns], corner_low], axis=0), PLAIN)
        after[:, columns] = before[:, columns] - (main[:rows] + main[rows:] + rest)
        pltpu.make_async_copy(after.at[:, columns], out_ref.at[:, columns], sems.at[3, at]).start()
    for at, (begin, count) in enumerate(parts):
        columns = pl.ds(begin, count)
        pltpu.make_async_copy(after.at[:, columns], out_ref.at[:, columns], sems.at[3, at]).wait()


def fixed(shape):
    return pl.BlockSpec(shape, lambda i: tuple(0 for _ in shape))


def moving(array, tile):
    lead = array.shape[:-1]
    return pl.BlockSpec((*lead, tile), lambda i: (*(0 for _ in lead), i))


def products(kernel, streamed, shape, kept=()):
    width = streamed[0].shape[-1]
    tile = divisor(width, TILE_LIMIT)
    return pl.pallas_call(
        kernel,
        grid=(width // tile,),
        in_specs=[moving(a, tile) for a in streamed],
        out_specs=[fixed(shape), *(moving(a, tile) for a in kept)],
        out_shape=[jax.ShapeDtypeStruct(shape, jnp.float32), *kept],
        compiler_params=pltpu.CompilerParams(vmem_limit_bytes=VMEM_LIMIT),
        cost_estimate=COST,
    )(*streamed)


def small(kernel, shapes, *arrays):
    return pl.pallas_call(
        kernel,
        out_shape=[jax.ShapeDtypeStruct(shape, jnp.float32) for shape in shapes],
        compiler_params=pltpu.CompilerParams(vmem_limit_bytes=SMALL_LIMIT),
        cost_estimate=COST,
    )(*arrays)


def update(near, terms, shares, slab, high, low, corner):
    width = slab.shape[1]
    whole, streamed = [near, *terms, *shares], [slab, high, low, *corner]
    return pl.pallas_call(
        functools.partial(update_kernel, len(terms)),
        in_specs=[pl.BlockSpec(memory_space=pltpu.VMEM)] * len(whole) + [pl.BlockSpec(memory_space=pl.ANY)] * len(streamed),
        out_specs=pl.BlockSpec(memory_space=pl.ANY),
        out_shape=jax.ShapeDtypeStruct(slab.shape, jnp.float32),
        scratch_shapes=[
            pltpu.VMEM(high.shape, jnp.bfloat16),
            pltpu.VMEM(low.shape, jnp.bfloat16),
            pltpu.VMEM((sum(a.shape[0] for a in corner), width), jnp.float32),
            pltpu.VMEM(slab.shape, jnp.float32),
            pltpu.VMEM(slab.shape, jnp.float32),
            pltpu.SemaphoreType.DMA((4 + len(corner), len(cut_columns(width)))),
        ],
        compiler_params=pltpu.CompilerParams(vmem_limit_bytes=VMEM_LIMIT),
        cost_estimate=COST,
    )(*whole, *streamed)


def exchange(array, bit, size, axis):
    return lax.ppermute(array, axis, [(i, i ^ bit) for i in range(size)])


def summed_terms(value, depth):
    terms, reach = [value], 1
    while reach < depth:
        if reach > 1:
            terms = [sum(terms[1:], terms[0])]
        span = min(4, depth // reach)
        terms = terms + [exchange(terms[0], k * reach, depth, "prow") for k in range(1, span)]
        reach *= span
    return terms


def over_rest(arrays, bit, across):
    lower, arrays = 1, list(arrays)
    while lower <= bit:
        arrays += [across(array, lower) for array in arrays]
        lower *= 2
    return arrays


def body(sizes, slab, reflectors, factors):
    size, depth = sizes["pcol"], sizes["prow"]
    rows = slab.shape[0]
    block, nb = factors.shape[1:]
    high, low = size // 2, size // 4
    across = functools.partial(exchange, size=size, axis="pcol")
    me = lax.axis_index("pcol")
    place = jnp.arange(nb)
    order = (place[:, None] == ((place // block) ^ me) * block + place % block).astype(jnp.float32)

    by_high, by_low = across(reflectors, high), across(reflectors, low)
    corner = [across(by_high[0], low), across(by_low[1], high)]
    near = [array for held in (reflectors, by_low, by_high) for array in over_rest([held], low // 2, across)]
    (turned,) = small(turn_kernel, [factors.shape], factors, order)
    turned = over_rest([turned], low // 2, across)
    near, turned = lax.optimization_barrier((near, turned))
    kept = jax.ShapeDtypeStruct((PANELS * (nb - nb // 4), slab.shape[1]), jnp.bfloat16)
    total, near_high, near_low = products(near_kernel, [slab, *near], (2 * rows + nb // 4, nb), [kept, kept])
    terms = summed_terms(total, depth)
    terms, corner = lax.optimization_barrier((terms, corner))
    far = [array for held in corner for array in over_rest([held], low // 2, across)]
    inner, share = small(
        functools.partial(share_kernel, len(terms)), [(2 * rows, nb), ((1 + PANELS) * nb // 4, nb)], *terms, *turned
    )
    shares = [share] + [across(share, side * low) for side in range(1, 4)]
    (found,) = products(corner_kernel, [slab, *far], (2 * rows // 4, nb))
    return update(inner, summed_terms(found, depth), shares, slab, near_high, near_low, far)


def solution(mesh):
    in_specs = (P("pcol", "prow"), P(None, "pcol", "prow"), P(None, "pcol", None))
    out_specs = P("pcol", "prow")
    return jax.shard_map(functools.partial(body, dict(mesh.shape)), mesh=mesh, in_specs=in_specs, out_specs=out_specs, check_vma=False)
```

```python
import functools

import jax
import jax.numpy as jnp
from jax import lax
from jax.experimental import pallas as pl
from jax.experimental.pallas import tpu as pltpu
from jax.sharding import PartitionSpec as P


UNIT_LIMIT = 2048
TILE_LIMIT = 8192
VMEM_LIMIT = 32 * 1024 * 1024
SMALL_LIMIT = 8 * 1024 * 1024
COST = pl.CostEstimate(flops=1, bytes_accessed=1, transcendentals=0)
PANELS = 2
ROWS = (((1,), (1,)), ((), ()))
PLAIN = (((1,), (0,)), ((), ()))


def divisor(width, limit):
    for unit in (128, 1):
        fits = [t for t in range(unit, min(limit, width) + 1, unit) if width % t == 0]
        if fits:
            return max(fits)
    return width


def split(value):
    high = value.astype(jnp.bfloat16)
    return high, (value - high.astype(jnp.float32)).astype(jnp.bfloat16)


def dot(left, right, dims):
    return lax.dot_general(left, right, dims, preferred_element_type=jnp.float32)


def exact(left, right, dims):
    return lax.dot_general(left, right, dims, precision=lax.Precision.HIGHEST, preferred_element_type=jnp.float32)


def panel_rows(refs, panel):
    return jnp.concatenate([ref[panel] for ref in refs], axis=0)


def add_up(out_ref, value):
    @pl.when(pl.program_id(0) == 0)
    def _():
        out_ref[...] = value

    @pl.when(pl.program_id(0) > 0)
    def _():
        out_ref[...] += value


def near_kernel(slab_ref, *refs):
    vector_refs, out_ref = refs[:-1], refs[-1]
    rows, nb = slab_ref.shape[0], out_ref.shape[1]
    group = nb // 4
    (fh, fl), (sh, sl) = (split(panel_rows(vector_refs, p)) for p in range(PANELS))
    ch, cl = split(slab_ref[...])
    first = dot(jnp.concatenate([ch, cl], axis=0), fh, ROWS)
    first = first[:rows] + first[rows:] + dot(ch, fl, ROWS)
    high = jnp.concatenate([ch, fh[: 2 * group]], axis=0)
    low = jnp.concatenate([cl, fl[: 2 * group]], axis=0)
    second = dot(jnp.concatenate([high, low], axis=0), sh, ROWS)
    second = second[: high.shape[0]] + second[high.shape[0] :] + dot(high, sl, ROWS)
    inner, own, via = second[:rows], second[rows : rows + group], second[rows + group :]
    inner = jnp.concatenate([first, inner], axis=0)
    inner = jnp.concatenate([inner, jnp.zeros((2 * rows, group), jnp.float32)], axis=1)
    share = jnp.concatenate([own, via[:, 2 * group :]], axis=1)
    add_up(out_ref, jnp.concatenate([inner, share], axis=0))


def corner_kernel(slab_ref, *refs):
    vector_refs, out_ref = refs[:-1], refs[-1]
    rows, (part, nb) = slab_ref.shape[0], out_ref.shape
    (vh, vl), (ch, cl) = split(jnp.concatenate([ref[...] for ref in vector_refs], axis=0)), split(slab_ref[...])
    found = dot(jnp.concatenate([ch, cl], axis=0), vh, ROWS)
    found = found[:rows] + found[rows:] + dot(ch, vl, ROWS)
    found = jnp.concatenate([found[:, : nb // 4], found[:, nb // 4 :]], axis=0)
    add_up(out_ref, jnp.concatenate([found[k * part : (k + 1) * part] for k in range(4)], axis=1))


def turn_kernel(factors_ref, order_ref, out_ref):
    for p in range(PANELS):
        out_ref[p] = exact(factors_ref[p], order_ref[...], PLAIN)


def share_kernel(terms, *refs):
    term_refs, turned_refs, inner_ref, share_ref = refs[:terms], refs[terms:-2], *refs[-2:]
    group = share_ref.shape[0] // (1 + PANELS)
    nb = share_ref.shape[1]
    block = group // len(turned_refs)
    total = term_refs[0][...]
    for ref in term_refs[1:]:
        total += ref[...]
    inner_ref[...] = total[:-group]
    share_ref[:group] = total[-group:]
    lane = lax.broadcasted_iota(jnp.int32, (1, nb), 1)
    turned = [[from_place(ref[p], q, block, lane) for q, ref in enumerate(turned_refs)] for p in range(PANELS)]
    share_ref[group:] = jnp.concatenate([rows for part in turned for rows in part], axis=0)


def from_place(value, q, block, lane):
    width = value.shape[1]
    bit = 1
    while bit * block < width:
        if q & bit:
            shift = bit * block
            ahead, behind = pltpu.roll(value, width - shift, 1), pltpu.roll(value, shift, 1)
            value = jnp.where((lane // shift) % 2 == 0, ahead, behind)
        bit *= 2
    return value


def cut_columns(width):
    sub = divisor(width, UNIT_LIMIT)
    count = width // sub
    firsts = [0, *range(1, count, 2)] if count % 2 else list(range(0, count, 2))
    return [(begin * sub, (end - begin) * sub) for begin, end in zip(firsts, [*firsts[1:], count])]


def update_kernel(pieces, terms, *refs):
    near_ref, term_refs, share_refs = refs[0], refs[1 : 1 + terms], refs[1 + terms : 5 + terms]
    slab_ref, *vector_refs = refs[5 + terms : -5]
    out_ref, vectors, before, after, sems = refs[-5:]
    rows, nb = near_ref.shape[0] // PANELS, near_ref.shape[1]
    group = nb // 4
    block = PANELS * nb // len(pieces)
    parts = cut_columns(slab_ref.shape[1])

    for at, (begin, count) in enumerate(parts):
        columns = pl.ds(begin, count)
        pltpu.make_async_copy(slab_ref.at[:, columns], before.at[:, columns], sems.at[1, at]).start()
        for place, (ref, panel) in enumerate(pieces):
            ref = vector_refs[ref]
            source = ref.at[:, columns] if panel is None else ref.at[panel, :, columns]
            target = vectors.at[pl.ds(place * block, block), columns]
            pltpu.make_async_copy(source, target, sems.at[0, at]).start()

    total = term_refs[0][...]
    for ref in term_refs[1:]:
        total += ref[...]
    total = jnp.concatenate([total[:, k * group : (k + 1) * group] for k in range(4)], axis=0)
    total = near_ref[...] + jnp.concatenate([jnp.zeros((PANELS * rows, nb - group), jnp.float32), total], axis=1)
    lane = lax.broadcasted_iota(jnp.int32, (1, nb), 1)
    between, triangles = [], [[] for _ in range(PANELS)]
    for side in range(4):
        held = from_place(share_refs[side][...], side, group, lane)
        other = from_place(share_refs[side ^ 1][:group], side, group, lane)
        far = ((lane // group) ^ side) == 3
        between.append(jnp.where(far, other, held[:group]))
        for p in range(PANELS):
            triangles[p].append(held[(1 + p) * group : (2 + p) * group])
    between, first, second = (jnp.concatenate(pieces, axis=0) for pieces in (between, *triangles))
    scaled = exact(total[:rows], first, ROWS)
    inner = total[rows:] - exact(scaled, between, PLAIN)
    later = exact(inner, second, ROWS)
    both = jnp.concatenate(split(jnp.concatenate([scaled, later], axis=1)), axis=0)

    for at, (begin, count) in enumerate(parts):
        columns = pl.ds(begin, count)
        held = vectors.at[:, columns]
        pltpu.make_async_copy(held, held, sems.at[0, at]).wait()
        pltpu.make_async_copy(slab_ref.at[:, columns], before.at[:, columns], sems.at[1, at]).wait()
        high, low = split(vectors[:, columns])
        main = dot(both, high, PLAIN)
        rest = dot(both[:rows], low, PLAIN)
        after[:, columns] = before[:, columns] - (main[:rows] + main[rows:] + rest)
        pltpu.make_async_copy(after.at[:, columns], out_ref.at[:, columns], sems.at[2, at]).start()
    for at, (begin, count) in enumerate(parts):
        columns = pl.ds(begin, count)
        pltpu.make_async_copy(after.at[:, columns], out_ref.at[:, columns], sems.at[2, at]).wait()


def fixed(shape):
    return pl.BlockSpec(shape, lambda i: tuple(0 for _ in shape))


def moving(array, tile):
    lead = array.shape[:-1]
    return pl.BlockSpec((*lead, tile), lambda i: (*(0 for _ in lead), i))


def products(kernel, streamed, shape):
    width = streamed[0].shape[-1]
    tile = divisor(width, TILE_LIMIT)
    return pl.pallas_call(
        kernel,
        grid=(width // tile,),
        in_specs=[moving(a, tile) for a in streamed],
        out_specs=fixed(shape),
        out_shape=jax.ShapeDtypeStruct(shape, jnp.float32),
        compiler_params=pltpu.CompilerParams(vmem_limit_bytes=VMEM_LIMIT),
        cost_estimate=COST,
    )(*streamed)


def small(kernel, shapes, *arrays):
    return pl.pallas_call(
        kernel,
        out_shape=[jax.ShapeDtypeStruct(shape, jnp.float32) for shape in shapes],
        compiler_params=pltpu.CompilerParams(vmem_limit_bytes=SMALL_LIMIT),
        cost_estimate=COST,
    )(*arrays)


def update(near, terms, shares, slab, arrays, pieces):
    width, nb = slab.shape[1], near.shape[1]
    whole, streamed = [near, *terms, *shares], [slab, *arrays]
    return pl.pallas_call(
        functools.partial(update_kernel, pieces, len(terms)),
        in_specs=[pl.BlockSpec(memory_space=pltpu.VMEM)] * len(whole) + [pl.BlockSpec(memory_space=pl.ANY)] * len(streamed),
        out_specs=pl.BlockSpec(memory_space=pl.ANY),
        out_shape=jax.ShapeDtypeStruct(slab.shape, jnp.float32),
        scratch_shapes=[
            pltpu.VMEM((PANELS * nb, width), jnp.float32),
            pltpu.VMEM(slab.shape, jnp.float32),
            pltpu.VMEM(slab.shape, jnp.float32),
            pltpu.SemaphoreType.DMA((3, len(cut_columns(width)))),
        ],
        compiler_params=pltpu.CompilerParams(vmem_limit_bytes=VMEM_LIMIT),
        cost_estimate=COST,
    )(*whole, *streamed)


def exchange(array, bit, size, axis):
    return lax.ppermute(array, axis, [(i, i ^ bit) for i in range(size)])


def summed_terms(value, depth):
    terms, reach = [value], 1
    while reach < depth:
        if reach > 1:
            terms = [sum(terms[1:], terms[0])]
        span = min(4, depth // reach)
        terms = terms + [exchange(terms[0], k * reach, depth, "prow") for k in range(1, span)]
        reach *= span
    return terms


def over_rest(arrays, bit, across):
    lower, arrays = 1, list(arrays)
    while lower <= bit:
        arrays += [across(array, lower) for array in arrays]
        lower *= 2
    return arrays


def body(sizes, slab, reflectors, factors):
    size, depth = sizes["pcol"], sizes["prow"]
    rows = slab.shape[0]
    block, nb = factors.shape[1:]
    high, low = size // 2, size // 4
    across = functools.partial(exchange, size=size, axis="pcol")
    me = lax.axis_index("pcol")
    place = jnp.arange(nb)
    order = (place[:, None] == ((place // block) ^ me) * block + place % block).astype(jnp.float32)

    by_high, by_low = across(reflectors, high), across(reflectors, low)
    corner = [across(by_high[0], low), across(by_low[1], high)]
    near = [array for held in (reflectors, by_low, by_high) for array in over_rest([held], low // 2, across)]
    (turned,) = small(turn_kernel, [factors.shape], factors, order)
    turned = over_rest([turned], low // 2, across)
    near, turned = lax.optimization_barrier((near, turned))
    total = products(near_kernel, [slab, *near], (2 * rows + nb // 4, nb))
    terms = summed_terms(total, depth)
    terms, corner = lax.optimization_barrier((terms, corner))
    far = [array for held in corner for array in over_rest([held], low // 2, across)]
    inner, share = small(
        functools.partial(share_kernel, len(terms)), [(2 * rows, nb), ((1 + PANELS) * nb // 4, nb)], *terms, *turned
    )
    shares = [share] + [across(share, side * low) for side in range(1, 4)]
    found = products(corner_kernel, [slab, *far], (2 * rows // 4, nb))
    count, part = len(near), len(far) // PANELS
    pieces = [piece for p in range(PANELS) for piece in (*((at, p) for at in range(count)), *((count + p * part + at, None) for at in range(part)))]
    return update(inner, summed_terms(found, depth), shares, slab, [*near, *far], pieces)


def solution(mesh):
    in_specs = (P("pcol", "prow"), P(None, "pcol", "prow"), P(None, "pcol", None))
    out_specs = P("pcol", "prow")
    return jax.shard_map(functools.partial(body, dict(mesh.shape)), mesh=mesh, in_specs=in_specs, out_specs=out_specs, check_vma=False)
```

```python
import functools

import jax
import jax.numpy as jnp
from jax import lax
from jax.experimental import pallas as pl
from jax.experimental.pallas import tpu as pltpu
from jax.sharding import PartitionSpec as P


UNIT_LIMIT = 2048
TILE_LIMIT = 8192
VMEM_LIMIT = 32 * 1024 * 1024
SMALL_LIMIT = 8 * 1024 * 1024
COST = pl.CostEstimate(flops=1, bytes_accessed=1, transcendentals=0)
PANELS = 2
ROWS = (((1,), (1,)), ((), ()))
PLAIN = (((1,), (0,)), ((), ()))


def divisor(width, limit):
    for unit in (128, 1):
        fits = [t for t in range(unit, min(limit, width) + 1, unit) if width % t == 0]
        if fits:
            return max(fits)
    return width


def split(value):
    high = value.astype(jnp.bfloat16)
    return high, (value - high.astype(jnp.float32)).astype(jnp.bfloat16)


def dot(left, right, dims):
    return lax.dot_general(left, right, dims, preferred_element_type=jnp.float32)


def exact(left, right, dims):
    return lax.dot_general(left, right, dims, precision=lax.Precision.HIGHEST, preferred_element_type=jnp.float32)


def column_tiles(width, limit):
    tile = divisor(width, limit)
    return [pl.ds(begin, tile) for begin in range(0, width, tile)]


def panel_rows(refs, panel, columns):
    return jnp.concatenate([ref[panel, :, columns] for ref in refs], axis=0)


def near_kernel(slab_ref, *refs):
    vector_refs, out_ref = refs[:-1], refs[-1]
    (rows, width), nb = slab_ref.shape, out_ref.shape[1]
    group = nb // 4
    total = 0
    for columns in column_tiles(width, TILE_LIMIT):
        (fh, fl), (sh, sl) = (split(panel_rows(vector_refs, p, columns)) for p in range(PANELS))
        ch, cl = split(slab_ref[:, columns])
        first = dot(jnp.concatenate([ch, cl], axis=0), fh, ROWS)
        first = first[:rows] + first[rows:] + dot(ch, fl, ROWS)
        high = jnp.concatenate([ch, fh[: 2 * group]], axis=0)
        low = jnp.concatenate([cl, fl[: 2 * group]], axis=0)
        second = dot(jnp.concatenate([high, low], axis=0), sh, ROWS)
        second = second[: high.shape[0]] + second[high.shape[0] :] + dot(high, sl, ROWS)
        total += jnp.concatenate([first, second], axis=0)
    inner, own, via = total[: 2 * rows], total[2 * rows : 2 * rows + group], total[2 * rows + group :]
    inner = jnp.concatenate([inner, jnp.zeros((2 * rows, group), jnp.float32)], axis=1)
    share = jnp.concatenate([own, via[:, 2 * group :]], axis=1)
    out_ref[...] = jnp.concatenate([inner, share], axis=0)


def corner_kernel(slab_ref, *refs):
    vector_refs, out_ref = refs[:-1], refs[-1]
    (rows, width), (part, nb) = slab_ref.shape, out_ref.shape
    total = 0
    for columns in column_tiles(width, TILE_LIMIT):
        vh, vl = split(jnp.concatenate([ref[:, columns] for ref in vector_refs], axis=0))
        ch, cl = split(slab_ref[:, columns])
        found = dot(jnp.concatenate([ch, cl], axis=0), vh, ROWS)
        total += found[:rows] + found[rows:] + dot(ch, vl, ROWS)
    total = jnp.concatenate([total[:, : nb // 4], total[:, nb // 4 :]], axis=0)
    out_ref[...] = jnp.concatenate([total[k * part : (k + 1) * part] for k in range(4)], axis=1)


def turn_kernel(factors_ref, order_ref, out_ref):
    for p in range(PANELS):
        out_ref[p] = exact(factors_ref[p], order_ref[...], PLAIN)


def share_kernel(terms, *refs):
    term_refs, turned_refs, inner_ref, share_ref = refs[:terms], refs[terms:-2], *refs[-2:]
    group = share_ref.shape[0] // (1 + PANELS)
    nb = share_ref.shape[1]
    block = group // len(turned_refs)
    total = term_refs[0][...]
    for ref in term_refs[1:]:
        total += ref[...]
    inner_ref[...] = total[:-group]
    share_ref[:group] = total[-group:]
    lane = lax.broadcasted_iota(jnp.int32, (1, nb), 1)
    turned = [[from_place(ref[p], q, block, lane) for q, ref in enumerate(turned_refs)] for p in range(PANELS)]
    share_ref[group:] = jnp.concatenate([rows for part in turned for rows in part], axis=0)


def from_place(value, q, block, lane):
    width = value.shape[1]
    bit = 1
    while bit * block < width:
        if q & bit:
            shift = bit * block
            ahead, behind = pltpu.roll(value, width - shift, 1), pltpu.roll(value, shift, 1)
            value = jnp.where((lane // shift) % 2 == 0, ahead, behind)
        bit *= 2
    return value


def update_kernel(pieces, terms, *refs):
    near_ref, term_refs, share_refs = refs[0], refs[1 : 1 + terms], refs[1 + terms : 5 + terms]
    slab_ref, *vector_refs = refs[5 + terms : -3]
    out_ref, after, sems = refs[-3:]
    (rows, width), nb = slab_ref.shape, near_ref.shape[1]
    group = nb // 4

    total = term_refs[0][...]
    for ref in term_refs[1:]:
        total += ref[...]
    total = jnp.concatenate([total[:, k * group : (k + 1) * group] for k in range(4)], axis=0)
    total = near_ref[...] + jnp.concatenate([jnp.zeros((PANELS * rows, nb - group), jnp.float32), total], axis=1)
    lane = lax.broadcasted_iota(jnp.int32, (1, nb), 1)
    between, triangles = [], [[] for _ in range(PANELS)]
    for side in range(4):
        held = from_place(share_refs[side][...], side, group, lane)
        other = from_place(share_refs[side ^ 1][:group], side, group, lane)
        far = ((lane // group) ^ side) == 3
        between.append(jnp.where(far, other, held[:group]))
        for p in range(PANELS):
            triangles[p].append(held[(1 + p) * group : (2 + p) * group])
    between, first, second = (jnp.concatenate(pieces, axis=0) for pieces in (between, *triangles))
    scaled = exact(total[:rows], first, ROWS)
    inner = total[rows:] - exact(scaled, between, PLAIN)
    later = exact(inner, second, ROWS)
    both = jnp.concatenate(split(jnp.concatenate([scaled, later], axis=1)), axis=0)

    copies = []
    for at, columns in enumerate(column_tiles(width, UNIT_LIMIT)):
        blocks = [vector_refs[ref][:, columns] if p is None else vector_refs[ref][p, :, columns] for ref, p in pieces]
        high, low = split(jnp.concatenate(blocks, axis=0))
        main = dot(both, high, PLAIN)
        rest = dot(both[:rows], low, PLAIN)
        after[:, columns] = slab_ref[:, columns] - (main[:rows] + main[rows:] + rest)
        copies.append(pltpu.make_async_copy(after.at[:, columns], out_ref.at[:, columns], sems.at[at]))
        copies[-1].start()
    for copy in copies:
        copy.wait()


def products(kernel, arrays, shape):
    return pl.pallas_call(
        kernel,
        in_specs=[pl.BlockSpec(memory_space=pltpu.VMEM)] * len(arrays),
        out_specs=pl.BlockSpec(memory_space=pltpu.VMEM),
        out_shape=jax.ShapeDtypeStruct(shape, jnp.float32),
        compiler_params=pltpu.CompilerParams(vmem_limit_bytes=VMEM_LIMIT),
        cost_estimate=COST,
    )(*arrays)


def small(kernel, shapes, *arrays):
    return pl.pallas_call(
        kernel,
        out_shape=[jax.ShapeDtypeStruct(shape, jnp.float32) for shape in shapes],
        compiler_params=pltpu.CompilerParams(vmem_limit_bytes=SMALL_LIMIT),
        cost_estimate=COST,
    )(*arrays)


def update(near, terms, shares, slab, arrays, pieces):
    width = slab.shape[1]
    whole = [near, *terms, *shares, slab, *arrays]
    return pl.pallas_call(
        functools.partial(update_kernel, pieces, len(terms)),
        in_specs=[pl.BlockSpec(memory_space=pltpu.VMEM)] * len(whole),
        out_specs=pl.BlockSpec(memory_space=pl.ANY),
        out_shape=jax.ShapeDtypeStruct(slab.shape, jnp.float32),
        scratch_shapes=[
            pltpu.VMEM(slab.shape, jnp.float32),
            pltpu.SemaphoreType.DMA((len(column_tiles(width, UNIT_LIMIT)),)),
        ],
        compiler_params=pltpu.CompilerParams(vmem_limit_bytes=VMEM_LIMIT),
        cost_estimate=COST,
    )(*whole)


def exchange(array, bit, size, axis):
    return lax.ppermute(array, axis, [(i, i ^ bit) for i in range(size)])


def summed_terms(value, depth):
    terms, reach = [value], 1
    while reach < depth:
        if reach > 1:
            terms = [sum(terms[1:], terms[0])]
        span = min(4, depth // reach)
        terms = terms + [exchange(terms[0], k * reach, depth, "prow") for k in range(1, span)]
        reach *= span
    return terms


def over_rest(arrays, bit, across):
    lower, arrays = 1, list(arrays)
    while lower <= bit:
        arrays += [across(array, lower) for array in arrays]
        lower *= 2
    return arrays


def body(sizes, slab, reflectors, factors):
    size, depth = sizes["pcol"], sizes["prow"]
    rows = slab.shape[0]
    block, nb = factors.shape[1:]
    high, low = size // 2, size // 4
    across = functools.partial(exchange, size=size, axis="pcol")
    me = lax.axis_index("pcol")
    place = jnp.arange(nb)
    order = (place[:, None] == ((place // block) ^ me) * block + place % block).astype(jnp.float32)

    by_high, by_low = across(reflectors, high), across(reflectors, low)
    corner = [across(by_high[0], low), across(by_low[1], high)]
    near = [array for held in (reflectors, by_low, by_high) for array in over_rest([held], low // 2, across)]
    (turned,) = small(turn_kernel, [factors.shape], factors, order)
    turned = over_rest([turned], low // 2, across)
    near, turned = lax.optimization_barrier((near, turned))
    total = products(near_kernel, [slab, *near], (2 * rows + nb // 4, nb))
    terms = summed_terms(total, depth)
    terms, corner = lax.optimization_barrier((terms, corner))
    far = [array for held in corner for array in over_rest([held], low // 2, across)]
    inner, share = small(
        functools.partial(share_kernel, len(terms)), [(2 * rows, nb), ((1 + PANELS) * nb // 4, nb)], *terms, *turned
    )
    shares = [share] + [across(share, side * low) for side in range(1, 4)]
    found = products(corner_kernel, [slab, *far], (2 * rows // 4, nb))
    count, part = len(near), len(far) // PANELS
    pieces = [piece for p in range(PANELS) for piece in (*((at, p) for at in range(count)), *((count + p * part + at, None) for at in range(part)))]
    return update(inner, summed_terms(found, depth), shares, slab, [*near, *far], pieces)


def solution(mesh):
    in_specs = (P("pcol", "prow"), P(None, "pcol", "prow"), P(None, "pcol", None))
    out_specs = P("pcol", "prow")
    return jax.shard_map(functools.partial(body, dict(mesh.shape)), mesh=mesh, in_specs=in_specs, out_specs=out_specs, check_vma=False)
```

```python
import functools

import jax
import jax.numpy as jnp
from jax import lax
from jax.experimental import pallas as pl
from jax.experimental.pallas import tpu as pltpu
from jax.sharding import PartitionSpec as P


UNIT_LIMIT = 2048
TILE_LIMIT = 8192
VMEM_LIMIT = 32 * 1024 * 1024
SMALL_LIMIT = 8 * 1024 * 1024
COST = pl.CostEstimate(flops=1, bytes_accessed=1, transcendentals=0)
PANELS = 2
ROWS = (((1,), (1,)), ((), ()))
PLAIN = (((1,), (0,)), ((), ()))


def divisor(width, limit):
    for unit in (128, 1):
        fits = [t for t in range(unit, min(limit, width) + 1, unit) if width % t == 0]
        if fits:
            return max(fits)
    return width


def split(value):
    high = value.astype(jnp.bfloat16)
    return high, (value - high.astype(jnp.float32)).astype(jnp.bfloat16)


def dot(left, right, dims):
    return lax.dot_general(left, right, dims, preferred_element_type=jnp.float32)


def exact(left, right, dims):
    return lax.dot_general(left, right, dims, precision=lax.Precision.HIGHEST, preferred_element_type=jnp.float32)


def column_tiles(width, limit):
    tile = divisor(width, limit)
    return [pl.ds(begin, tile) for begin in range(0, width, tile)]


def panel_rows(refs, panel, columns):
    return jnp.concatenate([ref[panel, :, columns] for ref in refs], axis=0)


def near_kernel(slab_ref, *refs):
    vector_refs, out_ref = refs[:-1], refs[-1]
    (rows, width), nb = slab_ref.shape, out_ref.shape[1]
    group = nb // 4
    total = 0
    for columns in column_tiles(width, TILE_LIMIT):
        (fh, fl), (sh, sl) = (split(panel_rows(vector_refs, p, columns)) for p in range(PANELS))
        ch, cl = split(slab_ref[:, columns])
        first = dot(jnp.concatenate([ch, cl], axis=0), fh, ROWS)
        first = first[:rows] + first[rows:] + dot(ch, fl, ROWS)
        high = jnp.concatenate([ch, fh[: 2 * group]], axis=0)
        low = jnp.concatenate([cl, fl[: 2 * group]], axis=0)
        second = dot(jnp.concatenate([high, low], axis=0), sh, ROWS)
        second = second[: high.shape[0]] + second[high.shape[0] :] + dot(high, sl, ROWS)
        total += jnp.concatenate([first, second], axis=0)
    inner, own, via = total[: 2 * rows], total[2 * rows : 2 * rows + group], total[2 * rows + group :]
    inner = jnp.concatenate([inner, jnp.zeros((2 * rows, group), jnp.float32)], axis=1)
    share = jnp.concatenate([own, via[:, 2 * group :]], axis=1)
    out_ref[...] = jnp.concatenate([inner, share], axis=0)


def corner_kernel(slab_ref, *refs):
    vector_refs, out_ref = refs[:-1], refs[-1]
    (rows, width), (part, nb) = slab_ref.shape, out_ref.shape
    total = 0
    for columns in column_tiles(width, TILE_LIMIT):
        vh, vl = split(jnp.concatenate([ref[:, columns] for ref in vector_refs], axis=0))
        ch, cl = split(slab_ref[:, columns])
        found = dot(jnp.concatenate([ch, cl], axis=0), vh, ROWS)
        total += found[:rows] + found[rows:] + dot(ch, vl, ROWS)
    total = jnp.concatenate([total[:, : nb // 4], total[:, nb // 4 :]], axis=0)
    out_ref[...] = jnp.concatenate([total[k * part : (k + 1) * part] for k in range(4)], axis=1)


def turn_kernel(factors_ref, order_ref, out_ref):
    for p in range(PANELS):
        out_ref[p] = exact(factors_ref[p], order_ref[...], PLAIN)


def share_kernel(terms, *refs):
    term_refs, turned_refs, inner_ref, share_ref = refs[:terms], refs[terms:-2], *refs[-2:]
    group = share_ref.shape[0] // (1 + PANELS)
    nb = share_ref.shape[1]
    block = group // len(turned_refs)
    total = term_refs[0][...]
    for ref in term_refs[1:]:
        total += ref[...]
    inner_ref[...] = total[:-group]
    share_ref[:group] = total[-group:]
    lane = lax.broadcasted_iota(jnp.int32, (1, nb), 1)
    turned = [[from_place(ref[p], q, block, lane) for q, ref in enumerate(turned_refs)] for p in range(PANELS)]
    share_ref[group:] = jnp.concatenate([rows for part in turned for rows in part], axis=0)


def from_place(value, q, block, lane):
    width = value.shape[1]
    bit = 1
    while bit * block < width:
        if q & bit:
            shift = bit * block
            ahead, behind = pltpu.roll(value, width - shift, 1), pltpu.roll(value, shift, 1)
            value = jnp.where((lane // shift) % 2 == 0, ahead, behind)
        bit *= 2
    return value


def matrices_kernel(*refs):
    share_refs, between_ref, triangle_refs = refs[:4], refs[4], refs[5:]
    nb = between_ref.shape[0]
    group = nb // 4
    lane = lax.broadcasted_iota(jnp.int32, (1, nb), 1)
    triangles = [[] for _ in range(PANELS)]
    for side in range(4):
        held = from_place(share_refs[side][...], side, group, lane)
        other = from_place(share_refs[side ^ 1][:group], side, group, lane)
        far = ((lane // group) ^ side) == 3
        between_ref[side * group : (side + 1) * group] = jnp.where(far, other, held[:group])
        for p in range(PANELS):
            triangles[p].append(held[(1 + p) * group : (2 + p) * group])
    for p in range(PANELS):
        triangle_refs[p][...] = jnp.concatenate(triangles[p], axis=0).T


def update_kernel(pieces, terms, *refs):
    near_ref, term_refs, (between_ref, first_ref, second_ref) = refs[0], refs[1 : 1 + terms], refs[1 + terms : 4 + terms]
    slab_ref, *vector_refs = refs[4 + terms : -3]
    out_ref, after, sems = refs[-3:]
    (rows, width), nb = slab_ref.shape, near_ref.shape[1]
    group = nb // 4

    total = term_refs[0][...]
    for ref in term_refs[1:]:
        total += ref[...]
    total = jnp.concatenate([total[:, k * group : (k + 1) * group] for k in range(4)], axis=0)
    total = near_ref[...] + jnp.concatenate([jnp.zeros((PANELS * rows, nb - group), jnp.float32), total], axis=1)
    scaled = exact(total[:rows], first_ref[...], PLAIN)
    inner = total[rows:] - exact(scaled, between_ref[...], PLAIN)
    later = exact(inner, second_ref[...], PLAIN)
    both = jnp.concatenate(split(jnp.concatenate([scaled, later], axis=1)), axis=0)

    copies = []
    for at, columns in enumerate(column_tiles(width, UNIT_LIMIT)):
        blocks = [vector_refs[ref][:, columns] if p is None else vector_refs[ref][p, :, columns] for ref, p in pieces]
        high, low = split(jnp.concatenate(blocks, axis=0))
        main = dot(both, high, PLAIN)
        rest = dot(both[:rows], low, PLAIN)
        after[:, columns] = slab_ref[:, columns] - (main[:rows] + main[rows:] + rest)
        copies.append(pltpu.make_async_copy(after.at[:, columns], out_ref.at[:, columns], sems.at[at]))
        copies[-1].start()
    for copy in copies:
        copy.wait()


def products(kernel, arrays, shape):
    return pl.pallas_call(
        kernel,
        in_specs=[pl.BlockSpec(memory_space=pltpu.VMEM)] * len(arrays),
        out_specs=pl.BlockSpec(memory_space=pltpu.VMEM),
        out_shape=jax.ShapeDtypeStruct(shape, jnp.float32),
        compiler_params=pltpu.CompilerParams(vmem_limit_bytes=VMEM_LIMIT),
        cost_estimate=COST,
    )(*arrays)


def small(kernel, shapes, *arrays):
    return pl.pallas_call(
        kernel,
        out_shape=[jax.ShapeDtypeStruct(shape, jnp.float32) for shape in shapes],
        compiler_params=pltpu.CompilerParams(vmem_limit_bytes=SMALL_LIMIT),
        cost_estimate=COST,
    )(*arrays)


def update(near, terms, matrices, slab, arrays, pieces):
    width = slab.shape[1]
    whole = [near, *terms, *matrices, slab, *arrays]
    return pl.pallas_call(
        functools.partial(update_kernel, pieces, len(terms)),
        in_specs=[pl.BlockSpec(memory_space=pltpu.VMEM)] * len(whole),
        out_specs=pl.BlockSpec(memory_space=pl.ANY),
        out_shape=jax.ShapeDtypeStruct(slab.shape, jnp.float32),
        scratch_shapes=[
            pltpu.VMEM(slab.shape, jnp.float32),
            pltpu.SemaphoreType.DMA((len(column_tiles(width, UNIT_LIMIT)),)),
        ],
        compiler_params=pltpu.CompilerParams(vmem_limit_bytes=VMEM_LIMIT),
        cost_estimate=COST,
    )(*whole)


def exchange(array, bit, size, axis):
    return lax.ppermute(array, axis, [(i, i ^ bit) for i in range(size)])


def summed_terms(value, depth, step):
    terms, reach = [value], 1
    while reach < depth:
        value = sum(terms[1:], terms[0])
        span = min(step, depth // reach)
        terms = [value] + [exchange(value, k * reach, depth, "prow") for k in range(1, span)]
        reach *= span
    return terms


def over_rest(arrays, bit, across):
    lower, arrays = 1, list(arrays)
    while lower <= bit:
        arrays += [across(array, lower) for array in arrays]
        lower *= 2
    return arrays


def body(sizes, slab, reflectors, factors):
    size, depth = sizes["pcol"], sizes["prow"]
    rows = slab.shape[0]
    block, nb = factors.shape[1:]
    high, low = size // 2, size // 4
    across = functools.partial(exchange, size=size, axis="pcol")
    me = lax.axis_index("pcol")
    place = jnp.arange(nb)
    order = (place[:, None] == ((place // block) ^ me) * block + place % block).astype(jnp.float32)

    by_high, by_low = across(reflectors, high), across(reflectors, low)
    corner = [across(by_high[0], low), across(by_low[1], high)]
    near = [array for held in (reflectors, by_low, by_high) for array in over_rest([held], low // 2, across)]
    (turned,) = small(turn_kernel, [factors.shape], factors, order)
    turned = over_rest([turned], low // 2, across)
    near, turned = lax.optimization_barrier((near, turned))
    total = products(near_kernel, [slab, *near], (2 * rows + nb // 4, nb))
    terms = summed_terms(total, depth, 4)
    terms, corner = lax.optimization_barrier((terms, corner))
    inner, share = small(
        functools.partial(share_kernel, len(terms)), [(2 * rows, nb), ((1 + PANELS) * nb // 4, nb)], *terms, *turned
    )
    shares = [share] + [across(share, side * low) for side in range(1, 4)]
    far = [array for held in corner for array in over_rest([held], low // 2, across)]
    matrices = small(matrices_kernel, [(nb, nb)] * (1 + PANELS), *shares)
    found = products(corner_kernel, [slab, *far], (2 * rows // 4, nb))
    count, part = len(near), len(far) // PANELS
    pieces = [piece for p in range(PANELS) for piece in (*((at, p) for at in range(count)), *((count + p * part + at, None) for at in range(part)))]
    return update(inner, summed_terms(found, depth, 2), matrices, slab, [*near, *far], pieces)


def solution(mesh):
    in_specs = (P("pcol", "prow"), P(None, "pcol", "prow"), P(None, "pcol", None))
    out_specs = P("pcol", "prow")
    return jax.shard_map(functools.partial(body, dict(mesh.shape)), mesh=mesh, in_specs=in_specs, out_specs=out_specs, check_vma=False)
```

```python
import functools

import jax
import jax.numpy as jnp
from jax import lax
from jax.experimental import pallas as pl
from jax.experimental.pallas import tpu as pltpu
from jax.sharding import PartitionSpec as P


UNIT_LIMIT = 2048
TILE_LIMIT = 8192
VMEM_LIMIT = 32 * 1024 * 1024
SMALL_LIMIT = 8 * 1024 * 1024
COST = pl.CostEstimate(flops=1, bytes_accessed=1, transcendentals=0)
PANELS = 2
ROWS = (((1,), (1,)), ((), ()))
PLAIN = (((1,), (0,)), ((), ()))


def divisor(width, limit):
    for unit in (128, 1):
        fits = [t for t in range(unit, min(limit, width) + 1, unit) if width % t == 0]
        if fits:
            return max(fits)
    return width


def split(value):
    high = value.astype(jnp.bfloat16)
    return high, (value - high.astype(jnp.float32)).astype(jnp.bfloat16)


def dot(left, right, dims):
    return lax.dot_general(left, right, dims, preferred_element_type=jnp.float32)


def exact(left, right, dims):
    return lax.dot_general(left, right, dims, precision=lax.Precision.HIGHEST, preferred_element_type=jnp.float32)


def column_tiles(width, limit):
    tile = divisor(width, limit)
    return [pl.ds(begin, tile) for begin in range(0, width, tile)]


def panel_rows(refs, panel, columns):
    return jnp.concatenate([ref[panel, :, columns] for ref in refs], axis=0)


def near_kernel(kept, slab_ref, *refs):
    vector_refs, out_ref, kept_refs = refs[: -1 - kept], refs[-1 - kept], refs[len(refs) - kept :]
    for ref, kept_ref in zip(vector_refs[1:], kept_refs):
        kept_ref[...] = ref[...]
    (rows, width), nb = slab_ref.shape, out_ref.shape[1]
    group = nb // 4
    total = 0
    for columns in column_tiles(width, TILE_LIMIT):
        (fh, fl), (sh, sl) = (split(panel_rows(vector_refs, p, columns)) for p in range(PANELS))
        ch, cl = split(slab_ref[:, columns])
        first = dot(jnp.concatenate([ch, cl], axis=0), fh, ROWS)
        first = first[:rows] + first[rows:] + dot(ch, fl, ROWS)
        high = jnp.concatenate([ch, fh[: 2 * group]], axis=0)
        low = jnp.concatenate([cl, fl[: 2 * group]], axis=0)
        second = dot(jnp.concatenate([high, low], axis=0), sh, ROWS)
        second = second[: high.shape[0]] + second[high.shape[0] :] + dot(high, sl, ROWS)
        total += jnp.concatenate([first, second], axis=0)
    inner, own, via = total[: 2 * rows], total[2 * rows : 2 * rows + group], total[2 * rows + group :]
    inner = jnp.concatenate([inner, jnp.zeros((2 * rows, group), jnp.float32)], axis=1)
    share = jnp.concatenate([own, via[:, 2 * group :]], axis=1)
    out_ref[...] = jnp.concatenate([inner, share], axis=0)


def corner_kernel(slab_ref, *refs):
    vector_refs, out_ref = refs[:-1], refs[-1]
    (rows, width), (part, nb) = slab_ref.shape, out_ref.shape
    total = 0
    for columns in column_tiles(width, TILE_LIMIT):
        vh, vl = split(jnp.concatenate([ref[:, columns] for ref in vector_refs], axis=0))
        ch, cl = split(slab_ref[:, columns])
        found = dot(jnp.concatenate([ch, cl], axis=0), vh, ROWS)
        total += found[:rows] + found[rows:] + dot(ch, vl, ROWS)
    total = jnp.concatenate([total[:, : nb // 4], total[:, nb // 4 :]], axis=0)
    out_ref[...] = jnp.concatenate([total[k * part : (k + 1) * part] for k in range(4)], axis=1)


def turn_kernel(order_ref, *refs):
    factor_refs, out_ref = refs[:-1], refs[-1]
    rows = [ref[p] for p in range(PANELS) for ref in factor_refs]
    out_ref[...] = exact(jnp.concatenate(rows, axis=0), order_ref[...], PLAIN)


def share_kernel(terms, *refs):
    term_refs, turned_ref, inner_ref, share_ref = refs[:terms], *refs[terms:]
    group = share_ref.shape[0] // (1 + PANELS)
    total = term_refs[0][...]
    for ref in term_refs[1:]:
        total += ref[...]
    inner_ref[...] = total[:-group]
    share_ref[:group] = total[-group:]
    share_ref[group:] = turned_ref[...]


def from_place(value, q, block, lane):
    width = value.shape[1]
    bit = 1
    while bit * block < width:
        if q & bit:
            shift = bit * block
            ahead, behind = pltpu.roll(value, width - shift, 1), pltpu.roll(value, shift, 1)
            value = jnp.where((lane // shift) % 2 == 0, ahead, behind)
        bit *= 2
    return value


def matrices_kernel(*refs):
    share_refs, between_ref, triangle_refs = refs[:4], refs[4], refs[5:]
    nb = between_ref.shape[0]
    group = nb // 4
    lane = lax.broadcasted_iota(jnp.int32, (1, nb), 1)
    triangles = [[] for _ in range(PANELS)]
    for side in range(4):
        held = from_place(share_refs[side][...], side, group, lane)
        other = from_place(share_refs[side ^ 1][:group], side, group, lane)
        far = ((lane // group) ^ side) == 3
        between_ref[side * group : (side + 1) * group] = jnp.where(far, other, held[:group])
        for p in range(PANELS):
            triangles[p].append(held[(1 + p) * group : (2 + p) * group])
    for p in range(PANELS):
        triangle_refs[p][...] = jnp.concatenate(triangles[p], axis=0).T


def update_kernel(pieces, terms, *refs):
    near_ref, term_refs, (between_ref, first_ref, second_ref) = refs[0], refs[1 : 1 + terms], refs[1 + terms : 4 + terms]
    slab_ref, *vector_refs = refs[4 + terms : -3]
    out_ref, after, sems = refs[-3:]
    (rows, width), nb = slab_ref.shape, near_ref.shape[1]
    group = nb // 4

    total = term_refs[0][...]
    for ref in term_refs[1:]:
        total += ref[...]
    total = jnp.concatenate([total[:, k * group : (k + 1) * group] for k in range(4)], axis=0)
    total = near_ref[...] + jnp.concatenate([jnp.zeros((PANELS * rows, nb - group), jnp.float32), total], axis=1)
    scaled = exact(total[:rows], first_ref[...], PLAIN)
    inner = total[rows:] - exact(scaled, between_ref[...], PLAIN)
    later = exact(inner, second_ref[...], PLAIN)
    both = jnp.concatenate(split(jnp.concatenate([scaled, later], axis=1)), axis=0)

    copies = []
    for at, columns in enumerate(column_tiles(width, UNIT_LIMIT)):
        blocks = [vector_refs[ref][:, columns] if p is None else vector_refs[ref][p, :, columns] for ref, p in pieces]
        high, low = split(jnp.concatenate(blocks, axis=0))
        main = dot(both, high, PLAIN)
        rest = dot(both[:rows], low, PLAIN)
        after[:, columns] = slab_ref[:, columns] - (main[:rows] + main[rows:] + rest)
        copies.append(pltpu.make_async_copy(after.at[:, columns], out_ref.at[:, columns], sems.at[at]))
        copies[-1].start()
    for copy in copies:
        copy.wait()


def products(kernel, arrays, *shapes):
    return pl.pallas_call(
        kernel,
        in_specs=[pl.BlockSpec(memory_space=pltpu.VMEM)] * len(arrays),
        out_specs=[pl.BlockSpec(memory_space=pltpu.VMEM)] * len(shapes),
        out_shape=[jax.ShapeDtypeStruct(shape, jnp.float32) for shape in shapes],
        compiler_params=pltpu.CompilerParams(vmem_limit_bytes=VMEM_LIMIT),
        cost_estimate=COST,
    )(*arrays)


def small(kernel, shapes, *arrays):
    return pl.pallas_call(
        kernel,
        out_shape=[jax.ShapeDtypeStruct(shape, jnp.float32) for shape in shapes],
        compiler_params=pltpu.CompilerParams(vmem_limit_bytes=SMALL_LIMIT),
        cost_estimate=COST,
    )(*arrays)


def update(near, terms, matrices, slab, arrays, pieces):
    width = slab.shape[1]
    whole = [near, *terms, *matrices, slab, *arrays]
    return pl.pallas_call(
        functools.partial(update_kernel, pieces, len(terms)),
        in_specs=[pl.BlockSpec(memory_space=pltpu.VMEM)] * len(whole),
        out_specs=pl.BlockSpec(memory_space=pl.ANY),
        out_shape=jax.ShapeDtypeStruct(slab.shape, jnp.float32),
        scratch_shapes=[
            pltpu.VMEM(slab.shape, jnp.float32),
            pltpu.SemaphoreType.DMA((len(column_tiles(width, UNIT_LIMIT)),)),
        ],
        compiler_params=pltpu.CompilerParams(vmem_limit_bytes=VMEM_LIMIT),
        cost_estimate=COST,
    )(*whole)


def exchange(array, partner, size, axis):
    return lax.ppermute(array, axis, [(i, i ^ partner(i)) for i in range(size)])


def summed_terms(value, depth, step):
    terms, reach = [value], 1
    while reach < depth:
        value = sum(terms[1:], terms[0])
        span = min(step, depth // reach)
        terms = [value] + [exchange(value, lambda i, k=k: k * reach, depth, "prow") for k in range(1, span)]
        reach *= span
    return terms


def over_rest(held, low, across):
    bit = 1
    while bit < low:
        for q, array in list(held.items()):
            turned = q // low in (1, 2) and bit == 1
            held[(q ^ (3 * low) if turned else q) | bit] = across(array, lambda i, bit=bit: bit)
        bit *= 2
    return held


def body(sizes, slab, reflectors, factors):
    size, depth = sizes["pcol"], sizes["prow"]
    rows = slab.shape[0]
    block, nb = factors.shape[1:]
    high, low = size // 2, size // 4
    across = functools.partial(exchange, size=size, axis="pcol")
    opposite = low > 1
    first = lambda i: high if opposite and i % 2 else low
    second = lambda i: low if opposite and i % 2 else high
    both = lambda i: high | low

    me = lax.axis_index("pcol")
    column = jnp.arange(nb)
    place = column // block
    role = place // low
    bits = jnp.where((role == 1) | (role == 2), jnp.where(opposite & (me % 2 == 1), 3 - role, role), role) * low + place % low
    order = (column[:, None] == ((bits ^ me) * block + column % block)[None, :]).astype(jnp.float32)

    by_first, by_second = across(reflectors, first), across(reflectors, second)
    corner = [across(by_second[0], first), across(by_first[1], second)]
    near = over_rest({0: reflectors, low: by_first, high: by_second}, low, across)
    near = [near[q] for q in sorted(near)]
    group = over_rest({0: factors}, low, across)
    (turned,) = small(turn_kernel, [(PANELS * nb // 4, nb)], order, *[group[q] for q in sorted(group)])
    near, turned = lax.optimization_barrier((near, turned))
    mates = size // 4 - 1
    total, *kept = products(
        functools.partial(near_kernel, mates), [slab, *near], (2 * rows + nb // 4, nb), *[reflectors.shape] * mates
    )
    near[1 : 1 + mates] = kept
    terms = summed_terms(total, depth, 4)
    terms, corner = lax.optimization_barrier((terms, corner))
    inner, share = small(
        functools.partial(share_kernel, len(terms)), [(2 * rows, nb), ((1 + PANELS) * nb // 4, nb)], *terms, turned
    )
    shares = [share, *(across(share, way) for way in (first, second, both))]
    far = [over_rest({high | low: array}, low, across) for array in corner]
    far = [held[q] for held in far for q in sorted(held)]
    matrices = small(matrices_kernel, [(nb, nb)] * (1 + PANELS), *shares)
    (found,) = products(corner_kernel, [slab, *far], (2 * rows // 4, nb))
    count, part = len(near), len(far) // PANELS
    pieces = [piece for p in range(PANELS) for piece in (*((at, p) for at in range(count)), *((count + p * part + at, None) for at in range(part)))]
    return update(inner, summed_terms(found, depth, 4), matrices, slab, [*near, *far], pieces)


def solution(mesh):
    in_specs = (P("pcol", "prow"), P(None, "pcol", "prow"), P(None, "pcol", None))
    out_specs = P("pcol", "prow")
    return jax.shard_map(functools.partial(body, dict(mesh.shape)), mesh=mesh, in_specs=in_specs, out_specs=out_specs, check_vma=False)
```

```python
import functools

import jax
import jax.numpy as jnp
from jax import lax
from jax.experimental import pallas as pl
from jax.experimental.pallas import tpu as pltpu
from jax.sharding import PartitionSpec as P


UNIT_LIMIT = 2048
TILE_LIMIT = 8192
VMEM_LIMIT = 32 * 1024 * 1024
SMALL_LIMIT = 8 * 1024 * 1024
COST = pl.CostEstimate(flops=1, bytes_accessed=1, transcendentals=0)
PANELS = 2
ROWS = (((1,), (1,)), ((), ()))
PLAIN = (((1,), (0,)), ((), ()))


def divisor(width, limit):
    for unit in (128, 1):
        fits = [t for t in range(unit, min(limit, width) + 1, unit) if width % t == 0]
        if fits:
            return max(fits)
    return width


def split(value):
    high = value.astype(jnp.bfloat16)
    return high, (value - high.astype(jnp.float32)).astype(jnp.bfloat16)


def dot(left, right, dims):
    return lax.dot_general(left, right, dims, preferred_element_type=jnp.float32)


def exact(left, right, dims):
    return lax.dot_general(left, right, dims, precision=lax.Precision.HIGHEST, preferred_element_type=jnp.float32)


def column_tiles(width, limit):
    tile = divisor(width, limit)
    return [pl.ds(begin, tile) for begin in range(0, width, tile)]


def panel_rows(refs, panel, columns):
    return jnp.concatenate([ref[panel, :, columns] for ref in refs], axis=0)


def near_kernel(kept, slab_ref, *refs):
    vector_refs, out_ref, kept_refs = refs[: -1 - kept], refs[-1 - kept], refs[len(refs) - kept :]
    for ref, kept_ref in zip(vector_refs[1:], kept_refs):
        kept_ref[...] = ref[...]
    (rows, width), nb = slab_ref.shape, out_ref.shape[1]
    group = nb // 4
    total = 0
    for columns in column_tiles(width, TILE_LIMIT):
        (fh, fl), (sh, sl) = (split(panel_rows(vector_refs, p, columns)) for p in range(PANELS))
        ch, cl = split(slab_ref[:, columns])
        first = dot(jnp.concatenate([ch, cl], axis=0), fh, ROWS)
        first = first[:rows] + first[rows:] + dot(ch, fl, ROWS)
        high = jnp.concatenate([ch, fh[: 2 * group]], axis=0)
        low = jnp.concatenate([cl, fl[: 2 * group]], axis=0)
        second = dot(jnp.concatenate([high, low], axis=0), sh, ROWS)
        second = second[: high.shape[0]] + second[high.shape[0] :] + dot(high, sl, ROWS)
        total += jnp.concatenate([first, second], axis=0)
    inner, own, via = total[: 2 * rows], total[2 * rows : 2 * rows + group], total[2 * rows + group :]
    inner = jnp.concatenate([inner, jnp.zeros((2 * rows, group), jnp.float32)], axis=1)
    share = jnp.concatenate([own, via[:, 2 * group :]], axis=1)
    out_ref[...] = jnp.concatenate([inner, share], axis=0)


def corner_kernel(slab_ref, *refs):
    vector_refs, out_ref = refs[:-1], refs[-1]
    (rows, width), (part, nb) = slab_ref.shape, out_ref.shape
    total = 0
    for columns in column_tiles(width, TILE_LIMIT):
        vh, vl = split(jnp.concatenate([ref[:, columns] for ref in vector_refs], axis=0))
        ch, cl = split(slab_ref[:, columns])
        found = dot(jnp.concatenate([ch, cl], axis=0), vh, ROWS)
        total += found[:rows] + found[rows:] + dot(ch, vl, ROWS)
    total = jnp.concatenate([total[:, : nb // 4], total[:, nb // 4 :]], axis=0)
    out_ref[...] = jnp.concatenate([total[k * part : (k + 1) * part] for k in range(4)], axis=1)


def turn_kernel(size, *refs):
    factor_refs, out_ref = refs[:-1], refs[-1]
    nb, low = out_ref.shape[1], size // 4
    block = nb // size
    me = lax.axis_index("pcol")
    column = lax.broadcasted_iota(jnp.int32, (nb, nb), 1)
    place = column // block
    role = place // low
    swapped = ((role == 1) | (role == 2)) & (opposite(size) * (me % 2) == 1)
    bits = jnp.where(swapped, 3 - role, role) * low + place % low
    order = lax.broadcasted_iota(jnp.int32, (nb, nb), 0) == (bits ^ me) * block + column % block
    rows = [ref[p] for p in range(PANELS) for ref in factor_refs]
    out_ref[...] = exact(jnp.concatenate(rows, axis=0), order.astype(jnp.float32), PLAIN)


def share_kernel(terms, *refs):
    term_refs, turned_ref, inner_ref, share_ref = refs[:terms], *refs[terms:]
    group = share_ref.shape[0] // (1 + PANELS)
    total = term_refs[0][...]
    for ref in term_refs[1:]:
        total += ref[...]
    inner_ref[...] = total[:-group]
    share_ref[:group] = total[-group:]
    share_ref[group:] = turned_ref[...]


def from_place(value, q, block, lane):
    width = value.shape[1]
    bit = 1
    while bit * block < width:
        if q & bit:
            shift = bit * block
            ahead, behind = pltpu.roll(value, width - shift, 1), pltpu.roll(value, shift, 1)
            value = jnp.where((lane // shift) % 2 == 0, ahead, behind)
        bit *= 2
    return value


def matrices_kernel(*refs):
    share_refs, between_ref, triangle_refs = refs[:4], refs[4], refs[5:]
    nb = between_ref.shape[0]
    group = nb // 4
    lane = lax.broadcasted_iota(jnp.int32, (1, nb), 1)
    triangles = [[] for _ in range(PANELS)]
    for side in range(4):
        held = from_place(share_refs[side][...], side, group, lane)
        other = from_place(share_refs[side ^ 1][:group], side, group, lane)
        far = ((lane // group) ^ side) == 3
        between_ref[side * group : (side + 1) * group] = jnp.where(far, other, held[:group])
        for p in range(PANELS):
            triangles[p].append(held[(1 + p) * group : (2 + p) * group])
    for p in range(PANELS):
        triangle_refs[p][...] = jnp.concatenate(triangles[p], axis=0).T


def update_kernel(pieces, terms, *refs):
    near_ref, term_refs, (between_ref, first_ref, second_ref) = refs[0], refs[1 : 1 + terms], refs[1 + terms : 4 + terms]
    slab_ref, *vector_refs = refs[4 + terms : -3]
    out_ref, after, sems = refs[-3:]
    (rows, width), nb = slab_ref.shape, near_ref.shape[1]
    group = nb // 4

    total = term_refs[0][...]
    for ref in term_refs[1:]:
        total += ref[...]
    total = jnp.concatenate([total[:, k * group : (k + 1) * group] for k in range(4)], axis=0)
    total = near_ref[...] + jnp.concatenate([jnp.zeros((PANELS * rows, nb - group), jnp.float32), total], axis=1)
    scaled = exact(total[:rows], first_ref[...], PLAIN)
    inner = total[rows:] - exact(scaled, between_ref[...], PLAIN)
    later = exact(inner, second_ref[...], PLAIN)
    both = jnp.concatenate(split(jnp.concatenate([scaled, later], axis=1)), axis=0)

    copies = []
    for at, columns in enumerate(column_tiles(width, UNIT_LIMIT)):
        blocks = [vector_refs[ref][:, columns] if p is None else vector_refs[ref][p, :, columns] for ref, p in pieces]
        high, low = split(jnp.concatenate(blocks, axis=0))
        main = dot(both, high, PLAIN)
        rest = dot(both[:rows], low, PLAIN)
        after[:, columns] = slab_ref[:, columns] - (main[:rows] + main[rows:] + rest)
        copies.append(pltpu.make_async_copy(after.at[:, columns], out_ref.at[:, columns], sems.at[at]))
        copies[-1].start()
    for copy in copies:
        copy.wait()


def products(kernel, arrays, *shapes):
    return pl.pallas_call(
        kernel,
        in_specs=[pl.BlockSpec(memory_space=pltpu.VMEM)] * len(arrays),
        out_specs=[pl.BlockSpec(memory_space=pltpu.VMEM)] * len(shapes),
        out_shape=[jax.ShapeDtypeStruct(shape, jnp.float32) for shape in shapes],
        compiler_params=pltpu.CompilerParams(vmem_limit_bytes=VMEM_LIMIT),
        cost_estimate=COST,
    )(*arrays)


def small(kernel, shapes, *arrays):
    return pl.pallas_call(
        kernel,
        out_shape=[jax.ShapeDtypeStruct(shape, jnp.float32) for shape in shapes],
        compiler_params=pltpu.CompilerParams(vmem_limit_bytes=SMALL_LIMIT),
        cost_estimate=COST,
    )(*arrays)


def update(near, terms, matrices, slab, arrays, pieces):
    width = slab.shape[1]
    whole = [near, *terms, *matrices, slab, *arrays]
    return pl.pallas_call(
        functools.partial(update_kernel, pieces, len(terms)),
        in_specs=[pl.BlockSpec(memory_space=pltpu.VMEM)] * len(whole),
        out_specs=pl.BlockSpec(memory_space=pl.ANY),
        out_shape=jax.ShapeDtypeStruct(slab.shape, jnp.float32),
        scratch_shapes=[
            pltpu.VMEM(slab.shape, jnp.float32),
            pltpu.SemaphoreType.DMA((len(column_tiles(width, UNIT_LIMIT)),)),
        ],
        compiler_params=pltpu.CompilerParams(vmem_limit_bytes=VMEM_LIMIT),
        cost_estimate=COST,
    )(*whole)


def opposite(size):
    return int(size > 4)


def exchange(array, partner, size, axis):
    return lax.ppermute(array, axis, [(i, i ^ partner(i)) for i in range(size)])


def summed_terms(value, depth, step):
    terms, reach = [value], 1
    while reach < depth:
        value = sum(terms[1:], terms[0])
        span = min(step, depth // reach)
        terms = [value] + [exchange(value, lambda i, k=k: k * reach, depth, "prow") for k in range(1, span)]
        reach *= span
    return terms


def over_rest(held, low, across):
    bit = 1
    while bit < low:
        for q, array in list(held.items()):
            turned = q // low in (1, 2) and bit == 1
            held[(q ^ (3 * low) if turned else q) | bit] = across(array, lambda i, bit=bit: bit)
        bit *= 2
    return held


def body(sizes, slab, reflectors, factors):
    size, depth = sizes["pcol"], sizes["prow"]
    rows = slab.shape[0]
    block, nb = factors.shape[1:]
    high, low = size // 2, size // 4
    across = functools.partial(exchange, size=size, axis="pcol")
    first = lambda i: high if opposite(size) * (i % 2) else low
    second = lambda i: low if opposite(size) * (i % 2) else high
    both = lambda i: high | low

    by_first, by_second = across(reflectors, first), across(reflectors, second)
    corner = [across(by_second[0], first), across(by_first[1], second)]
    near = over_rest({0: reflectors, low: by_first, high: by_second}, low, across)
    near = [near[q] for q in sorted(near)]
    group = over_rest({0: factors}, low, across)
    (turned,) = small(functools.partial(turn_kernel, size), [(PANELS * nb // 4, nb)], *[group[q] for q in sorted(group)])
    near, turned = lax.optimization_barrier((near, turned))
    (total,) = products(functools.partial(near_kernel, 0), [slab, *near], (2 * rows + nb // 4, nb))
    terms = summed_terms(total, depth, 4)
    terms, corner = lax.optimization_barrier((terms, corner))
    inner, share = small(
        functools.partial(share_kernel, len(terms)), [(2 * rows, nb), ((1 + PANELS) * nb // 4, nb)], *terms, turned
    )
    shares = [share, *(across(share, way) for way in (first, second, both))]
    far = [over_rest({high | low: array}, low, across) for array in corner]
    far = [held[q] for held in far for q in sorted(held)]
    matrices = small(matrices_kernel, [(nb, nb)] * (1 + PANELS), *shares)
    (found,) = products(corner_kernel, [slab, *far], (2 * rows // 4, nb))
    count, part = len(near), len(far) // PANELS
    pieces = [piece for p in range(PANELS) for piece in (*((at, p) for at in range(count)), *((count + p * part + at, None) for at in range(part)))]
    return update(inner, summed_terms(found, depth, 4), matrices, slab, [*near, *far], pieces)


def solution(mesh):
    in_specs = (P("pcol", "prow"), P(None, "pcol", "prow"), P(None, "pcol", None))
    out_specs = P("pcol", "prow")
    return jax.shard_map(functools.partial(body, dict(mesh.shape)), mesh=mesh, in_specs=in_specs, out_specs=out_specs, check_vma=False)
```

```python
import functools

import jax
import jax.numpy as jnp
from jax import lax
from jax.experimental import pallas as pl
from jax.experimental.pallas import tpu as pltpu
from jax.sharding import PartitionSpec as P


UNIT_LIMIT = 2048
TILE_LIMIT = 8192
VMEM_LIMIT = 32 * 1024 * 1024
SMALL_LIMIT = 8 * 1024 * 1024
COST = pl.CostEstimate(flops=1, bytes_accessed=1, transcendentals=0)
PANELS = 2
ROWS = (((1,), (1,)), ((), ()))
PLAIN = (((1,), (0,)), ((), ()))


def divisor(width, limit):
    for unit in (128, 1):
        fits = [t for t in range(unit, min(limit, width) + 1, unit) if width % t == 0]
        if fits:
            return max(fits)
    return width


def split(value):
    high = value.astype(jnp.bfloat16)
    return high, (value - high.astype(jnp.float32)).astype(jnp.bfloat16)


def dot(left, right, dims):
    return lax.dot_general(left, right, dims, preferred_element_type=jnp.float32)


def exact(left, right, dims):
    return lax.dot_general(left, right, dims, precision=lax.Precision.HIGHEST, preferred_element_type=jnp.float32)


def column_tiles(width, limit):
    tile = divisor(width, limit)
    return [pl.ds(begin, tile) for begin in range(0, width, tile)]


def panel_rows(refs, panel, columns):
    return jnp.concatenate([ref[panel, :, columns] for ref in refs], axis=0)


def near_kernel(kept, slab_ref, *refs):
    vector_refs, out_ref, kept_refs = refs[: -1 - kept], refs[-1 - kept], refs[len(refs) - kept :]
    for ref, kept_ref in zip(vector_refs[1:], kept_refs):
        kept_ref[...] = ref[...]
    (rows, width), nb = slab_ref.shape, out_ref.shape[1]
    group = nb // 4
    total = 0
    for columns in column_tiles(width, TILE_LIMIT):
        (fh, fl), (sh, sl) = (split(panel_rows(vector_refs, p, columns)) for p in range(PANELS))
        ch, cl = split(slab_ref[:, columns])
        first = dot(jnp.concatenate([ch, cl], axis=0), fh, ROWS)
        first = first[:rows] + first[rows:] + dot(ch, fl, ROWS)
        high = jnp.concatenate([ch, fh[: 2 * group]], axis=0)
        low = jnp.concatenate([cl, fl[: 2 * group]], axis=0)
        second = dot(jnp.concatenate([high, low], axis=0), sh, ROWS)
        second = second[: high.shape[0]] + second[high.shape[0] :] + dot(high, sl, ROWS)
        total += jnp.concatenate([first, second], axis=0)
    inner, own, via = total[: 2 * rows], total[2 * rows : 2 * rows + group], total[2 * rows + group :]
    inner = jnp.concatenate([inner, jnp.zeros((2 * rows, group), jnp.float32)], axis=1)
    share = jnp.concatenate([own, via[:, 2 * group :]], axis=1)
    out_ref[...] = jnp.concatenate([inner, share], axis=0)


def with_slab(slab_ref, vector_refs):
    total = 0
    for columns in column_tiles(slab_ref.shape[1], TILE_LIMIT):
        vh, vl = split(jnp.concatenate([ref[:, columns] for ref in vector_refs], axis=0))
        ch, cl = split(slab_ref[:, columns])
        found = dot(jnp.concatenate([ch, cl], axis=0), vh, ROWS)
        total += found[: ch.shape[0]] + found[ch.shape[0] :] + dot(ch, vl, ROWS)
    return total


def corner_kernel(slab_ref, *refs):
    refs[-1][...] = with_slab(slab_ref, refs[:-1])


def corner_rest_kernel(own_ref, slab_ref, *refs):
    vector_refs, out_ref = refs[:-1], refs[-1]
    part = out_ref.shape[0]
    own, total = own_ref[...], own_ref[...]
    if vector_refs:
        rest = with_slab(slab_ref, vector_refs)
        width, rest_width = own.shape[1] // PANELS, rest.shape[1] // PANELS
        total = [value for p in range(PANELS) for value in (own[:, p * width : (p + 1) * width], rest[:, p * rest_width : (p + 1) * rest_width])]
        total = jnp.concatenate(total, axis=1)
    half = total.shape[1] // PANELS
    total = jnp.concatenate([total[:, p * half : (p + 1) * half] for p in range(PANELS)], axis=0)
    out_ref[...] = jnp.concatenate([total[k * part : (k + 1) * part] for k in range(4)], axis=1)


def turn_kernel(size, *refs):
    factor_refs, out_ref = refs[:-1], refs[-1]
    nb, low = out_ref.shape[1], size // 4
    block = nb // size
    me = lax.axis_index("pcol")
    column = lax.broadcasted_iota(jnp.int32, (nb, nb), 1)
    place = column // block
    role = place // low
    swapped = ((role == 1) | (role == 2)) & (opposite(size) * (me % 2) == 1)
    bits = jnp.where(swapped, 3 - role, role) * low + place % low
    order = lax.broadcasted_iota(jnp.int32, (nb, nb), 0) == (bits ^ me) * block + column % block
    rows = [ref[p] for p in range(PANELS) for ref in factor_refs]
    out_ref[...] = exact(jnp.concatenate(rows, axis=0), order.astype(jnp.float32), PLAIN)


def share_kernel(terms, *refs):
    term_refs, turned_ref, inner_ref, share_ref = refs[:terms], *refs[terms:]
    group = share_ref.shape[0] // (1 + PANELS)
    total = term_refs[0][...]
    for ref in term_refs[1:]:
        total += ref[...]
    inner_ref[...] = total[:-group]
    share_ref[:group] = total[-group:]
    share_ref[group:] = turned_ref[...]


def from_place(value, q, block, lane):
    width = value.shape[1]
    bit = 1
    while bit * block < width:
        if q & bit:
            shift = bit * block
            ahead, behind = pltpu.roll(value, width - shift, 1), pltpu.roll(value, shift, 1)
            value = jnp.where((lane // shift) % 2 == 0, ahead, behind)
        bit *= 2
    return value


def matrices_kernel(*refs):
    share_refs, between_ref, triangle_refs = refs[:4], refs[4], refs[5:]
    nb = between_ref.shape[0]
    group = nb // 4
    lane = lax.broadcasted_iota(jnp.int32, (1, nb), 1)
    triangles = [[] for _ in range(PANELS)]
    for side in range(4):
        held = from_place(share_refs[side][...], side, group, lane)
        other = from_place(share_refs[side ^ 1][:group], side, group, lane)
        far = ((lane // group) ^ side) == 3
        between_ref[side * group : (side + 1) * group] = jnp.where(far, other, held[:group])
        for p in range(PANELS):
            triangles[p].append(held[(1 + p) * group : (2 + p) * group])
    for p in range(PANELS):
        triangle_refs[p][...] = jnp.concatenate(triangles[p], axis=0).T


def update_kernel(pieces, terms, *refs):
    near_ref, term_refs, (between_ref, first_ref, second_ref) = refs[0], refs[1 : 1 + terms], refs[1 + terms : 4 + terms]
    slab_ref, *vector_refs = refs[4 + terms : -3]
    out_ref, after, sems = refs[-3:]
    (rows, width), nb = slab_ref.shape, near_ref.shape[1]
    group = nb // 4

    total = term_refs[0][...]
    for ref in term_refs[1:]:
        total += ref[...]
    total = jnp.concatenate([total[:, k * group : (k + 1) * group] for k in range(4)], axis=0)
    total = near_ref[...] + jnp.concatenate([jnp.zeros((PANELS * rows, nb - group), jnp.float32), total], axis=1)
    scaled = exact(total[:rows], first_ref[...], PLAIN)
    inner = total[rows:] - exact(scaled, between_ref[...], PLAIN)
    later = exact(inner, second_ref[...], PLAIN)
    both = jnp.concatenate(split(jnp.concatenate([scaled, later], axis=1)), axis=0)

    copies = []
    for at, columns in enumerate(column_tiles(width, UNIT_LIMIT)):
        blocks = [vector_refs[ref][:, columns] if p is None else vector_refs[ref][p, :, columns] for ref, p in pieces]
        high, low = split(jnp.concatenate(blocks, axis=0))
        main = dot(both, high, PLAIN)
        rest = dot(both[:rows], low, PLAIN)
        after[:, columns] = slab_ref[:, columns] - (main[:rows] + main[rows:] + rest)
        copies.append(pltpu.make_async_copy(after.at[:, columns], out_ref.at[:, columns], sems.at[at]))
        copies[-1].start()
    for copy in copies:
        copy.wait()


def products(kernel, arrays, *shapes):
    return pl.pallas_call(
        kernel,
        in_specs=[pl.BlockSpec(memory_space=pltpu.VMEM)] * len(arrays),
        out_specs=[pl.BlockSpec(memory_space=pltpu.VMEM)] * len(shapes),
        out_shape=[jax.ShapeDtypeStruct(shape, jnp.float32) for shape in shapes],
        compiler_params=pltpu.CompilerParams(vmem_limit_bytes=VMEM_LIMIT),
        cost_estimate=COST,
    )(*arrays)


def small(kernel, shapes, *arrays):
    return pl.pallas_call(
        kernel,
        out_shape=[jax.ShapeDtypeStruct(shape, jnp.float32) for shape in shapes],
        compiler_params=pltpu.CompilerParams(vmem_limit_bytes=SMALL_LIMIT),
        cost_estimate=COST,
    )(*arrays)


def update(near, terms, matrices, slab, arrays, pieces):
    width = slab.shape[1]
    whole = [near, *terms, *matrices, slab, *arrays]
    return pl.pallas_call(
        functools.partial(update_kernel, pieces, len(terms)),
        in_specs=[pl.BlockSpec(memory_space=pltpu.VMEM)] * len(whole),
        out_specs=pl.BlockSpec(memory_space=pl.ANY),
        out_shape=jax.ShapeDtypeStruct(slab.shape, jnp.float32),
        scratch_shapes=[
            pltpu.VMEM(slab.shape, jnp.float32),
            pltpu.SemaphoreType.DMA((len(column_tiles(width, UNIT_LIMIT)),)),
        ],
        compiler_params=pltpu.CompilerParams(vmem_limit_bytes=VMEM_LIMIT),
        cost_estimate=COST,
    )(*whole)


def opposite(size):
    return int(size > 4)


def exchange(array, partner, size, axis):
    return lax.ppermute(array, axis, [(i, i ^ partner(i)) for i in range(size)])


def summed_terms(value, depth, step):
    terms, reach = [value], 1
    while reach < depth:
        value = sum(terms[1:], terms[0])
        span = min(step, depth // reach)
        terms = [value] + [exchange(value, lambda i, k=k: k * reach, depth, "prow") for k in range(1, span)]
        reach *= span
    return terms


def over_rest(held, low, across):
    bit = 1
    while bit < low:
        for q, array in list(held.items()):
            turned = q // low in (1, 2) and bit == 1
            held[(q ^ (3 * low) if turned else q) | bit] = across(array, lambda i, bit=bit: bit)
        bit *= 2
    return held


def body(sizes, slab, reflectors, factors):
    size, depth = sizes["pcol"], sizes["prow"]
    rows = slab.shape[0]
    block, nb = factors.shape[1:]
    high, low = size // 2, size // 4
    across = functools.partial(exchange, size=size, axis="pcol")
    first = lambda i: high if opposite(size) * (i % 2) else low
    second = lambda i: low if opposite(size) * (i % 2) else high
    both = lambda i: high | low

    by_first, by_second = across(reflectors, first), across(reflectors, second)
    corner = [across(by_second[0], first), across(by_first[1], second)]
    by_first, by_second = lax.optimization_barrier((by_first, by_second))
    near = over_rest({0: reflectors, low: by_first, high: by_second}, low, across)
    near = [near[q] for q in sorted(near)]
    group = over_rest({0: factors}, low, across)
    (turned,) = small(functools.partial(turn_kernel, size), [(PANELS * nb // 4, nb)], *[group[q] for q in sorted(group)])
    near, turned = lax.optimization_barrier((near, turned))
    (total,) = products(functools.partial(near_kernel, 0), [slab, *near], (2 * rows + nb // 4, nb))
    terms = summed_terms(total, depth, 4)
    inner, share = small(
        functools.partial(share_kernel, len(terms)), [(2 * rows, nb), ((1 + PANELS) * nb // 4, nb)], *terms, turned
    )
    shares = [share, *(across(share, way) for way in (first, second, both))]
    shares, corner = lax.optimization_barrier((shares, corner))
    far = [over_rest({high | low: array}, low, across) for array in corner]
    mates = [held[q] for held in far for q in sorted(held)[1:]]
    far = [held[q] for held in far for q in sorted(held)]
    matrices = small(matrices_kernel, [(nb, nb)] * (1 + PANELS), *shares)
    (own,) = products(corner_kernel, [slab, *corner], (rows, PANELS * block))
    (found,) = products(corner_rest_kernel, [own, slab, *mates], (2 * rows // 4, nb))
    count, part = len(near), len(far) // PANELS
    pieces = [piece for p in range(PANELS) for piece in (*((at, p) for at in range(count)), *((count + p * part + at, None) for at in range(part)))]
    return update(inner, summed_terms(found, depth, 4), matrices, slab, [*near, *far], pieces)


def solution(mesh):
    in_specs = (P("pcol", "prow"), P(None, "pcol", "prow"), P(None, "pcol", None))
    out_specs = P("pcol", "prow")
    return jax.shard_map(functools.partial(body, dict(mesh.shape)), mesh=mesh, in_specs=in_specs, out_specs=out_specs, check_vma=False)
```

```python
import functools

import jax
import jax.numpy as jnp
from jax import lax
from jax.experimental import pallas as pl
from jax.experimental.pallas import tpu as pltpu
from jax.sharding import PartitionSpec as P


UNIT_LIMIT = 2048
TILE_LIMIT = 8192
VMEM_LIMIT = 32 * 1024 * 1024
SMALL_LIMIT = 8 * 1024 * 1024
COST = pl.CostEstimate(flops=1, bytes_accessed=1, transcendentals=0)
PANELS = 2
ROWS = (((1,), (1,)), ((), ()))
PLAIN = (((1,), (0,)), ((), ()))


def divisor(width, limit):
    for unit in (128, 1):
        fits = [t for t in range(unit, min(limit, width) + 1, unit) if width % t == 0]
        if fits:
            return max(fits)
    return width


def split(value):
    high = value.astype(jnp.bfloat16)
    return high, (value - high.astype(jnp.float32)).astype(jnp.bfloat16)


def dot(left, right, dims):
    return lax.dot_general(left, right, dims, preferred_element_type=jnp.float32)


def exact(left, right, dims):
    return lax.dot_general(left, right, dims, precision=lax.Precision.HIGHEST, preferred_element_type=jnp.float32)


def column_tiles(width, limit):
    tile = divisor(width, limit)
    return [pl.ds(begin, tile) for begin in range(0, width, tile)]


def panel_rows(refs, panel, columns):
    return jnp.concatenate([ref[panel, :, columns] for ref in refs], axis=0)


def near_kernel(kept, slab_ref, *refs):
    vector_refs, out_ref, kept_refs = refs[: -1 - kept], refs[-1 - kept], refs[len(refs) - kept :]
    for ref, kept_ref in zip(vector_refs[1:], kept_refs):
        kept_ref[...] = ref[...]
    (rows, width), nb = slab_ref.shape, out_ref.shape[1]
    group = nb // 4
    total = 0
    for columns in column_tiles(width, TILE_LIMIT):
        (fh, fl), (sh, sl) = (split(panel_rows(vector_refs, p, columns)) for p in range(PANELS))
        ch, cl = split(slab_ref[:, columns])
        first = dot(jnp.concatenate([ch, cl], axis=0), fh, ROWS)
        first = first[:rows] + first[rows:] + dot(ch, fl, ROWS)
        high = jnp.concatenate([ch, fh[: 2 * group]], axis=0)
        low = jnp.concatenate([cl, fl[: 2 * group]], axis=0)
        second = dot(jnp.concatenate([high, low], axis=0), sh, ROWS)
        second = second[: high.shape[0]] + second[high.shape[0] :] + dot(high, sl, ROWS)
        total += jnp.concatenate([first, second], axis=0)
    inner, own, via = total[: 2 * rows], total[2 * rows : 2 * rows + group], total[2 * rows + group :]
    inner = jnp.concatenate([inner, jnp.zeros((2 * rows, group), jnp.float32)], axis=1)
    share = jnp.concatenate([own, via[:, 2 * group :]], axis=1)
    out_ref[...] = jnp.concatenate([inner, share], axis=0)


def corner_kernel(slab_ref, *refs):
    vector_refs, out_ref = refs[:-1], refs[-1]
    (rows, width), (part, nb) = slab_ref.shape, out_ref.shape
    total = 0
    for columns in column_tiles(width, TILE_LIMIT):
        vh, vl = split(jnp.concatenate([ref[:, columns] for ref in vector_refs], axis=0))
        ch, cl = split(slab_ref[:, columns])
        found = dot(jnp.concatenate([ch, cl], axis=0), vh, ROWS)
        total += found[:rows] + found[rows:] + dot(ch, vl, ROWS)
    total = jnp.concatenate([total[:, : nb // 4], total[:, nb // 4 :]], axis=0)
    out_ref[...] = jnp.concatenate([total[k * part : (k + 1) * part] for k in range(4)], axis=1)


def turn_kernel(size, *refs):
    factor_refs, out_ref = refs[:-1], refs[-1]
    nb, low = out_ref.shape[1], size // 4
    block = nb // size
    me = lax.axis_index("pcol")
    column = lax.broadcasted_iota(jnp.int32, (nb, nb), 1)
    place = column // block
    role = place // low
    swapped = ((role == 1) | (role == 2)) & (opposite(size) * (me % 2) == 1)
    bits = jnp.where(swapped, 3 - role, role) * low + place % low
    order = lax.broadcasted_iota(jnp.int32, (nb, nb), 0) == (bits ^ me) * block + column % block
    rows = [ref[p] for p in range(PANELS) for ref in factor_refs]
    out_ref[...] = exact(jnp.concatenate(rows, axis=0), order.astype(jnp.float32), PLAIN)


def share_kernel(terms, *refs):
    term_refs, turned_ref, inner_ref, share_ref = refs[:terms], *refs[terms:]
    group = share_ref.shape[0] // (1 + PANELS)
    total = term_refs[0][...]
    for ref in term_refs[1:]:
        total += ref[...]
    inner_ref[...] = total[:-group]
    share_ref[:group] = total[-group:]
    share_ref[group:] = turned_ref[...]


def from_place(value, q, block, lane):
    width = value.shape[1]
    bit = 1
    while bit * block < width:
        if q & bit:
            shift = bit * block
            ahead, behind = pltpu.roll(value, width - shift, 1), pltpu.roll(value, shift, 1)
            value = jnp.where((lane // shift) % 2 == 0, ahead, behind)
        bit *= 2
    return value


def matrices_kernel(*refs):
    share_refs, between_ref, triangle_refs = refs[:4], refs[4], refs[5:]
    nb = between_ref.shape[0]
    group = nb // 4
    lane = lax.broadcasted_iota(jnp.int32, (1, nb), 1)
    triangles = [[] for _ in range(PANELS)]
    for side in range(4):
        held = from_place(share_refs[side][...], side, group, lane)
        other = from_place(share_refs[side ^ 1][:group], side, group, lane)
        far = ((lane // group) ^ side) == 3
        between_ref[side * group : (side + 1) * group] = jnp.where(far, other, held[:group])
        for p in range(PANELS):
            triangles[p].append(held[(1 + p) * group : (2 + p) * group])
    for p in range(PANELS):
        triangle_refs[p][...] = jnp.concatenate(triangles[p], axis=0).T


def update_kernel(pieces, terms, *refs):
    near_ref, term_refs, (between_ref, first_ref, second_ref) = refs[0], refs[1 : 1 + terms], refs[1 + terms : 4 + terms]
    slab_ref, *vector_refs = refs[4 + terms : -3]
    out_ref, after, sems = refs[-3:]
    (rows, width), nb = slab_ref.shape, near_ref.shape[1]
    group = nb // 4

    total = term_refs[0][...]
    for ref in term_refs[1:]:
        total += ref[...]
    total = jnp.concatenate([total[:, k * group : (k + 1) * group] for k in range(4)], axis=0)
    total = near_ref[...] + jnp.concatenate([jnp.zeros((PANELS * rows, nb - group), jnp.float32), total], axis=1)
    scaled = exact(total[:rows], first_ref[...], PLAIN)
    inner = total[rows:] - exact(scaled, between_ref[...], PLAIN)
    later = exact(inner, second_ref[...], PLAIN)
    both = jnp.concatenate(split(jnp.concatenate([scaled, later], axis=1)), axis=0)

    copies = []
    for at, columns in enumerate(column_tiles(width, UNIT_LIMIT)):
        blocks = [vector_refs[ref][:, columns] if p is None else vector_refs[ref][p, :, columns] for ref, p in pieces]
        high, low = split(jnp.concatenate(blocks, axis=0))
        main = dot(both, high, PLAIN)
        rest = dot(both[:rows], low, PLAIN)
        after[:, columns] = slab_ref[:, columns] - (main[:rows] + main[rows:] + rest)
        copies.append(pltpu.make_async_copy(after.at[:, columns], out_ref.at[:, columns], sems.at[at]))
        copies[-1].start()
    for copy in copies:
        copy.wait()


def products(kernel, arrays, *shapes):
    return pl.pallas_call(
        kernel,
        in_specs=[pl.BlockSpec(memory_space=pltpu.VMEM)] * len(arrays),
        out_specs=[pl.BlockSpec(memory_space=pltpu.VMEM)] * len(shapes),
        out_shape=[jax.ShapeDtypeStruct(shape, jnp.float32) for shape in shapes],
        compiler_params=pltpu.CompilerParams(vmem_limit_bytes=VMEM_LIMIT),
        cost_estimate=COST,
    )(*arrays)


def small(kernel, shapes, *arrays):
    return pl.pallas_call(
        kernel,
        out_shape=[jax.ShapeDtypeStruct(shape, jnp.float32) for shape in shapes],
        compiler_params=pltpu.CompilerParams(vmem_limit_bytes=SMALL_LIMIT),
        cost_estimate=COST,
    )(*arrays)


def update(near, terms, matrices, slab, arrays, pieces):
    width = slab.shape[1]
    whole = [near, *terms, *matrices, slab, *arrays]
    return pl.pallas_call(
        functools.partial(update_kernel, pieces, len(terms)),
        in_specs=[pl.BlockSpec(memory_space=pltpu.VMEM)] * len(whole),
        out_specs=pl.BlockSpec(memory_space=pl.ANY),
        out_shape=jax.ShapeDtypeStruct(slab.shape, jnp.float32),
        scratch_shapes=[
            pltpu.VMEM(slab.shape, jnp.float32),
            pltpu.SemaphoreType.DMA((len(column_tiles(width, UNIT_LIMIT)),)),
        ],
        compiler_params=pltpu.CompilerParams(vmem_limit_bytes=VMEM_LIMIT),
        cost_estimate=COST,
    )(*whole)


def opposite(size):
    return int(size > 4)


def exchange(array, partner, size, axis):
    return lax.ppermute(array, axis, [(i, i ^ partner(i)) for i in range(size)])


def summed_terms(value, depth, step):
    terms, reach = [value], 1
    while reach < depth:
        value = sum(terms[1:], terms[0])
        span = min(step, depth // reach)
        terms = [value] + [exchange(value, lambda i, k=k: k * reach, depth, "prow") for k in range(1, span)]
        reach *= span
    return terms


def over_rest(held, low, across):
    bit = 1
    while bit < low:
        for q, array in list(held.items()):
            turned = q // low in (1, 2) and bit == 1
            held[(q ^ (3 * low) if turned else q) | bit] = across(array, lambda i, bit=bit: bit)
        bit *= 2
    return held


def body(sizes, slab, reflectors, factors):
    size, depth = sizes["pcol"], sizes["prow"]
    rows = slab.shape[0]
    block, nb = factors.shape[1:]
    high, low = size // 2, size // 4
    across = functools.partial(exchange, size=size, axis="pcol")
    first = lambda i: high if opposite(size) * (i % 2) else low
    second = lambda i: low if opposite(size) * (i % 2) else high
    both = lambda i: high | low

    by_first, by_second = across(reflectors, first), across(reflectors, second)
    corner = [across(by_second[0], first), across(by_first[1], second)]
    group = over_rest({0: factors}, low, across)
    mine, group = lax.optimization_barrier((reflectors, group))
    near = over_rest({0: mine, low: by_first, high: by_second}, low, across)
    near = [near[q] for q in sorted(near)]
    (turned,) = small(functools.partial(turn_kernel, size), [(PANELS * nb // 4, nb)], *[group[q] for q in sorted(group)])
    near, turned = lax.optimization_barrier((near, turned))
    (total,) = products(functools.partial(near_kernel, 0), [slab, *near], (2 * rows + nb // 4, nb))
    terms = summed_terms(total, depth, 4)
    terms, corner = lax.optimization_barrier((terms, corner))
    inner, share = small(
        functools.partial(share_kernel, len(terms)), [(2 * rows, nb), ((1 + PANELS) * nb // 4, nb)], *terms, turned
    )
    shares = [share, *(across(share, way) for way in (first, second, both))]
    far = [over_rest({high | low: array}, low, across) for array in corner]
    far = [held[q] for held in far for q in sorted(held)]
    matrices = small(matrices_kernel, [(nb, nb)] * (1 + PANELS), *shares)
    (found,) = products(corner_kernel, [slab, *far], (2 * rows // 4, nb))
    count, part = len(near), len(far) // PANELS
    pieces = [piece for p in range(PANELS) for piece in (*((at, p) for at in range(count)), *((count + p * part + at, None) for at in range(part)))]
    return update(inner, summed_terms(found, depth, 4), matrices, slab, [*near, *far], pieces)


def solution(mesh):
    in_specs = (P("pcol", "prow"), P(None, "pcol", "prow"), P(None, "pcol", None))
    out_specs = P("pcol", "prow")
    return jax.shard_map(functools.partial(body, dict(mesh.shape)), mesh=mesh, in_specs=in_specs, out_specs=out_specs, check_vma=False)
```

```python
import functools

import jax
import jax.numpy as jnp
from jax import lax
from jax.experimental import pallas as pl
from jax.experimental.pallas import tpu as pltpu
from jax.sharding import PartitionSpec as P


UNIT_LIMIT = 2048
TILE_LIMIT = 8192
VMEM_LIMIT = 32 * 1024 * 1024
SMALL_LIMIT = 8 * 1024 * 1024
COST = pl.CostEstimate(flops=1, bytes_accessed=1, transcendentals=0)
PANELS = 2
ROWS = (((1,), (1,)), ((), ()))
PLAIN = (((1,), (0,)), ((), ()))


def divisor(width, limit):
    for unit in (128, 1):
        fits = [t for t in range(unit, min(limit, width) + 1, unit) if width % t == 0]
        if fits:
            return max(fits)
    return width


def split(value):
    high = value.astype(jnp.bfloat16)
    return high, (value - high.astype(jnp.float32)).astype(jnp.bfloat16)


def dot(left, right, dims):
    return lax.dot_general(left, right, dims, preferred_element_type=jnp.float32)


def exact(left, right, dims):
    return lax.dot_general(left, right, dims, precision=lax.Precision.HIGHEST, preferred_element_type=jnp.float32)


def column_tiles(width, limit):
    tile = divisor(width, limit)
    return [pl.ds(begin, tile) for begin in range(0, width, tile)]


def panel_rows(refs, panel, columns):
    return jnp.concatenate([ref[panel, :, columns] for ref in refs], axis=0)


def near_kernel(kept, slab_ref, *refs):
    vector_refs, out_ref, kept_refs = refs[: -1 - kept], refs[-1 - kept], refs[len(refs) - kept :]
    for ref, kept_ref in zip(vector_refs[1:], kept_refs):
        kept_ref[...] = ref[...]
    (rows, width), nb = slab_ref.shape, out_ref.shape[1]
    group = nb // 4
    total = 0
    for columns in column_tiles(width, TILE_LIMIT):
        (fh, fl), (sh, sl) = (split(panel_rows(vector_refs, p, columns)) for p in range(PANELS))
        ch, cl = split(slab_ref[:, columns])
        first = dot(jnp.concatenate([ch, cl], axis=0), fh, ROWS)
        first = first[:rows] + first[rows:] + dot(ch, fl, ROWS)
        high = jnp.concatenate([ch, fh[: 2 * group]], axis=0)
        low = jnp.concatenate([cl, fl[: 2 * group]], axis=0)
        second = dot(jnp.concatenate([high, low], axis=0), sh, ROWS)
        second = second[: high.shape[0]] + second[high.shape[0] :] + dot(high, sl, ROWS)
        total += jnp.concatenate([first, second], axis=0)
    inner, own, via = total[: 2 * rows], total[2 * rows : 2 * rows + group], total[2 * rows + group :]
    inner = jnp.concatenate([inner, jnp.zeros((2 * rows, group), jnp.float32)], axis=1)
    share = jnp.concatenate([own, via[:, 2 * group :]], axis=1)
    out_ref[...] = jnp.concatenate([inner, share], axis=0)


def corner_kernel(slab_ref, *refs):
    vector_refs, out_ref = refs[:-1], refs[-1]
    (rows, width), (part, nb) = slab_ref.shape, out_ref.shape
    total = 0
    for columns in column_tiles(width, TILE_LIMIT):
        vh, vl = split(jnp.concatenate([ref[:, columns] for ref in vector_refs], axis=0))
        ch, cl = split(slab_ref[:, columns])
        found = dot(jnp.concatenate([ch, cl], axis=0), vh, ROWS)
        total += found[:rows] + found[rows:] + dot(ch, vl, ROWS)
    total = jnp.concatenate([total[:, : nb // 4], total[:, nb // 4 :]], axis=0)
    out_ref[...] = jnp.concatenate([total[k * part : (k + 1) * part] for k in range(4)], axis=1)


def turn_kernel(size, *refs):
    factor_refs, out_ref = refs[:-1], refs[-1]
    nb, low = out_ref.shape[1], size // 4
    block = nb // size
    me = lax.axis_index("pcol")
    column = lax.broadcasted_iota(jnp.int32, (nb, nb), 1)
    place = column // block
    role = place // low
    swapped = ((role == 1) | (role == 2)) & (opposite(size) * (me % 2) == 1)
    bits = jnp.where(swapped, 3 - role, role) * low + place % low
    order = lax.broadcasted_iota(jnp.int32, (nb, nb), 0) == (bits ^ me) * block + column % block
    rows = [ref[p] for p in range(PANELS) for ref in factor_refs]
    out_ref[...] = exact(jnp.concatenate(rows, axis=0), order.astype(jnp.float32), PLAIN)


def share_kernel(terms, *refs):
    term_refs, turned_ref, inner_ref, share_ref = refs[:terms], *refs[terms:]
    group = share_ref.shape[0] // (1 + PANELS)
    total = term_refs[0][...]
    for ref in term_refs[1:]:
        total += ref[...]
    inner_ref[...] = total[:-group]
    share_ref[:group] = total[-group:]
    share_ref[group:] = turned_ref[...]


def from_place(value, q, block, lane):
    width = value.shape[1]
    bit = 1
    while bit * block < width:
        if q & bit:
            shift = bit * block
            ahead, behind = pltpu.roll(value, width - shift, 1), pltpu.roll(value, shift, 1)
            value = jnp.where((lane // shift) % 2 == 0, ahead, behind)
        bit *= 2
    return value


def matrices_kernel(*refs):
    share_refs, between_ref, triangle_refs = refs[:4], refs[4], refs[5:]
    nb = between_ref.shape[0]
    group = nb // 4
    lane = lax.broadcasted_iota(jnp.int32, (1, nb), 1)
    triangles = [[] for _ in range(PANELS)]
    for side in range(4):
        held = from_place(share_refs[side][...], side, group, lane)
        other = from_place(share_refs[side ^ 1][:group], side, group, lane)
        far = ((lane // group) ^ side) == 3
        between_ref[side * group : (side + 1) * group] = jnp.where(far, other, held[:group])
        for p in range(PANELS):
            triangles[p].append(held[(1 + p) * group : (2 + p) * group])
    for p in range(PANELS):
        triangle_refs[p][...] = jnp.concatenate(triangles[p], axis=0).T


def update_kernel(pieces, terms, *refs):
    near_ref, term_refs, (between_ref, first_ref, second_ref) = refs[0], refs[1 : 1 + terms], refs[1 + terms : 4 + terms]
    slab_ref, *vector_refs = refs[4 + terms : -3]
    out_ref, after, sems = refs[-3:]
    (rows, width), nb = slab_ref.shape, near_ref.shape[1]
    group = nb // 4

    total = jnp.sum(term_refs[0][...], axis=0)
    total = jnp.concatenate([total[:, k * group : (k + 1) * group] for k in range(4)], axis=0)
    total = near_ref[...] + jnp.concatenate([jnp.zeros((PANELS * rows, nb - group), jnp.float32), total], axis=1)
    scaled = exact(total[:rows], first_ref[...], PLAIN)
    inner = total[rows:] - exact(scaled, between_ref[...], PLAIN)
    later = exact(inner, second_ref[...], PLAIN)
    both = jnp.concatenate(split(jnp.concatenate([scaled, later], axis=1)), axis=0)

    copies = []
    for at, columns in enumerate(column_tiles(width, UNIT_LIMIT)):
        blocks = [vector_refs[ref][:, columns] if p is None else vector_refs[ref][p, :, columns] for ref, p in pieces]
        high, low = split(jnp.concatenate(blocks, axis=0))
        main = dot(both, high, PLAIN)
        rest = dot(both[:rows], low, PLAIN)
        after[:, columns] = slab_ref[:, columns] - (main[:rows] + main[rows:] + rest)
        copies.append(pltpu.make_async_copy(after.at[:, columns], out_ref.at[:, columns], sems.at[at]))
        copies[-1].start()
    for copy in copies:
        copy.wait()


def products(kernel, arrays, *shapes):
    return pl.pallas_call(
        kernel,
        in_specs=[pl.BlockSpec(memory_space=pltpu.VMEM)] * len(arrays),
        out_specs=[pl.BlockSpec(memory_space=pltpu.VMEM)] * len(shapes),
        out_shape=[jax.ShapeDtypeStruct(shape, jnp.float32) for shape in shapes],
        compiler_params=pltpu.CompilerParams(vmem_limit_bytes=VMEM_LIMIT),
        cost_estimate=COST,
    )(*arrays)


def small(kernel, shapes, *arrays):
    return pl.pallas_call(
        kernel,
        out_shape=[jax.ShapeDtypeStruct(shape, jnp.float32) for shape in shapes],
        compiler_params=pltpu.CompilerParams(vmem_limit_bytes=SMALL_LIMIT),
        cost_estimate=COST,
    )(*arrays)


def update(near, terms, matrices, slab, arrays, pieces):
    width = slab.shape[1]
    whole = [near, *terms, *matrices, slab, *arrays]
    return pl.pallas_call(
        functools.partial(update_kernel, pieces, len(terms)),
        in_specs=[pl.BlockSpec(memory_space=pltpu.VMEM)] * len(whole),
        out_specs=pl.BlockSpec(memory_space=pl.ANY),
        out_shape=jax.ShapeDtypeStruct(slab.shape, jnp.float32),
        scratch_shapes=[
            pltpu.VMEM(slab.shape, jnp.float32),
            pltpu.SemaphoreType.DMA((len(column_tiles(width, UNIT_LIMIT)),)),
        ],
        compiler_params=pltpu.CompilerParams(vmem_limit_bytes=VMEM_LIMIT),
        cost_estimate=COST,
    )(*whole)


def opposite(size):
    return int(size > 4)


def exchange(array, partner, size, axis):
    return lax.ppermute(array, axis, [(i, i ^ partner(i)) for i in range(size)])


def summed_terms(value, depth, step):
    terms, reach = [value], 1
    while reach < depth:
        value = sum(terms[1:], terms[0])
        span = min(step, depth // reach)
        terms = [value] + [exchange(value, lambda i, k=k: k * reach, depth, "prow") for k in range(1, span)]
        reach *= span
    return terms


def over_rest(held, low, across):
    bit = 1
    while bit < low:
        for q, array in list(held.items()):
            turned = q // low in (1, 2) and bit == 1
            held[(q ^ (3 * low) if turned else q) | bit] = across(array, lambda i, bit=bit: bit)
        bit *= 2
    return held


def body(sizes, slab, reflectors, factors):
    size, depth = sizes["pcol"], sizes["prow"]
    rows = slab.shape[0]
    block, nb = factors.shape[1:]
    high, low = size // 2, size // 4
    across = functools.partial(exchange, size=size, axis="pcol")
    first = lambda i: high if opposite(size) * (i % 2) else low
    second = lambda i: low if opposite(size) * (i % 2) else high
    both = lambda i: high | low

    by_first, by_second = across(reflectors, first), across(reflectors, second)
    corner = [across(by_second[0], first), across(by_first[1], second)]
    near = over_rest({0: reflectors, low: by_first, high: by_second}, low, across)
    near = [near[q] for q in sorted(near)]
    group = over_rest({0: factors}, low, across)
    (turned,) = small(functools.partial(turn_kernel, size), [(PANELS * nb // 4, nb)], *[group[q] for q in sorted(group)])
    near, turned = lax.optimization_barrier((near, turned))
    (total,) = products(functools.partial(near_kernel, 0), [slab, *near], (2 * rows + nb // 4, nb))
    terms = summed_terms(total, depth, 4)
    terms, corner = lax.optimization_barrier((terms, corner))
    inner, share = small(
        functools.partial(share_kernel, len(terms)), [(2 * rows, nb), ((1 + PANELS) * nb // 4, nb)], *terms, turned
    )
    shares = [share, *(across(share, way) for way in (first, second, both))]
    far = [over_rest({high | low: array}, low, across) for array in corner]
    far = [held[q] for held in far for q in sorted(held)]
    (found,) = products(corner_kernel, [slab, *far], (2 * rows // 4, nb))
    count, part = len(near), len(far) // PANELS
    pieces = [piece for p in range(PANELS) for piece in (*((at, p) for at in range(count)), *((count + p * part + at, None) for at in range(part)))]
    terms = lax.all_gather(found, "prow", axis=0)
    shares, terms = lax.optimization_barrier((shares, terms))
    matrices = small(matrices_kernel, [(nb, nb)] * (1 + PANELS), *shares)
    return update(inner, [terms], matrices, slab, [*near, *far], pieces)


def solution(mesh):
    in_specs = (P("pcol", "prow"), P(None, "pcol", "prow"), P(None, "pcol", None))
    out_specs = P("pcol", "prow")
    return jax.shard_map(functools.partial(body, dict(mesh.shape)), mesh=mesh, in_specs=in_specs, out_specs=out_specs, check_vma=False)
```

```python
import functools

import jax
import jax.numpy as jnp
from jax import lax
from jax.experimental import pallas as pl
from jax.experimental.pallas import tpu as pltpu
from jax.sharding import PartitionSpec as P


UNIT_LIMIT = 2048
TILE_LIMIT = 8192
VMEM_LIMIT = 32 * 1024 * 1024
SMALL_LIMIT = 8 * 1024 * 1024
COST = pl.CostEstimate(flops=1, bytes_accessed=1, transcendentals=0)
PANELS = 2
ROWS = (((1,), (1,)), ((), ()))
PLAIN = (((1,), (0,)), ((), ()))


def divisor(width, limit):
    for unit in (128, 1):
        fits = [t for t in range(unit, min(limit, width) + 1, unit) if width % t == 0]
        if fits:
            return max(fits)
    return width


def split(value):
    high = value.astype(jnp.bfloat16)
    return high, (value - high.astype(jnp.float32)).astype(jnp.bfloat16)


def dot(left, right, dims):
    return lax.dot_general(left, right, dims, preferred_element_type=jnp.float32)


def exact(left, right, dims):
    return lax.dot_general(left, right, dims, precision=lax.Precision.HIGHEST, preferred_element_type=jnp.float32)


def column_tiles(width, limit):
    tile = divisor(width, limit)
    return [pl.ds(begin, tile) for begin in range(0, width, tile)]


def panel_rows(refs, panel, columns):
    return jnp.concatenate([ref[panel, :, columns] for ref in refs], axis=0)


def near_kernel(kept, slab_ref, *refs):
    vector_refs, out_ref, kept_refs = refs[: -1 - kept], refs[-1 - kept], refs[len(refs) - kept :]
    for ref, kept_ref in zip(vector_refs[1:], kept_refs):
        kept_ref[...] = ref[...]
    (rows, width), nb = slab_ref.shape, out_ref.shape[1]
    group = nb // 4
    total = 0
    for columns in column_tiles(width, TILE_LIMIT):
        (fh, fl), (sh, sl) = (split(panel_rows(vector_refs, p, columns)) for p in range(PANELS))
        ch, cl = split(slab_ref[:, columns])
        first = dot(jnp.concatenate([ch, cl], axis=0), fh, ROWS)
        first = first[:rows] + first[rows:] + dot(ch, fl, ROWS)
        high = jnp.concatenate([ch, fh[: 2 * group]], axis=0)
        low = jnp.concatenate([cl, fl[: 2 * group]], axis=0)
        second = dot(jnp.concatenate([high, low], axis=0), sh, ROWS)
        second = second[: high.shape[0]] + second[high.shape[0] :] + dot(high, sl, ROWS)
        total += jnp.concatenate([first, second], axis=0)
    inner, own, via = total[: 2 * rows], total[2 * rows : 2 * rows + group], total[2 * rows + group :]
    inner = jnp.concatenate([inner, jnp.zeros((2 * rows, group), jnp.float32)], axis=1)
    share = jnp.concatenate([own, via[:, 2 * group :]], axis=1)
    out_ref[...] = jnp.concatenate([inner, share], axis=0)


def corner_kernel(slab_ref, *refs):
    vector_refs, out_ref = refs[:-1], refs[-1]
    (rows, width), (part, nb) = slab_ref.shape, out_ref.shape
    total = 0
    for columns in column_tiles(width, TILE_LIMIT):
        vectors = jnp.concatenate(split(jnp.concatenate([ref[:, columns] for ref in vector_refs], axis=0)), axis=0)
        found = dot(vectors, jnp.concatenate(split(slab_ref[:, columns]), axis=0), ROWS)
        count = found.shape[0] // 2
        total += found[:count, :rows] + (found[:count, rows:] + found[count:, :rows])
    total = total.T
    total = jnp.concatenate([total[:, : nb // 4], total[:, nb // 4 :]], axis=0)
    out_ref[...] = jnp.concatenate([total[k * part : (k + 1) * part] for k in range(4)], axis=1)


def turn_kernel(size, *refs):
    factor_refs, out_ref = refs[:-1], refs[-1]
    nb, low = out_ref.shape[1], size // 4
    block = nb // size
    me = lax.axis_index("pcol")
    column = lax.broadcasted_iota(jnp.int32, (nb, nb), 1)
    place = column // block
    role = place // low
    swapped = ((role == 1) | (role == 2)) & (opposite(size) * (me % 2) == 1)
    bits = jnp.where(swapped, 3 - role, role) * low + place % low
    order = lax.broadcasted_iota(jnp.int32, (nb, nb), 0) == (bits ^ me) * block + column % block
    rows = [ref[p] for p in range(PANELS) for ref in factor_refs]
    out_ref[...] = exact(jnp.concatenate(rows, axis=0), order.astype(jnp.float32), PLAIN)


def share_kernel(terms, *refs):
    term_refs, turned_ref, inner_ref, share_ref = refs[:terms], *refs[terms:]
    group = share_ref.shape[0] // (1 + PANELS)
    total = term_refs[0][...]
    for ref in term_refs[1:]:
        total += ref[...]
    inner_ref[...] = total[:-group]
    share_ref[:group] = total[-group:]
    share_ref[group:] = turned_ref[...]


def from_place(value, q, block, lane):
    width = value.shape[1]
    bit = 1
    while bit * block < width:
        if q & bit:
            shift = bit * block
            ahead, behind = pltpu.roll(value, width - shift, 1), pltpu.roll(value, shift, 1)
            value = jnp.where((lane // shift) % 2 == 0, ahead, behind)
        bit *= 2
    return value


def matrices_kernel(*refs):
    share_refs, between_ref, triangle_refs = refs[:4], refs[4], refs[5:]
    nb = between_ref.shape[0]
    group = nb // 4
    lane = lax.broadcasted_iota(jnp.int32, (1, nb), 1)
    triangles = [[] for _ in range(PANELS)]
    for side in range(4):
        held = from_place(share_refs[side][...], side, group, lane)
        other = from_place(share_refs[side ^ 1][:group], side, group, lane)
        far = ((lane // group) ^ side) == 3
        between_ref[side * group : (side + 1) * group] = jnp.where(far, other, held[:group])
        for p in range(PANELS):
            triangles[p].append(held[(1 + p) * group : (2 + p) * group])
    for p in range(PANELS):
        triangle_refs[p][...] = jnp.concatenate(triangles[p], axis=0).T


def update_kernel(pieces, terms, *refs):
    near_ref, term_refs, (between_ref, first_ref, second_ref) = refs[0], refs[1 : 1 + terms], refs[1 + terms : 4 + terms]
    slab_ref, *vector_refs = refs[4 + terms : -3]
    out_ref, after, sems = refs[-3:]
    (rows, width), nb = slab_ref.shape, near_ref.shape[1]
    group = nb // 4

    total = term_refs[0][...]
    for ref in term_refs[1:]:
        total += ref[...]
    total = jnp.concatenate([total[:, k * group : (k + 1) * group] for k in range(4)], axis=0)
    total = near_ref[...] + jnp.concatenate([jnp.zeros((PANELS * rows, nb - group), jnp.float32), total], axis=1)
    scaled = exact(total[:rows], first_ref[...], PLAIN)
    inner = total[rows:] - exact(scaled, between_ref[...], PLAIN)
    later = exact(inner, second_ref[...], PLAIN)
    both = jnp.concatenate(split(jnp.concatenate([scaled, later], axis=1)), axis=0)

    copies = []
    for at, columns in enumerate(column_tiles(width, UNIT_LIMIT)):
        blocks = [vector_refs[ref][:, columns] if p is None else vector_refs[ref][p, :, columns] for ref, p in pieces]
        high, low = split(jnp.concatenate(blocks, axis=0))
        main = dot(both, high, PLAIN)
        rest = dot(both[:rows], low, PLAIN)
        after[:, columns] = slab_ref[:, columns] - (main[:rows] + main[rows:] + rest)
        copies.append(pltpu.make_async_copy(after.at[:, columns], out_ref.at[:, columns], sems.at[at]))
        copies[-1].start()
    for copy in copies:
        copy.wait()


def products(kernel, arrays, *shapes):
    return pl.pallas_call(
        kernel,
        in_specs=[pl.BlockSpec(memory_space=pltpu.VMEM)] * len(arrays),
        out_specs=[pl.BlockSpec(memory_space=pltpu.VMEM)] * len(shapes),
        out_shape=[jax.ShapeDtypeStruct(shape, jnp.float32) for shape in shapes],
        compiler_params=pltpu.CompilerParams(vmem_limit_bytes=VMEM_LIMIT),
        cost_estimate=COST,
    )(*arrays)


def small(kernel, shapes, *arrays):
    return pl.pallas_call(
        kernel,
        out_shape=[jax.ShapeDtypeStruct(shape, jnp.float32) for shape in shapes],
        compiler_params=pltpu.CompilerParams(vmem_limit_bytes=SMALL_LIMIT),
        cost_estimate=COST,
    )(*arrays)


def update(near, terms, matrices, slab, arrays, pieces):
    width = slab.shape[1]
    whole = [near, *terms, *matrices, slab, *arrays]
    return pl.pallas_call(
        functools.partial(update_kernel, pieces, len(terms)),
        in_specs=[pl.BlockSpec(memory_space=pltpu.VMEM)] * len(whole),
        out_specs=pl.BlockSpec(memory_space=pl.ANY),
        out_shape=jax.ShapeDtypeStruct(slab.shape, jnp.float32),
        scratch_shapes=[
            pltpu.VMEM(slab.shape, jnp.float32),
            pltpu.SemaphoreType.DMA((len(column_tiles(width, UNIT_LIMIT)),)),
        ],
        compiler_params=pltpu.CompilerParams(vmem_limit_bytes=VMEM_LIMIT),
        cost_estimate=COST,
    )(*whole)


def opposite(size):
    return int(size > 4)


def exchange(array, partner, size, axis):
    return lax.ppermute(array, axis, [(i, i ^ partner(i)) for i in range(size)])


def summed_terms(value, depth, step):
    terms, reach = [value], 1
    while reach < depth:
        value = sum(terms[1:], terms[0])
        span = min(step, depth // reach)
        terms = [value] + [exchange(value, lambda i, k=k: k * reach, depth, "prow") for k in reversed(range(1, span))]
        reach *= span
    return terms


def over_rest(held, low, across):
    bit = 1
    while bit < low:
        for q, array in list(held.items()):
            turned = q // low in (1, 2) and bit == 1
            held[(q ^ (3 * low) if turned else q) | bit] = across(array, lambda i, bit=bit: bit)
        bit *= 2
    return held


def body(sizes, slab, reflectors, factors):
    size, depth = sizes["pcol"], sizes["prow"]
    rows = slab.shape[0]
    block, nb = factors.shape[1:]
    high, low = size // 2, size // 4
    across = functools.partial(exchange, size=size, axis="pcol")
    first = lambda i: high if opposite(size) * (i % 2) else low
    second = lambda i: low if opposite(size) * (i % 2) else high
    both = lambda i: high | low

    by_first, by_second = across(reflectors, first), across(reflectors, second)
    corner = [across(by_second[0], first), across(by_first[1], second)]
    near = over_rest({0: reflectors, low: by_first, high: by_second}, low, across)
    near = [near[q] for q in sorted(near)]
    group = over_rest({0: factors}, low, across)
    (turned,) = small(functools.partial(turn_kernel, size), [(PANELS * nb // 4, nb)], *[group[q] for q in sorted(group)])
    near, turned = lax.optimization_barrier((near, turned))
    (total,) = products(functools.partial(near_kernel, 0), [slab, *near], (2 * rows + nb // 4, nb))
    terms = summed_terms(total, depth, 4)
    terms, corner = lax.optimization_barrier((terms, corner))
    inner, share = small(
        functools.partial(share_kernel, len(terms)), [(2 * rows, nb), ((1 + PANELS) * nb // 4, nb)], *terms, turned
    )
    shares = [share, *(across(share, way) for way in (first, second, both))]
    far = [over_rest({high | low: array}, low, across) for array in corner]
    far = [held[q] for held in far for q in sorted(held)]
    matrices = small(matrices_kernel, [(nb, nb)] * (1 + PANELS), *shares)
    (found,) = products(corner_kernel, [slab, *far], (2 * rows // 4, nb))
    count, part = len(near), len(far) // PANELS
    pieces = [piece for p in range(PANELS) for piece in (*((at, p) for at in range(count)), *((count + p * part + at, None) for at in range(part)))]
    return update(inner, summed_terms(found, depth, 4), matrices, slab, [*near, *far], pieces)


def solution(mesh):
    in_specs = (P("pcol", "prow"), P(None, "pcol", "prow"), P(None, "pcol", None))
    out_specs = P("pcol", "prow")
    return jax.shard_map(functools.partial(body, dict(mesh.shape)), mesh=mesh, in_specs=in_specs, out_specs=out_specs, check_vma=False)
```

```python
import functools

import jax
import jax.numpy as jnp
from jax import lax
from jax.experimental import pallas as pl
from jax.experimental.pallas import tpu as pltpu
from jax.sharding import PartitionSpec as P


UNIT_LIMIT = 2048
TILE_LIMIT = 8192
VMEM_LIMIT = 32 * 1024 * 1024
SMALL_LIMIT = 8 * 1024 * 1024
COST = pl.CostEstimate(flops=1, bytes_accessed=1, transcendentals=0)
PANELS = 2
ROWS = (((1,), (1,)), ((), ()))
PLAIN = (((1,), (0,)), ((), ()))


def divisor(width, limit):
    for unit in (128, 1):
        fits = [t for t in range(unit, min(limit, width) + 1, unit) if width % t == 0]
        if fits:
            return max(fits)
    return width


def split(value):
    high = value.astype(jnp.bfloat16)
    return high, (value - high.astype(jnp.float32)).astype(jnp.bfloat16)


def dot(left, right, dims):
    return lax.dot_general(left, right, dims, preferred_element_type=jnp.float32)


def exact(left, right, dims):
    return lax.dot_general(left, right, dims, precision=lax.Precision.HIGHEST, preferred_element_type=jnp.float32)


def column_tiles(width, limit):
    tile = divisor(width, limit)
    return [pl.ds(begin, tile) for begin in range(0, width, tile)]


def panel_rows(refs, panel, columns):
    return jnp.concatenate([ref[panel, :, columns] for ref in refs], axis=0)


def near_kernel(kept, slab_ref, *refs):
    vector_refs, out_ref, kept_refs = refs[: -1 - kept], refs[-1 - kept], refs[len(refs) - kept :]
    for ref, kept_ref in zip(vector_refs[1:], kept_refs):
        kept_ref[...] = ref[...]
    (rows, width), nb = slab_ref.shape, out_ref.shape[1]
    group = nb // 4
    total = 0
    for columns in column_tiles(width, TILE_LIMIT):
        (fh, fl), (sh, sl) = (split(panel_rows(vector_refs, p, columns)) for p in range(PANELS))
        ch, cl = split(slab_ref[:, columns])
        first = dot(jnp.concatenate([ch, cl], axis=0), fh, ROWS)
        first = first[:rows] + first[rows:] + dot(ch, fl, ROWS)
        high = jnp.concatenate([ch, fh[: 2 * group]], axis=0)
        low = jnp.concatenate([cl, fl[: 2 * group]], axis=0)
        second = dot(jnp.concatenate([high, low], axis=0), sh, ROWS)
        second = second[: high.shape[0]] + second[high.shape[0] :] + dot(high, sl, ROWS)
        total += jnp.concatenate([first, second], axis=0)
    inner, own, via = total[: 2 * rows], total[2 * rows : 2 * rows + group], total[2 * rows + group :]
    inner = jnp.concatenate([inner, jnp.zeros((2 * rows, group), jnp.float32)], axis=1)
    share = jnp.concatenate([own, via[:, 2 * group :]], axis=1)
    out_ref[...] = jnp.concatenate([inner, share], axis=0)


def corner_kernel(slab_ref, *refs):
    vector_refs, out_ref = refs[:-1], refs[-1]
    (rows, width), (part, nb) = slab_ref.shape, out_ref.shape
    total = 0
    for columns in column_tiles(width, width):
        vh, vl = split(jnp.concatenate([ref[:, columns] for ref in vector_refs], axis=0))
        ch, cl = split(slab_ref[:, columns])
        found = dot(jnp.concatenate([ch, cl], axis=0), vh, ROWS)
        total += found[:rows] + found[rows:] + dot(ch, vl, ROWS)
    total = jnp.concatenate([total[:, : nb // 4], total[:, nb // 4 :]], axis=0)
    out_ref[...] = jnp.concatenate([total[k * part : (k + 1) * part] for k in range(4)], axis=1)


def turn_kernel(size, *refs):
    factor_refs, out_ref = refs[:-1], refs[-1]
    nb, low = out_ref.shape[1], size // 4
    block = nb // size
    me = lax.axis_index("pcol")
    column = lax.broadcasted_iota(jnp.int32, (nb, nb), 1)
    place = column // block
    role = place // low
    swapped = ((role == 1) | (role == 2)) & (opposite(size) * (me % 2) == 1)
    bits = jnp.where(swapped, 3 - role, role) * low + place % low
    order = lax.broadcasted_iota(jnp.int32, (nb, nb), 0) == (bits ^ me) * block + column % block
    rows = [ref[p] for p in range(PANELS) for ref in factor_refs]
    out_ref[...] = exact(jnp.concatenate(rows, axis=0), order.astype(jnp.float32), PLAIN)


def share_kernel(terms, *refs):
    term_refs, turned_ref, inner_ref, share_ref = refs[:terms], *refs[terms:]
    group = share_ref.shape[0] // (1 + PANELS)
    total = term_refs[0][...]
    for ref in term_refs[1:]:
        total += ref[...]
    inner_ref[...] = total[:-group]
    share_ref[:group] = total[-group:]
    share_ref[group:] = turned_ref[...]


def from_place(value, q, block, lane):
    width = value.shape[1]
    bit = 1
    while bit * block < width:
        if q & bit:
            shift = bit * block
            ahead, behind = pltpu.roll(value, width - shift, 1), pltpu.roll(value, shift, 1)
            value = jnp.where((lane // shift) % 2 == 0, ahead, behind)
        bit *= 2
    return value


def matrices_kernel(*refs):
    share_refs, between_ref, triangle_refs = refs[:4], refs[4], refs[5:]
    nb = between_ref.shape[1]
    group = nb // 4
    lane = lax.broadcasted_iota(jnp.int32, (1, nb), 1)
    between, triangles = [], [[] for _ in range(PANELS)]
    for side in range(4):
        held = from_place(share_refs[side][...], side, group, lane)
        other = from_place(share_refs[side ^ 1][:group], side, group, lane)
        far = ((lane // group) ^ side) == 3
        between.append(jnp.where(far, other, held[:group]))
        for p in range(PANELS):
            triangles[p].append(held[(1 + p) * group : (2 + p) * group])
    between_ref[...] = jnp.concatenate(split(jnp.concatenate(between, axis=0)), axis=0)
    for p in range(PANELS):
        triangle_refs[p][...] = jnp.concatenate(split(jnp.concatenate(triangles[p], axis=0).T), axis=0)


def times(left, parts):
    rows, depth = left.shape
    high, low = split(left)
    main = dot(jnp.concatenate([high, low], axis=0), parts[:depth], PLAIN)
    return main[:rows] + (main[rows:] + dot(high, parts[depth:], PLAIN))


def update_kernel(pieces, terms, *refs):
    near_ref, term_refs, (between_ref, first_ref, second_ref) = refs[0], refs[1 : 1 + terms], refs[1 + terms : 4 + terms]
    slab_ref, *vector_refs = refs[4 + terms : -3]
    out_ref, after, sems = refs[-3:]
    (rows, width), nb = slab_ref.shape, near_ref.shape[1]
    group = nb // 4

    total = term_refs[0][...]
    for ref in term_refs[1:]:
        total += ref[...]
    total = jnp.concatenate([total[:, k * group : (k + 1) * group] for k in range(4)], axis=0)
    total = near_ref[...] + jnp.concatenate([jnp.zeros((PANELS * rows, nb - group), jnp.float32), total], axis=1)
    scaled = times(total[:rows], first_ref[...])
    inner = total[rows:] - times(scaled, between_ref[...])
    later = times(inner, second_ref[...])
    both = jnp.concatenate(split(jnp.concatenate([scaled, later], axis=1)), axis=0)

    copies = []
    for at, columns in enumerate(column_tiles(width, UNIT_LIMIT)):
        blocks = [vector_refs[ref][:, columns] if p is None else vector_refs[ref][p, :, columns] for ref, p in pieces]
        high, low = split(jnp.concatenate(blocks, axis=0))
        main = dot(both, high, PLAIN)
        rest = dot(both[:rows], low, PLAIN)
        after[:, columns] = slab_ref[:, columns] - (main[:rows] + main[rows:] + rest)
        copies.append(pltpu.make_async_copy(after.at[:, columns], out_ref.at[:, columns], sems.at[at]))
        copies[-1].start()
    for copy in copies:
        copy.wait()


def products(kernel, arrays, *shapes):
    return pl.pallas_call(
        kernel,
        in_specs=[pl.BlockSpec(memory_space=pltpu.VMEM)] * len(arrays),
        out_specs=[pl.BlockSpec(memory_space=pltpu.VMEM)] * len(shapes),
        out_shape=[jax.ShapeDtypeStruct(shape, jnp.float32) for shape in shapes],
        compiler_params=pltpu.CompilerParams(vmem_limit_bytes=VMEM_LIMIT),
        cost_estimate=COST,
    )(*arrays)


def small(kernel, shapes, *arrays, kind=jnp.float32):
    return pl.pallas_call(
        kernel,
        out_shape=[jax.ShapeDtypeStruct(shape, kind) for shape in shapes],
        compiler_params=pltpu.CompilerParams(vmem_limit_bytes=SMALL_LIMIT),
        cost_estimate=COST,
    )(*arrays)


def update(near, terms, matrices, slab, arrays, pieces):
    width = slab.shape[1]
    whole = [near, *terms, *matrices, slab, *arrays]
    return pl.pallas_call(
        functools.partial(update_kernel, pieces, len(terms)),
        in_specs=[pl.BlockSpec(memory_space=pltpu.VMEM)] * len(whole),
        out_specs=pl.BlockSpec(memory_space=pl.ANY),
        out_shape=jax.ShapeDtypeStruct(slab.shape, jnp.float32),
        scratch_shapes=[
            pltpu.VMEM(slab.shape, jnp.float32),
            pltpu.SemaphoreType.DMA((len(column_tiles(width, UNIT_LIMIT)),)),
        ],
        compiler_params=pltpu.CompilerParams(vmem_limit_bytes=VMEM_LIMIT),
        cost_estimate=COST,
    )(*whole)


def opposite(size):
    return int(size > 4)


def exchange(array, partner, size, axis):
    return lax.ppermute(array, axis, [(i, i ^ partner(i)) for i in range(size)])


def summed_terms(value, depth, step):
    terms, reach = [value], 1
    while reach < depth:
        value = sum(terms[1:], terms[0])
        span = min(step, depth // reach)
        terms = [value] + [exchange(value, lambda i, k=k: k * reach, depth, "prow") for k in range(1, span)]
        reach *= span
    return terms


def over_rest(held, low, across):
    bit = 1
    while bit < low:
        for q, array in list(held.items()):
            turned = q // low in (1, 2) and bit == 1
            held[(q ^ (3 * low) if turned else q) | bit] = across(array, lambda i, bit=bit: bit)
        bit *= 2
    return held


def body(sizes, slab, reflectors, factors):
    size, depth = sizes["pcol"], sizes["prow"]
    rows = slab.shape[0]
    block, nb = factors.shape[1:]
    high, low = size // 2, size // 4
    across = functools.partial(exchange, size=size, axis="pcol")
    first = lambda i: high if opposite(size) * (i % 2) else low
    second = lambda i: low if opposite(size) * (i % 2) else high
    both = lambda i: high | low

    by_first, by_second = across(reflectors, first), across(reflectors, second)
    corner = [across(by_second[0], first), across(by_first[1], second)]
    near = over_rest({0: reflectors, low: by_first, high: by_second}, low, across)
    near = [near[q] for q in sorted(near)]
    group = over_rest({0: factors}, low, across)
    (turned,) = small(functools.partial(turn_kernel, size), [(PANELS * nb // 4, nb)], *[group[q] for q in sorted(group)])
    near, turned = lax.optimization_barrier((near, turned))
    (total,) = products(functools.partial(near_kernel, 0), [slab, *near], (2 * rows + nb // 4, nb))
    terms = summed_terms(total, depth, 4)
    terms, corner = lax.optimization_barrier((terms, corner))
    inner, share = small(
        functools.partial(share_kernel, len(terms)), [(2 * rows, nb), ((1 + PANELS) * nb // 4, nb)], *terms, turned
    )
    shares = [share, *(across(share, way) for way in (first, second, both))]
    far = [over_rest({high | low: array}, low, across) for array in corner]
    far = [held[q] for held in far for q in sorted(held)]
    matrices = small(matrices_kernel, [(2 * nb, nb)] * (1 + PANELS), *shares, kind=jnp.bfloat16)
    (found,) = products(corner_kernel, [slab, *far], (2 * rows // 4, nb))
    count, part = len(near), len(far) // PANELS
    pieces = [piece for p in range(PANELS) for piece in (*((at, p) for at in range(count)), *((count + p * part + at, None) for at in range(part)))]
    return update(inner, summed_terms(found, depth, 4), matrices, slab, [*near, *far], pieces)


def solution(mesh):
    in_specs = (P("pcol", "prow"), P(None, "pcol", "prow"), P(None, "pcol", None))
    out_specs = P("pcol", "prow")
    return jax.shard_map(functools.partial(body, dict(mesh.shape)), mesh=mesh, in_specs=in_specs, out_specs=out_specs, check_vma=False)
```

```python
import functools

import jax
import jax.numpy as jnp
from jax import lax
from jax.experimental import pallas as pl
from jax.experimental.pallas import tpu as pltpu
from jax.sharding import PartitionSpec as P


TILE_LIMIT = 8192
VMEM_LIMIT = 32 * 1024 * 1024
SMALL_LIMIT = 8 * 1024 * 1024
COST = pl.CostEstimate(flops=1, bytes_accessed=1, transcendentals=0)
PANELS = 2
ROWS = (((1,), (1,)), ((), ()))
PLAIN = (((1,), (0,)), ((), ()))


def divisor(width, limit):
    for unit in (128, 1):
        fits = [t for t in range(unit, min(limit, width) + 1, unit) if width % t == 0]
        if fits:
            return max(fits)
    return width


def split(value):
    high = value.astype(jnp.bfloat16)
    return high, (value - high.astype(jnp.float32)).astype(jnp.bfloat16)


def dot(left, right, dims):
    return lax.dot_general(left, right, dims, preferred_element_type=jnp.float32)


def exact(left, right, dims):
    return lax.dot_general(left, right, dims, precision=lax.Precision.HIGHEST, preferred_element_type=jnp.float32)


def column_tiles(width, limit):
    tile = divisor(width, limit)
    return [pl.ds(begin, tile) for begin in range(0, width, tile)]


def panel_rows(refs, panel, columns):
    return jnp.concatenate([ref[panel, :, columns] for ref in refs], axis=0)


def near_kernel(kept, slab_ref, *refs):
    vector_refs, out_ref, kept_refs = refs[: -1 - kept], refs[-1 - kept], refs[len(refs) - kept :]
    for ref, kept_ref in zip(vector_refs[1:], kept_refs):
        kept_ref[...] = ref[...]
    (rows, width), nb = slab_ref.shape, out_ref.shape[1]
    group = nb // 4
    total = 0
    for columns in column_tiles(width, TILE_LIMIT):
        (fh, fl), (sh, sl) = (split(panel_rows(vector_refs, p, columns)) for p in range(PANELS))
        ch, cl = split(slab_ref[:, columns])
        first = dot(jnp.concatenate([ch, cl], axis=0), fh, ROWS)
        first = first[:rows] + first[rows:] + dot(ch, fl, ROWS)
        high = jnp.concatenate([ch, fh[: 2 * group]], axis=0)
        low = jnp.concatenate([cl, fl[: 2 * group]], axis=0)
        second = dot(jnp.concatenate([high, low], axis=0), sh, ROWS)
        second = second[: high.shape[0]] + second[high.shape[0] :] + dot(high, sl, ROWS)
        total += jnp.concatenate([first, second], axis=0)
    inner, own, via = total[: 2 * rows], total[2 * rows : 2 * rows + group], total[2 * rows + group :]
    inner = jnp.concatenate([inner, jnp.zeros((2 * rows, group), jnp.float32)], axis=1)
    share = jnp.concatenate([own, via[:, 2 * group :]], axis=1)
    out_ref[...] = jnp.concatenate([inner, share], axis=0)


def corner_kernel(slab_ref, *refs):
    vector_refs, out_ref = refs[:-1], refs[-1]
    (rows, width), (part, nb) = slab_ref.shape, out_ref.shape
    total = 0
    for columns in column_tiles(width, TILE_LIMIT):
        vh, vl = split(jnp.concatenate([ref[:, columns] for ref in vector_refs], axis=0))
        ch, cl = split(slab_ref[:, columns])
        found = dot(jnp.concatenate([ch, cl], axis=0), vh, ROWS)
        total += found[:rows] + found[rows:] + dot(ch, vl, ROWS)
    total = jnp.concatenate([total[:, : nb // 4], total[:, nb // 4 :]], axis=0)
    out_ref[...] = jnp.concatenate([total[k * part : (k + 1) * part] for k in range(4)], axis=1)


def turn_kernel(size, *refs):
    factor_refs, out_ref = refs[:-1], refs[-1]
    nb, low = out_ref.shape[1], size // 4
    block = nb // size
    me = lax.axis_index("pcol")
    column = lax.broadcasted_iota(jnp.int32, (nb, nb), 1)
    place = column // block
    role = place // low
    swapped = ((role == 1) | (role == 2)) & (opposite(size) * (me % 2) == 1)
    bits = jnp.where(swapped, 3 - role, role) * low + place % low
    order = lax.broadcasted_iota(jnp.int32, (nb, nb), 0) == (bits ^ me) * block + column % block
    rows = [ref[p] for p in range(PANELS) for ref in factor_refs]
    out_ref[...] = exact(jnp.concatenate(rows, axis=0), order.astype(jnp.float32), PLAIN)


def share_kernel(terms, *refs):
    term_refs, turned_ref, inner_ref, share_ref = refs[:terms], *refs[terms:]
    group = share_ref.shape[0] // (1 + PANELS)
    total = term_refs[0][...]
    for ref in term_refs[1:]:
        total += ref[...]
    inner_ref[...] = total[:-group]
    share_ref[:group] = total[-group:]
    share_ref[group:] = turned_ref[...]


def from_place(value, q, block, lane):
    width = value.shape[1]
    bit = 1
    while bit * block < width:
        if q & bit:
            shift = bit * block
            ahead, behind = pltpu.roll(value, width - shift, 1), pltpu.roll(value, shift, 1)
            value = jnp.where((lane // shift) % 2 == 0, ahead, behind)
        bit *= 2
    return value


def matrices_kernel(*refs):
    share_refs, between_ref, triangle_refs = refs[:4], refs[4], refs[5:]
    nb = between_ref.shape[0]
    group = nb // 4
    lane = lax.broadcasted_iota(jnp.int32, (1, nb), 1)
    triangles = [[] for _ in range(PANELS)]
    for side in range(4):
        held = from_place(share_refs[side][...], side, group, lane)
        other = from_place(share_refs[side ^ 1][:group], side, group, lane)
        far = ((lane // group) ^ side) == 3
        between_ref[side * group : (side + 1) * group] = jnp.where(far, other, held[:group])
        for p in range(PANELS):
            triangles[p].append(held[(1 + p) * group : (2 + p) * group])
    for p in range(PANELS):
        triangle_refs[p][...] = jnp.concatenate(triangles[p], axis=0).T


def update_kernel(pieces, terms, *refs):
    near_ref, term_refs, (between_ref, first_ref, second_ref) = refs[0], refs[1 : 1 + terms], refs[1 + terms : 4 + terms]
    slab_ref, *vector_refs = refs[4 + terms : -3]
    out_ref, after, sems = refs[-3:]
    (rows, width), nb = slab_ref.shape, near_ref.shape[1]
    group = nb // 4

    total = term_refs[0][...]
    for ref in term_refs[1:]:
        total += ref[...]
    total = jnp.concatenate([total[:, k * group : (k + 1) * group] for k in range(4)], axis=0)
    total = near_ref[...] + jnp.concatenate([jnp.zeros((PANELS * rows, nb - group), jnp.float32), total], axis=1)
    scaled = exact(total[:rows], first_ref[...], PLAIN)
    inner = total[rows:] - exact(scaled, between_ref[...], PLAIN)
    later = exact(inner, second_ref[...], PLAIN)
    both = jnp.concatenate(split(jnp.concatenate([scaled, later], axis=1)), axis=0)

    copies = []
    for at, columns in enumerate(column_tiles(width, TILE_LIMIT)):
        blocks = [vector_refs[ref][:, columns] if p is None else vector_refs[ref][p, :, columns] for ref, p in pieces]
        high, low = split(jnp.concatenate(blocks, axis=0))
        main = dot(both, high, PLAIN)
        rest = dot(both[:rows], low, PLAIN)
        after[:, columns] = slab_ref[:, columns] - (main[:rows] + main[rows:] + rest)
        copies.append(pltpu.make_async_copy(after.at[:, columns], out_ref.at[:, columns], sems.at[at]))
        copies[-1].start()
    for copy in copies:
        copy.wait()


def products(kernel, arrays, *shapes):
    return pl.pallas_call(
        kernel,
        in_specs=[pl.BlockSpec(memory_space=pltpu.VMEM)] * len(arrays),
        out_specs=[pl.BlockSpec(memory_space=pltpu.VMEM)] * len(shapes),
        out_shape=[jax.ShapeDtypeStruct(shape, jnp.float32) for shape in shapes],
        compiler_params=pltpu.CompilerParams(vmem_limit_bytes=VMEM_LIMIT),
        cost_estimate=COST,
    )(*arrays)


def small(kernel, shapes, *arrays):
    return pl.pallas_call(
        kernel,
        out_shape=[jax.ShapeDtypeStruct(shape, jnp.float32) for shape in shapes],
        compiler_params=pltpu.CompilerParams(vmem_limit_bytes=SMALL_LIMIT),
        cost_estimate=COST,
    )(*arrays)


def update(near, terms, matrices, slab, arrays, pieces):
    width = slab.shape[1]
    whole = [near, *terms, *matrices, slab, *arrays]
    return pl.pallas_call(
        functools.partial(update_kernel, pieces, len(terms)),
        in_specs=[pl.BlockSpec(memory_space=pltpu.VMEM)] * len(whole),
        out_specs=pl.BlockSpec(memory_space=pl.ANY),
        out_shape=jax.ShapeDtypeStruct(slab.shape, jnp.float32),
        scratch_shapes=[
            pltpu.VMEM(slab.shape, jnp.float32),
            pltpu.SemaphoreType.DMA((len(column_tiles(width, TILE_LIMIT)),)),
        ],
        compiler_params=pltpu.CompilerParams(vmem_limit_bytes=VMEM_LIMIT),
        cost_estimate=COST,
    )(*whole)


def opposite(size):
    return int(size > 4)


def exchange(array, partner, size, axis):
    return lax.ppermute(array, axis, [(i, i ^ partner(i)) for i in range(size)])


def summed_terms(value, depth, step):
    terms, reach = [value], 1
    while reach < depth:
        value = sum(terms[1:], terms[0])
        span = min(step, depth // reach)
        terms = [value] + [exchange(value, lambda i, k=k: k * reach, depth, "prow") for k in range(1, span)]
        reach *= span
    return terms


def over_rest(held, low, across):
    bit = 1
    while bit < low:
        for q, array in list(held.items()):
            turned = q // low in (1, 2) and bit == 1
            held[(q ^ (3 * low) if turned else q) | bit] = across(array, lambda i, bit=bit: bit)
        bit *= 2
    return held


def body(sizes, slab, reflectors, factors):
    size, depth = sizes["pcol"], sizes["prow"]
    rows = slab.shape[0]
    block, nb = factors.shape[1:]
    high, low = size // 2, size // 4
    across = functools.partial(exchange, size=size, axis="pcol")
    first = lambda i: high if opposite(size) * (i % 2) else low
    second = lambda i: low if opposite(size) * (i % 2) else high
    both = lambda i: high | low

    by_first, by_second = across(reflectors, first), across(reflectors, second)
    corner = [across(by_second[0], first), across(by_first[1], second)]
    near = over_rest({0: reflectors, low: by_first, high: by_second}, low, across)
    near = [near[q] for q in sorted(near)]
    group = over_rest({0: factors}, low, across)
    (turned,) = small(functools.partial(turn_kernel, size), [(PANELS * nb // 4, nb)], *[group[q] for q in sorted(group)])
    near, turned = lax.optimization_barrier((near, turned))
    (total,) = products(functools.partial(near_kernel, 0), [slab, *near], (2 * rows + nb // 4, nb))
    terms = summed_terms(total, depth, 4)
    terms, corner = lax.optimization_barrier((terms, corner))
    inner, share = small(
        functools.partial(share_kernel, len(terms)), [(2 * rows, nb), ((1 + PANELS) * nb // 4, nb)], *terms, turned
    )
    shares = [share, *(across(share, way) for way in (first, second, both))]
    far = [over_rest({high | low: array}, low, across) for array in corner]
    far = [held[q] for held in far for q in sorted(held)]
    matrices = small(matrices_kernel, [(nb, nb)] * (1 + PANELS), *shares)
    (found,) = products(corner_kernel, [slab, *far], (2 * rows // 4, nb))
    count, part = len(near), len(far) // PANELS
    pieces = [piece for p in range(PANELS) for piece in (*((at, p) for at in range(count)), *((count + p * part + at, None) for at in range(part)))]
    return update(inner, summed_terms(found, depth, 4), matrices, slab, [*near, *far], pieces)


def solution(mesh):
    in_specs = (P("pcol", "prow"), P(None, "pcol", "prow"), P(None, "pcol", None))
    out_specs = P("pcol", "prow")
    return jax.shard_map(functools.partial(body, dict(mesh.shape)), mesh=mesh, in_specs=in_specs, out_specs=out_specs, check_vma=False)
```

```python
import functools

import jax
import jax.numpy as jnp
from jax import lax
from jax.experimental import pallas as pl
from jax.experimental.pallas import tpu as pltpu
from jax.sharding import PartitionSpec as P


UNIT_LIMIT = 2048
TILE_LIMIT = 8192
VMEM_LIMIT = 32 * 1024 * 1024
SMALL_LIMIT = 8 * 1024 * 1024
COST = pl.CostEstimate(flops=1, bytes_accessed=1, transcendentals=0)
PANELS = 2
ROWS = (((1,), (1,)), ((), ()))
PLAIN = (((1,), (0,)), ((), ()))


def divisor(width, limit):
    for unit in (128, 1):
        fits = [t for t in range(unit, min(limit, width) + 1, unit) if width % t == 0]
        if fits:
            return max(fits)
    return width


def split(value):
    high = value.astype(jnp.bfloat16)
    return high, (value - high.astype(jnp.float32)).astype(jnp.bfloat16)


def dot(left, right, dims):
    return lax.dot_general(left, right, dims, preferred_element_type=jnp.float32)


def exact(left, right, dims):
    return lax.dot_general(left, right, dims, precision=lax.Precision.HIGHEST, preferred_element_type=jnp.float32)


def column_tiles(width, limit):
    tile = divisor(width, limit)
    return [pl.ds(begin, tile) for begin in range(0, width, tile)]


def panel_rows(refs, panel, columns):
    return jnp.concatenate([ref[panel, :, columns] for ref in refs], axis=0)


def near_kernel(kept, slab_ref, *refs):
    vector_refs, out_ref, kept_refs = refs[: -1 - kept], refs[-1 - kept], refs[len(refs) - kept :]
    for ref, kept_ref in zip(vector_refs[1:], kept_refs):
        kept_ref[...] = ref[...]
    (rows, width), nb = slab_ref.shape, out_ref.shape[1]
    group = nb // 4
    total = 0
    for columns in column_tiles(width, TILE_LIMIT):
        (fh, fl), (sh, sl) = (split(panel_rows(vector_refs, p, columns)) for p in range(PANELS))
        ch, cl = split(slab_ref[:, columns])
        first = dot(jnp.concatenate([ch, cl], axis=0), fh, ROWS)
        first = first[:rows] + first[rows:] + dot(ch, fl, ROWS)
        high = jnp.concatenate([ch, fh[: 2 * group]], axis=0)
        low = jnp.concatenate([cl, fl[: 2 * group]], axis=0)
        second = dot(jnp.concatenate([high, low], axis=0), sh, ROWS)
        second = second[: high.shape[0]] + second[high.shape[0] :] + dot(high, sl, ROWS)
        total += jnp.concatenate([first, second], axis=0)
    inner, own, via = total[: 2 * rows], total[2 * rows : 2 * rows + group], total[2 * rows + group :]
    inner = jnp.concatenate([inner, jnp.zeros((2 * rows, group), jnp.float32)], axis=1)
    share = jnp.concatenate([own, via[:, 2 * group :]], axis=1)
    out_ref[...] = jnp.concatenate([inner, share], axis=0)


def corner_kernel(slab_ref, *refs):
    vector_refs, out_ref = refs[:-1], refs[-1]
    (rows, width), (part, nb) = slab_ref.shape, out_ref.shape
    total = 0
    for columns in column_tiles(width, TILE_LIMIT):
        vh, vl = split(jnp.concatenate([ref[:, columns] for ref in vector_refs], axis=0))
        ch, cl = split(slab_ref[:, columns])
        found = dot(jnp.concatenate([ch, cl], axis=0), vh, ROWS)
        total += found[:rows] + found[rows:] + dot(ch, vl, ROWS)
    total = jnp.concatenate([total[:, : nb // 4], total[:, nb // 4 :]], axis=0)
    out_ref[...] = jnp.concatenate([total[k * part : (k + 1) * part] for k in range(4)], axis=1)


def turn_kernel(size, *refs):
    factor_refs, out_ref = refs[:-1], refs[-1]
    nb, low = out_ref.shape[1], size // 4
    block = nb // size
    me = lax.axis_index("pcol")
    column = lax.broadcasted_iota(jnp.int32, (nb, nb), 1)
    place = column // block
    role = place // low
    swapped = ((role == 1) | (role == 2)) & (opposite(size) * (me % 2) == 1)
    bits = jnp.where(swapped, 3 - role, role) * low + place % low
    order = lax.broadcasted_iota(jnp.int32, (nb, nb), 0) == (bits ^ me) * block + column % block
    rows = [ref[p] for p in range(PANELS) for ref in factor_refs]
    out_ref[...] = exact(jnp.concatenate(rows, axis=0), order.astype(jnp.float32), PLAIN)


def share_kernel(terms, *refs):
    term_refs, turned_ref, inner_ref, share_ref = refs[:terms], *refs[terms:]
    group = share_ref.shape[0] // (1 + PANELS)
    total = term_refs[0][...]
    for ref in term_refs[1:]:
        total += ref[...]
    inner_ref[...] = total[:-group]
    share_ref[:group] = total[-group:]
    share_ref[group:] = turned_ref[...]


def from_place(value, q, block, lane):
    width = value.shape[1]
    bit = 1
    while bit * block < width:
        if q & bit:
            shift = bit * block
            ahead, behind = pltpu.roll(value, width - shift, 1), pltpu.roll(value, shift, 1)
            value = jnp.where((lane // shift) % 2 == 0, ahead, behind)
        bit *= 2
    return value


def matrices_kernel(*refs):
    share_refs, between_ref, triangle_refs = refs[:4], refs[4], refs[5:]
    nb = between_ref.shape[0]
    group = nb // 4
    lane = lax.broadcasted_iota(jnp.int32, (1, nb), 1)
    triangles = [[] for _ in range(PANELS)]
    for side in range(4):
        held = from_place(share_refs[side][...], side, group, lane)
        other = from_place(share_refs[side ^ 1][:group], side, group, lane)
        far = ((lane // group) ^ side) == 3
        between_ref[side * group : (side + 1) * group] = jnp.where(far, other, held[:group])
        for p in range(PANELS):
            triangles[p].append(held[(1 + p) * group : (2 + p) * group])
    for p in range(PANELS):
        triangle_refs[p][...] = jnp.concatenate(triangles[p], axis=0).T


def update_kernel(pieces, terms, *refs):
    near_ref, term_refs, (between_ref, first_ref, second_ref) = refs[0], refs[1 : 1 + terms], refs[1 + terms : 4 + terms]
    slab_ref, *vector_refs = refs[4 + terms : -3]
    out_ref, after, sems = refs[-3:]
    (rows, width), nb = slab_ref.shape, near_ref.shape[1]
    group = nb // 4

    total = term_refs[0][...]
    for ref in term_refs[1:]:
        total += ref[...]
    total = jnp.concatenate([total[:, k * group : (k + 1) * group] for k in range(4)], axis=0)
    total = near_ref[...] + jnp.concatenate([jnp.zeros((PANELS * rows, nb - group), jnp.float32), total], axis=1)
    scaled = exact(total[:rows], first_ref[...], PLAIN)
    inner = total[rows:] - exact(scaled, between_ref[...], PLAIN)
    later = exact(inner, second_ref[...], PLAIN)
    both = jnp.concatenate(split(jnp.concatenate([scaled, later], axis=1)), axis=0)

    copies = []
    for at, columns in enumerate(column_tiles(width, UNIT_LIMIT)):
        blocks = [vector_refs[ref][:, columns] if p is None else vector_refs[ref][p, :, columns] for ref, p in pieces]
        high, low = split(jnp.concatenate(blocks, axis=0))
        main = dot(both, high, PLAIN)
        rest = dot(both[:rows], low, PLAIN)
        after[:, columns] = slab_ref[:, columns] - (main[:rows] + main[rows:] + rest)
        copies.append(pltpu.make_async_copy(after.at[:, columns], out_ref.at[:, columns], sems.at[at]))
        copies[-1].start()
    for copy in copies:
        copy.wait()


def products(kernel, arrays, *shapes):
    return pl.pallas_call(
        kernel,
        in_specs=[pl.BlockSpec(memory_space=pltpu.VMEM)] * len(arrays),
        out_specs=[pl.BlockSpec(memory_space=pltpu.VMEM)] * len(shapes),
        out_shape=[jax.ShapeDtypeStruct(shape, jnp.float32) for shape in shapes],
        compiler_params=pltpu.CompilerParams(vmem_limit_bytes=VMEM_LIMIT),
        cost_estimate=COST,
    )(*arrays)


def small(kernel, shapes, *arrays):
    return pl.pallas_call(
        kernel,
        out_shape=[jax.ShapeDtypeStruct(shape, jnp.float32) for shape in shapes],
        compiler_params=pltpu.CompilerParams(vmem_limit_bytes=SMALL_LIMIT),
        cost_estimate=COST,
    )(*arrays)


def update(near, terms, matrices, slab, arrays, pieces):
    width = slab.shape[1]
    whole = [near, *terms, *matrices, slab, *arrays]
    return pl.pallas_call(
        functools.partial(update_kernel, pieces, len(terms)),
        in_specs=[pl.BlockSpec(memory_space=pltpu.VMEM)] * len(whole),
        out_specs=pl.BlockSpec(memory_space=pl.ANY),
        out_shape=jax.ShapeDtypeStruct(slab.shape, jnp.float32),
        scratch_shapes=[
            pltpu.VMEM(slab.shape, jnp.float32),
            pltpu.SemaphoreType.DMA((len(column_tiles(width, UNIT_LIMIT)),)),
        ],
        compiler_params=pltpu.CompilerParams(vmem_limit_bytes=VMEM_LIMIT),
        cost_estimate=COST,
    )(*whole)


def opposite(size):
    return int(size > 4)


def exchange(array, partner, size, axis):
    return lax.ppermute(array, axis, [(i, i ^ partner(i)) for i in range(size)])


def summed_terms(value, depth, step):
    terms, reach = [value], 1
    while reach < depth:
        value = sum(terms[1:], terms[0])
        span = min(step, depth // reach)
        steps = sorted(range(1, span), key=lambda k: (k != 1, k != span - 1))
        terms = [value] + [exchange(value, lambda i, k=k: k * reach, depth, "prow") for k in steps]
        reach *= span
    return terms


def over_rest(held, low, across):
    bit = 1
    while bit < low:
        for q, array in list(held.items()):
            turned = q // low in (1, 2) and bit == 1
            held[(q ^ (3 * low) if turned else q) | bit] = across(array, lambda i, bit=bit: bit)
        bit *= 2
    return held


def body(sizes, slab, reflectors, factors):
    size, depth = sizes["pcol"], sizes["prow"]
    rows = slab.shape[0]
    block, nb = factors.shape[1:]
    high, low = size // 2, size // 4
    across = functools.partial(exchange, size=size, axis="pcol")
    first = lambda i: high if opposite(size) * (i % 2) else low
    second = lambda i: low if opposite(size) * (i % 2) else high
    both = lambda i: high | low

    by_first, by_second = across(reflectors, first), across(reflectors, second)
    corner = [across(by_second[0], first), across(by_first[1], second)]
    near = over_rest({0: reflectors, low: by_first, high: by_second}, low, across)
    near = [near[q] for q in sorted(near)]
    group = over_rest({0: factors}, low, across)
    (turned,) = small(functools.partial(turn_kernel, size), [(PANELS * nb // 4, nb)], *[group[q] for q in sorted(group)])
    near, turned = lax.optimization_barrier((near, turned))
    (total,) = products(functools.partial(near_kernel, 0), [slab, *near], (2 * rows + nb // 4, nb))
    terms = summed_terms(total, depth, 4)
    terms, corner = lax.optimization_barrier((terms, corner))
    inner, share = small(
        functools.partial(share_kernel, len(terms)), [(2 * rows, nb), ((1 + PANELS) * nb // 4, nb)], *terms, turned
    )
    shares = [share, *(across(share, way) for way in (first, second, both))]
    far = [over_rest({high | low: array}, low, across) for array in corner]
    far = [held[q] for held in far for q in sorted(held)]
    matrices = small(matrices_kernel, [(nb, nb)] * (1 + PANELS), *shares)
    (found,) = products(corner_kernel, [slab, *far], (2 * rows // 4, nb))
    count, part = len(near), len(far) // PANELS
    pieces = [piece for p in range(PANELS) for piece in (*((at, p) for at in range(count)), *((count + p * part + at, None) for at in range(part)))]
    return update(inner, summed_terms(found, depth, 4), matrices, slab, [*near, *far], pieces)


def solution(mesh):
    in_specs = (P("pcol", "prow"), P(None, "pcol", "prow"), P(None, "pcol", None))
    out_specs = P("pcol", "prow")
    return jax.shard_map(functools.partial(body, dict(mesh.shape)), mesh=mesh, in_specs=in_specs, out_specs=out_specs, check_vma=False)
```

```python
import functools

import jax
import jax.numpy as jnp
from jax import lax
from jax.experimental import pallas as pl
from jax.experimental.pallas import tpu as pltpu
from jax.sharding import PartitionSpec as P


UNIT_LIMIT = 2048
TILE_LIMIT = 8192
VMEM_LIMIT = 32 * 1024 * 1024
SMALL_LIMIT = 8 * 1024 * 1024
COST = pl.CostEstimate(flops=1, bytes_accessed=1, transcendentals=0)
PANELS = 2
ROWS = (((1,), (1,)), ((), ()))
PLAIN = (((1,), (0,)), ((), ()))


def divisor(width, limit):
    for unit in (128, 1):
        fits = [t for t in range(unit, min(limit, width) + 1, unit) if width % t == 0]
        if fits:
            return max(fits)
    return width


def split(value):
    high = value.astype(jnp.bfloat16)
    return high, (value - high.astype(jnp.float32)).astype(jnp.bfloat16)


def dot(left, right, dims):
    return lax.dot_general(left, right, dims, preferred_element_type=jnp.float32)


def exact(left, right, dims):
    return lax.dot_general(left, right, dims, precision=lax.Precision.HIGHEST, preferred_element_type=jnp.float32)


def column_tiles(width, limit):
    tile = divisor(width, limit)
    return [pl.ds(begin, tile) for begin in range(0, width, tile)]


def panel_rows(refs, panel, columns):
    return jnp.concatenate([ref[panel, :, columns] for ref in refs], axis=0)


def near_kernel(kept, slab_ref, *refs):
    vector_refs, out_ref, kept_refs = refs[: -1 - kept], refs[-1 - kept], refs[len(refs) - kept :]
    for ref, kept_ref in zip(vector_refs[1:], kept_refs):
        kept_ref[...] = ref[...]
    (rows, width), nb = slab_ref.shape, out_ref.shape[1]
    group = nb // 4
    total = 0
    for columns in column_tiles(width, TILE_LIMIT):
        (fh, fl), (sh, sl) = (split(panel_rows(vector_refs, p, columns)) for p in range(PANELS))
        ch, cl = split(slab_ref[:, columns])
        first = dot(jnp.concatenate([ch, cl], axis=0), fh, ROWS)
        first = first[:rows] + first[rows:] + dot(ch, fl, ROWS)
        high = jnp.concatenate([ch, fh[: 2 * group]], axis=0)
        low = jnp.concatenate([cl, fl[: 2 * group]], axis=0)
        second = dot(jnp.concatenate([high, low], axis=0), sh, ROWS)
        second = second[: high.shape[0]] + second[high.shape[0] :] + dot(high, sl, ROWS)
        total += jnp.concatenate([first, second], axis=0)
    inner, own, via = total[: 2 * rows], total[2 * rows : 2 * rows + group], total[2 * rows + group :]
    inner = jnp.concatenate([inner, jnp.zeros((2 * rows, group), jnp.float32)], axis=1)
    share = jnp.concatenate([own, via[:, 2 * group :]], axis=1)
    out_ref[...] = jnp.concatenate([inner, share], axis=0)


def corner_kernel(slab_ref, *refs):
    vector_refs, out_ref = refs[:-1], refs[-1]
    (rows, width), (part, nb) = slab_ref.shape, out_ref.shape
    total = 0
    for columns in column_tiles(width, TILE_LIMIT):
        vh, vl = split(jnp.concatenate([ref[:, columns] for ref in vector_refs], axis=0))
        ch, cl = split(slab_ref[:, columns])
        found = dot(jnp.concatenate([ch, cl], axis=0), vh, ROWS)
        total += found[:rows] + found[rows:] + dot(ch, vl, ROWS)
    total = jnp.concatenate([total[:, : nb // 4], total[:, nb // 4 :]], axis=0)
    out_ref[...] = jnp.concatenate([total[k * part : (k + 1) * part] for k in range(4)], axis=1)


def turn_kernel(size, *refs):
    factor_refs, out_ref = refs[:-1], refs[-1]
    nb, low = out_ref.shape[1], size // 4
    block = nb // size
    me = lax.axis_index("pcol")
    column = lax.broadcasted_iota(jnp.int32, (nb, nb), 1)
    place = column // block
    role = place // low
    swapped = ((role == 1) | (role == 2)) & (opposite(size) * (me % 2) == 1)
    bits = jnp.where(swapped, 3 - role, role) * low + place % low
    order = lax.broadcasted_iota(jnp.int32, (nb, nb), 0) == (bits ^ me) * block + column % block
    rows = [ref[p] for p in range(PANELS) for ref in factor_refs]
    out_ref[...] = exact(jnp.concatenate(rows, axis=0), order.astype(jnp.float32), PLAIN)


def share_kernel(terms, *refs):
    term_refs, turned_ref, inner_ref, share_ref = refs[:terms], *refs[terms:]
    group = share_ref.shape[0] // (1 + PANELS)
    total = term_refs[0][...]
    for ref in term_refs[1:]:
        total += ref[...]
    inner_ref[...] = total[:-group]
    share_ref[:group] = total[-group:]
    share_ref[group:] = turned_ref[...]


def from_place(value, q, block, lane):
    width = value.shape[1]
    bit = 1
    while bit * block < width:
        if q & bit:
            shift = bit * block
            ahead, behind = pltpu.roll(value, width - shift, 1), pltpu.roll(value, shift, 1)
            value = jnp.where((lane // shift) % 2 == 0, ahead, behind)
        bit *= 2
    return value


def matrices_kernel(*refs):
    share_refs, between_ref, triangle_refs = refs[:4], refs[4], refs[5:]
    nb = between_ref.shape[0]
    group = nb // 4
    lane = lax.broadcasted_iota(jnp.int32, (1, nb), 1)
    triangles = [[] for _ in range(PANELS)]
    for side in range(4):
        held = from_place(share_refs[side][...], side, group, lane)
        other = from_place(share_refs[side ^ 1][:group], side, group, lane)
        far = ((lane // group) ^ side) == 3
        between_ref[side * group : (side + 1) * group] = jnp.where(far, other, held[:group])
        for p in range(PANELS):
            triangles[p].append(held[(1 + p) * group : (2 + p) * group])
    for p in range(PANELS):
        triangle_refs[p][...] = jnp.concatenate(triangles[p], axis=0).T


def update_kernel(terms, *refs):
    near_ref, term_refs, (between_ref, first_ref, second_ref) = refs[0], refs[1 : 1 + terms], refs[1 + terms : 4 + terms]
    slab_ref, high_ref, low_ref, out_ref, after, sems = refs[4 + terms :]
    (rows, width), nb = slab_ref.shape, near_ref.shape[1]
    group = nb // 4

    total = term_refs[0][...]
    for ref in term_refs[1:]:
        total += ref[...]
    total = jnp.concatenate([total[:, k * group : (k + 1) * group] for k in range(4)], axis=0)
    total = near_ref[...] + jnp.concatenate([jnp.zeros((PANELS * rows, nb - group), jnp.float32), total], axis=1)
    scaled = exact(total[:rows], first_ref[...], PLAIN)
    inner = total[rows:] - exact(scaled, between_ref[...], PLAIN)
    later = exact(inner, second_ref[...], PLAIN)
    both = jnp.concatenate(split(jnp.concatenate([scaled, later], axis=1)), axis=0)

    copies = []
    for at, columns in enumerate(column_tiles(width, UNIT_LIMIT)):
        high, low = high_ref[:, columns], low_ref[:, columns]
        main = dot(both, high, PLAIN)
        rest = dot(both[:rows], low, PLAIN)
        after[:, columns] = slab_ref[:, columns] - (main[:rows] + main[rows:] + rest)
        copies.append(pltpu.make_async_copy(after.at[:, columns], out_ref.at[:, columns], sems.at[at]))
        copies[-1].start()
    for copy in copies:
        copy.wait()


def split_kernel(pieces, *refs):
    vector_refs, high_ref, low_ref = refs[:-2], *refs[-2:]
    for columns in column_tiles(high_ref.shape[1], UNIT_LIMIT):
        blocks = [vector_refs[ref][:, columns] if p is None else vector_refs[ref][p, :, columns] for ref, p in pieces]
        high_ref[:, columns], low_ref[:, columns] = split(jnp.concatenate(blocks, axis=0))


def products(kernel, arrays, *shapes):
    return pl.pallas_call(
        kernel,
        in_specs=[pl.BlockSpec(memory_space=pltpu.VMEM)] * len(arrays),
        out_specs=[pl.BlockSpec(memory_space=pltpu.VMEM)] * len(shapes),
        out_shape=[jax.ShapeDtypeStruct(shape, jnp.float32) for shape in shapes],
        compiler_params=pltpu.CompilerParams(vmem_limit_bytes=VMEM_LIMIT),
        cost_estimate=COST,
    )(*arrays)


def small(kernel, shapes, *arrays):
    return pl.pallas_call(
        kernel,
        out_shape=[jax.ShapeDtypeStruct(shape, jnp.float32) for shape in shapes],
        compiler_params=pltpu.CompilerParams(vmem_limit_bytes=SMALL_LIMIT),
        cost_estimate=COST,
    )(*arrays)


def update(near, terms, matrices, slab, parts):
    width = slab.shape[1]
    whole = [near, *terms, *matrices, slab, *parts]
    return pl.pallas_call(
        functools.partial(update_kernel, len(terms)),
        in_specs=[pl.BlockSpec(memory_space=pltpu.VMEM)] * len(whole),
        out_specs=pl.BlockSpec(memory_space=pl.ANY),
        out_shape=jax.ShapeDtypeStruct(slab.shape, jnp.float32),
        scratch_shapes=[
            pltpu.VMEM(slab.shape, jnp.float32),
            pltpu.SemaphoreType.DMA((len(column_tiles(width, UNIT_LIMIT)),)),
        ],
        compiler_params=pltpu.CompilerParams(vmem_limit_bytes=VMEM_LIMIT),
        cost_estimate=COST,
    )(*whole)


def opposite(size):
    return int(size > 4)


def exchange(array, partner, size, axis):
    return lax.ppermute(array, axis, [(i, i ^ partner(i)) for i in range(size)])


def summed_terms(value, depth, step):
    terms, reach = [value], 1
    while reach < depth:
        value = sum(terms[1:], terms[0])
        span = min(step, depth // reach)
        terms = [value] + [exchange(value, lambda i, k=k: k * reach, depth, "prow") for k in range(1, span)]
        reach *= span
    return terms


def over_rest(held, low, across):
    bit = 1
    while bit < low:
        for q, array in list(held.items()):
            turned = q // low in (1, 2) and bit == 1
            held[(q ^ (3 * low) if turned else q) | bit] = across(array, lambda i, bit=bit: bit)
        bit *= 2
    return held


def body(sizes, slab, reflectors, factors):
    size, depth = sizes["pcol"], sizes["prow"]
    rows = slab.shape[0]
    block, nb = factors.shape[1:]
    high, low = size // 2, size // 4
    across = functools.partial(exchange, size=size, axis="pcol")
    first = lambda i: high if opposite(size) * (i % 2) else low
    second = lambda i: low if opposite(size) * (i % 2) else high
    both = lambda i: high | low

    by_first, by_second = across(reflectors, first), across(reflectors, second)
    corner = [across(by_second[0], first), across(by_first[1], second)]
    near = over_rest({0: reflectors, low: by_first, high: by_second}, low, across)
    near = [near[q] for q in sorted(near)]
    group = over_rest({0: factors}, low, across)
    (turned,) = small(functools.partial(turn_kernel, size), [(PANELS * nb // 4, nb)], *[group[q] for q in sorted(group)])
    near, turned = lax.optimization_barrier((near, turned))
    (total,) = products(functools.partial(near_kernel, 0), [slab, *near], (2 * rows + nb // 4, nb))
    terms = summed_terms(total, depth, 4)
    terms, corner = lax.optimization_barrier((terms, corner))
    inner, share = small(
        functools.partial(share_kernel, len(terms)), [(2 * rows, nb), ((1 + PANELS) * nb // 4, nb)], *terms, turned
    )
    shares = [share, *(across(share, way) for way in (first, second, both))]
    far = [over_rest({high | low: array}, low, across) for array in corner]
    far = [held[q] for held in far for q in sorted(held)]
    matrices = small(matrices_kernel, [(nb, nb)] * (1 + PANELS), *shares)
    (found,) = products(corner_kernel, [slab, *far], (2 * rows // 4, nb))
    count, part = len(near), len(far) // PANELS
    pieces = [piece for p in range(PANELS) for piece in (*((at, p) for at in range(count)), *((count + p * part + at, None) for at in range(part)))]
    found, far = lax.optimization_barrier((found, far))
    parts = pl.pallas_call(
        functools.partial(split_kernel, pieces),
        in_specs=[pl.BlockSpec(memory_space=pltpu.VMEM)] * len([*near, *far]),
        out_specs=[pl.BlockSpec(memory_space=pltpu.VMEM)] * 2,
        out_shape=[jax.ShapeDtypeStruct((PANELS * nb, slab.shape[1]), jnp.bfloat16)] * 2,
        compiler_params=pltpu.CompilerParams(vmem_limit_bytes=SMALL_LIMIT),
        cost_estimate=pl.CostEstimate(flops=1, bytes_accessed=16 * PANELS * nb * slab.shape[1], transcendentals=0),
    )(*near, *far)
    return update(inner, summed_terms(found, depth, 4), matrices, slab, parts)


def solution(mesh):
    in_specs = (P("pcol", "prow"), P(None, "pcol", "prow"), P(None, "pcol", None))
    out_specs = P("pcol", "prow")
    return jax.shard_map(functools.partial(body, dict(mesh.shape)), mesh=mesh, in_specs=in_specs, out_specs=out_specs, check_vma=False)
```

```python
import functools

import jax
import jax.numpy as jnp
from jax import lax
from jax.experimental import pallas as pl
from jax.experimental.pallas import tpu as pltpu
from jax.sharding import PartitionSpec as P


UNIT_LIMIT = 2048
TILE_LIMIT = 8192
VMEM_LIMIT = 32 * 1024 * 1024
SMALL_LIMIT = 8 * 1024 * 1024
COST = pl.CostEstimate(flops=1, bytes_accessed=1, transcendentals=0)
PANELS = 2
ROWS = (((1,), (1,)), ((), ()))
PLAIN = (((1,), (0,)), ((), ()))


def divisor(width, limit):
    for unit in (128, 1):
        fits = [t for t in range(unit, min(limit, width) + 1, unit) if width % t == 0]
        if fits:
            return max(fits)
    return width


def split(value):
    high = value.astype(jnp.bfloat16)
    return high, (value - high.astype(jnp.float32)).astype(jnp.bfloat16)


def dot(left, right, dims):
    return lax.dot_general(left, right, dims, preferred_element_type=jnp.float32)


def exact(left, right, dims):
    return lax.dot_general(left, right, dims, precision=lax.Precision.HIGHEST, preferred_element_type=jnp.float32)


def column_tiles(width, limit):
    tile = divisor(width, limit)
    return [pl.ds(begin, tile) for begin in range(0, width, tile)]


def panel_rows(refs, panel, columns):
    return jnp.concatenate([ref[panel, :, columns] for ref in refs], axis=0)


def near_kernel(kept, slab_ref, *refs):
    vector_refs, out_ref, kept_refs = refs[: -1 - kept], refs[-1 - kept], refs[len(refs) - kept :]
    for ref, kept_ref in zip(vector_refs[1:], kept_refs):
        kept_ref[...] = ref[...]
    (rows, width), nb = slab_ref.shape, out_ref.shape[1]
    group = nb // 4
    total = 0
    for columns in column_tiles(width, TILE_LIMIT):
        (fh, fl), (sh, sl) = (split(panel_rows(vector_refs, p, columns)) for p in range(PANELS))
        ch, cl = split(slab_ref[:, columns])
        first = dot(jnp.concatenate([ch, cl], axis=0), fh, ROWS)
        first = first[:rows] + first[rows:] + dot(ch, fl, ROWS)
        high = jnp.concatenate([ch, fh[: 2 * group]], axis=0)
        low = jnp.concatenate([cl, fl[: 2 * group]], axis=0)
        second = dot(jnp.concatenate([high, low], axis=0), sh, ROWS)
        second = second[: high.shape[0]] + second[high.shape[0] :] + dot(high, sl, ROWS)
        total += jnp.concatenate([first, second], axis=0)
    inner, own, via = total[: 2 * rows], total[2 * rows : 2 * rows + group], total[2 * rows + group :]
    inner = jnp.concatenate([inner, jnp.zeros((2 * rows, group), jnp.float32)], axis=1)
    share = jnp.concatenate([own, via[:, 2 * group :]], axis=1)
    out_ref[...] = jnp.concatenate([inner, share], axis=0)


def corner_kernel(slab_ref, *refs):
    vector_refs, out_ref = refs[:-1], refs[-1]
    (rows, width), (part, nb) = slab_ref.shape, out_ref.shape
    total = 0
    for columns in column_tiles(width, TILE_LIMIT):
        vh, vl = split(jnp.concatenate([ref[:, columns] for ref in vector_refs], axis=0))
        ch, cl = split(slab_ref[:, columns])
        found = dot(jnp.concatenate([ch, cl], axis=0), vh, ROWS)
        total += found[:rows] + found[rows:] + dot(ch, vl, ROWS)
    total = jnp.concatenate([total[:, : nb // 4], total[:, nb // 4 :]], axis=0)
    out_ref[...] = jnp.concatenate([total[k * part : (k + 1) * part] for k in range(4)], axis=1)


def turn_kernel(size, *refs):
    factor_refs, out_ref = refs[:-1], refs[-1]
    nb, low = out_ref.shape[1], size // 4
    block = nb // size
    me = lax.axis_index("pcol")
    column = lax.broadcasted_iota(jnp.int32, (nb, nb), 1)
    place = column // block
    role = place // low
    swapped = ((role == 1) | (role == 2)) & (opposite(size) * (me % 2) == 1)
    bits = jnp.where(swapped, 3 - role, role) * low + place % low
    order = lax.broadcasted_iota(jnp.int32, (nb, nb), 0) == (bits ^ me) * block + column % block
    rows = [ref[p] for p in range(PANELS) for ref in factor_refs]
    out_ref[...] = exact(jnp.concatenate(rows, axis=0), order.astype(jnp.float32), PLAIN)


def share_kernel(terms, *refs):
    term_refs, turned_ref, inner_ref, share_ref = refs[:terms], *refs[terms:]
    group = share_ref.shape[0] // (1 + PANELS)
    total = term_refs[0][...]
    for ref in term_refs[1:]:
        total += ref[...]
    inner_ref[...] = total[:-group]
    share_ref[:group] = total[-group:]
    share_ref[group:] = turned_ref[...]


def from_place(value, q, block, lane):
    width = value.shape[1]
    bit = 1
    while bit * block < width:
        if q & bit:
            shift = bit * block
            ahead, behind = pltpu.roll(value, width - shift, 1), pltpu.roll(value, shift, 1)
            value = jnp.where((lane // shift) % 2 == 0, ahead, behind)
        bit *= 2
    return value


def matrices_kernel(*refs):
    share_refs, between_ref, triangle_refs = refs[:4], refs[4], refs[5:]
    nb = between_ref.shape[0]
    group = nb // 4
    lane = lax.broadcasted_iota(jnp.int32, (1, nb), 1)
    triangles = [[] for _ in range(PANELS)]
    for side in range(4):
        held = from_place(share_refs[side][...], side, group, lane)
        other = from_place(share_refs[side ^ 1][:group], side, group, lane)
        far = ((lane // group) ^ side) == 3
        between_ref[side * group : (side + 1) * group] = jnp.where(far, other, held[:group])
        for p in range(PANELS):
            triangles[p].append(held[(1 + p) * group : (2 + p) * group])
    for p in range(PANELS):
        triangle_refs[p][...] = jnp.concatenate(triangles[p], axis=0).T


def update_kernel(terms, *refs):
    near_ref, term_refs, (between_ref, first_ref, second_ref) = refs[0], refs[1 : 1 + terms], refs[1 + terms : 4 + terms]
    slab_ref, high_ref, low_ref, out_ref, after, sems = refs[4 + terms :]
    (rows, width), nb = slab_ref.shape, near_ref.shape[1]
    group = nb // 4

    total = term_refs[0][...]
    for ref in term_refs[1:]:
        total += ref[...]
    total = jnp.concatenate([total[:, k * group : (k + 1) * group] for k in range(4)], axis=0)
    total = near_ref[...] + jnp.concatenate([jnp.zeros((PANELS * rows, nb - group), jnp.float32), total], axis=1)
    scaled = exact(total[:rows], first_ref[...], PLAIN)
    inner = total[rows:] - exact(scaled, between_ref[...], PLAIN)
    later = exact(inner, second_ref[...], PLAIN)
    both = jnp.concatenate(split(jnp.concatenate([scaled, later], axis=1)), axis=0)

    copies = []
    for at, columns in enumerate(column_tiles(width, UNIT_LIMIT)):
        high, low = high_ref[:, columns], low_ref[:, columns]
        main = dot(both, high, PLAIN)
        rest = dot(both[:rows], low, PLAIN)
        after[:, columns] = slab_ref[:, columns] - (main[:rows] + main[rows:] + rest)
        copies.append(pltpu.make_async_copy(after.at[:, columns], out_ref.at[:, columns], sems.at[at]))
        copies[-1].start()
    for copy in copies:
        copy.wait()


def split_kernel(pieces, *refs):
    vector_refs, high_ref, low_ref = refs[:-2], *refs[-2:]
    for columns in column_tiles(high_ref.shape[1], UNIT_LIMIT):
        blocks = [vector_refs[ref][:, columns] if p is None else vector_refs[ref][p, :, columns] for ref, p in pieces]
        high_ref[:, columns], low_ref[:, columns] = split(jnp.concatenate(blocks, axis=0))


def products(kernel, arrays, *shapes):
    return pl.pallas_call(
        kernel,
        in_specs=[pl.BlockSpec(memory_space=pltpu.VMEM)] * len(arrays),
        out_specs=[pl.BlockSpec(memory_space=pltpu.VMEM)] * len(shapes),
        out_shape=[jax.ShapeDtypeStruct(shape, jnp.float32) for shape in shapes],
        compiler_params=pltpu.CompilerParams(vmem_limit_bytes=VMEM_LIMIT),
        cost_estimate=COST,
    )(*arrays)


def small(kernel, shapes, *arrays):
    return pl.pallas_call(
        kernel,
        out_shape=[jax.ShapeDtypeStruct(shape, jnp.float32) for shape in shapes],
        compiler_params=pltpu.CompilerParams(vmem_limit_bytes=SMALL_LIMIT),
        cost_estimate=COST,
    )(*arrays)


def update(near, terms, matrices, slab, parts):
    width = slab.shape[1]
    whole = [near, *terms, *matrices, slab, *parts]
    return pl.pallas_call(
        functools.partial(update_kernel, len(terms)),
        in_specs=[pl.BlockSpec(memory_space=pltpu.VMEM)] * len(whole),
        out_specs=pl.BlockSpec(memory_space=pl.ANY),
        out_shape=jax.ShapeDtypeStruct(slab.shape, jnp.float32),
        scratch_shapes=[
            pltpu.VMEM(slab.shape, jnp.float32),
            pltpu.SemaphoreType.DMA((len(column_tiles(width, UNIT_LIMIT)),)),
        ],
        compiler_params=pltpu.CompilerParams(vmem_limit_bytes=VMEM_LIMIT),
        cost_estimate=COST,
    )(*whole)


def opposite(size):
    return int(size > 4)


def exchange(array, partner, size, axis):
    return lax.ppermute(array, axis, [(i, i ^ partner(i)) for i in range(size)])


def summed_terms(value, depth, step, far_first=False):
    terms, reach = [value], 1
    while reach < depth:
        value = sum(terms[1:], terms[0])
        span = min(step, depth // reach)
        terms = [value] + [exchange(value, lambda i, k=k: k * reach, depth, "prow") for k in (reversed(range(1, span)) if far_first else range(1, span))]
        reach *= span
    return terms


def over_rest(held, low, across):
    bit = 1
    while bit < low:
        for q, array in list(held.items()):
            turned = q // low in (1, 2) and bit == 1
            held[(q ^ (3 * low) if turned else q) | bit] = across(array, lambda i, bit=bit: bit)
        bit *= 2
    return held


def body(sizes, slab, reflectors, factors):
    size, depth = sizes["pcol"], sizes["prow"]
    rows = slab.shape[0]
    block, nb = factors.shape[1:]
    high, low = size // 2, size // 4
    across = functools.partial(exchange, size=size, axis="pcol")
    first = lambda i: high if opposite(size) * (i % 2) else low
    second = lambda i: low if opposite(size) * (i % 2) else high
    both = lambda i: high | low

    by_first, by_second = across(reflectors, first), across(reflectors, second)
    corner = [across(by_second[0], first), across(by_first[1], second)]
    near = over_rest({0: reflectors, low: by_first, high: by_second}, low, across)
    near = [near[q] for q in sorted(near)]
    group = over_rest({0: factors}, low, across)
    (turned,) = small(functools.partial(turn_kernel, size), [(PANELS * nb // 4, nb)], *[group[q] for q in sorted(group)])
    near, turned = lax.optimization_barrier((near, turned))
    (total,) = products(functools.partial(near_kernel, 0), [slab, *near], (2 * rows + nb // 4, nb))
    terms = summed_terms(total, depth, 4)
    terms, corner = lax.optimization_barrier((terms, corner))
    inner, share = small(
        functools.partial(share_kernel, len(terms)), [(2 * rows, nb), ((1 + PANELS) * nb // 4, nb)], *terms, turned
    )
    shares = [share, *(across(share, way) for way in (first, second, both))]
    far = [over_rest({high | low: array}, low, across) for array in corner]
    far = [held[q] for held in far for q in sorted(held)]
    matrices = small(matrices_kernel, [(nb, nb)] * (1 + PANELS), *shares)
    (found,) = products(corner_kernel, [slab, *far], (2 * rows // 4, nb))
    count, part = len(near), len(far) // PANELS
    pieces = [piece for p in range(PANELS) for piece in (*((at, p) for at in range(count)), *((count + p * part + at, None) for at in range(part)))]
    found, far = lax.optimization_barrier((found, far))
    parts = pl.pallas_call(
        functools.partial(split_kernel, pieces),
        in_specs=[pl.BlockSpec(memory_space=pltpu.VMEM)] * len([*near, *far]),
        out_specs=[pl.BlockSpec(memory_space=pltpu.VMEM)] * 2,
        out_shape=[jax.ShapeDtypeStruct((PANELS * nb, slab.shape[1]), jnp.bfloat16)] * 2,
        compiler_params=pltpu.CompilerParams(vmem_limit_bytes=SMALL_LIMIT),
        cost_estimate=pl.CostEstimate(flops=1, bytes_accessed=16 * PANELS * nb * slab.shape[1], transcendentals=0),
    )(*near, *far)
    return update(inner, summed_terms(found, depth, 4, far_first=True), matrices, slab, parts)


def solution(mesh):
    in_specs = (P("pcol", "prow"), P(None, "pcol", "prow"), P(None, "pcol", None))
    out_specs = P("pcol", "prow")
    return jax.shard_map(functools.partial(body, dict(mesh.shape)), mesh=mesh, in_specs=in_specs, out_specs=out_specs, check_vma=False)
```

```python
import functools

import jax
import jax.numpy as jnp
from jax import lax
from jax.experimental import pallas as pl
from jax.experimental.pallas import tpu as pltpu
from jax.sharding import PartitionSpec as P


UNIT_LIMIT = 2048
TILE_LIMIT = 8192
VMEM_LIMIT = 32 * 1024 * 1024
SMALL_LIMIT = 8 * 1024 * 1024
COST = pl.CostEstimate(flops=1, bytes_accessed=1, transcendentals=0)
PANELS = 2
ROWS = (((1,), (1,)), ((), ()))
PLAIN = (((1,), (0,)), ((), ()))


def divisor(width, limit):
    for unit in (128, 1):
        fits = [t for t in range(unit, min(limit, width) + 1, unit) if width % t == 0]
        if fits:
            return max(fits)
    return width


def split(value):
    high = value.astype(jnp.bfloat16)
    return high, (value - high.astype(jnp.float32)).astype(jnp.bfloat16)


def dot(left, right, dims):
    return lax.dot_general(left, right, dims, preferred_element_type=jnp.float32)


def exact(left, right, dims):
    return lax.dot_general(left, right, dims, precision=lax.Precision.HIGHEST, preferred_element_type=jnp.float32)


def column_tiles(width, limit):
    tile = divisor(width, limit)
    return [pl.ds(begin, tile) for begin in range(0, width, tile)]


def panel_rows(refs, panel, columns):
    return jnp.concatenate([ref[panel, :, columns] for ref in refs], axis=0)


def near_kernel(kept, slab_ref, *refs):
    vector_refs, out_ref, kept_refs = refs[: -1 - kept], refs[-1 - kept], refs[len(refs) - kept :]
    for ref, kept_ref in zip(vector_refs[1:], kept_refs):
        kept_ref[...] = ref[...]
    (rows, width), nb = slab_ref.shape, out_ref.shape[1]
    group = nb // 4
    total = 0
    for columns in column_tiles(width, TILE_LIMIT):
        (fh, fl), (sh, sl) = (split(panel_rows(vector_refs, p, columns)) for p in range(PANELS))
        ch, cl = split(slab_ref[:, columns])
        first = dot(jnp.concatenate([ch, cl], axis=0), fh, ROWS)
        first = first[:rows] + first[rows:] + dot(ch, fl, ROWS)
        high = jnp.concatenate([ch, fh[: 2 * group]], axis=0)
        low = jnp.concatenate([cl, fl[: 2 * group]], axis=0)
        second = dot(jnp.concatenate([high, low], axis=0), sh, ROWS)
        second = second[: high.shape[0]] + second[high.shape[0] :] + dot(high, sl, ROWS)
        total += jnp.concatenate([first, second], axis=0)
    inner, own, via = total[: 2 * rows], total[2 * rows : 2 * rows + group], total[2 * rows + group :]
    inner = jnp.concatenate([inner, jnp.zeros((2 * rows, group), jnp.float32)], axis=1)
    share = jnp.concatenate([own, via[:, 2 * group :]], axis=1)
    out_ref[...] = jnp.concatenate([inner, share], axis=0)


def corner_kernel(slab_ref, *refs):
    vector_refs, out_ref = refs[:-1], refs[-1]
    (rows, width), (part, nb) = slab_ref.shape, out_ref.shape
    total = 0
    for columns in column_tiles(width, width):
        vh, vl = split(jnp.concatenate([ref[:, columns] for ref in vector_refs], axis=0))
        ch, cl = split(slab_ref[:, columns])
        found = dot(jnp.concatenate([ch, cl], axis=0), vh, ROWS)
        total += found[:rows] + found[rows:] + dot(ch, vl, ROWS)
    total = jnp.concatenate([total[:, : nb // 4], total[:, nb // 4 :]], axis=0)
    out_ref[...] = jnp.concatenate([total[k * part : (k + 1) * part] for k in range(4)], axis=1)


def turn_kernel(size, *refs):
    factor_refs, out_ref = refs[:-1], refs[-1]
    nb, low = out_ref.shape[1], size // 4
    block = nb // size
    me = lax.axis_index("pcol")
    column = lax.broadcasted_iota(jnp.int32, (nb, nb), 1)
    place = column // block
    role = place // low
    swapped = ((role == 1) | (role == 2)) & (opposite(size) * (me % 2) == 1)
    bits = jnp.where(swapped, 3 - role, role) * low + place % low
    order = lax.broadcasted_iota(jnp.int32, (nb, nb), 0) == (bits ^ me) * block + column % block
    rows = [ref[p] for p in range(PANELS) for ref in factor_refs]
    out_ref[...] = exact(jnp.concatenate(rows, axis=0), order.astype(jnp.float32), PLAIN)


def share_kernel(terms, *refs):
    term_refs, turned_ref, inner_ref, share_ref = refs[:terms], *refs[terms:]
    group = share_ref.shape[0] // (1 + PANELS)
    total = term_refs[0][...]
    for ref in term_refs[1:]:
        total += ref[...]
    inner_ref[...] = total[:-group]
    share_ref[:group] = total[-group:]
    share_ref[group:] = turned_ref[...]


def from_place(value, q, block, lane):
    width = value.shape[1]
    bit = 1
    while bit * block < width:
        if q & bit:
            shift = bit * block
            ahead, behind = pltpu.roll(value, width - shift, 1), pltpu.roll(value, shift, 1)
            value = jnp.where((lane // shift) % 2 == 0, ahead, behind)
        bit *= 2
    return value


def matrices_kernel(*refs):
    share_refs, between_ref, triangle_refs = refs[:4], refs[4], refs[5:]
    nb = between_ref.shape[1]
    group = nb // 4
    lane = lax.broadcasted_iota(jnp.int32, (1, nb), 1)
    between, triangles = [], [[] for _ in range(PANELS)]
    for side in range(4):
        held = from_place(share_refs[side][...], side, group, lane)
        other = from_place(share_refs[side ^ 1][:group], side, group, lane)
        far = ((lane // group) ^ side) == 3
        between.append(jnp.where(far, other, held[:group]))
        for p in range(PANELS):
            triangles[p].append(held[(1 + p) * group : (2 + p) * group])
    between_ref[...] = jnp.concatenate(split(jnp.concatenate(between, axis=0)), axis=0)
    for p in range(PANELS):
        triangle_refs[p][...] = jnp.concatenate(split(jnp.concatenate(triangles[p], axis=0).T), axis=0)


def times(left, parts):
    rows, depth = left.shape
    high, low = split(left)
    main = dot(jnp.concatenate([high, low], axis=0), parts[:depth], PLAIN)
    return main[:rows] + (main[rows:] + dot(high, parts[depth:], PLAIN))


def update_kernel(pieces, terms, *refs):
    near_ref, term_refs, (between_ref, first_ref, second_ref) = refs[0], refs[1 : 1 + terms], refs[1 + terms : 4 + terms]
    slab_ref, *vector_refs = refs[4 + terms : -3]
    out_ref, after, sems = refs[-3:]
    (rows, width), nb = slab_ref.shape, near_ref.shape[1]
    group = nb // 4

    total = term_refs[0][...]
    for ref in term_refs[1:]:
        total += ref[...]
    total = jnp.concatenate([total[:, k * group : (k + 1) * group] for k in range(4)], axis=0)
    total = near_ref[...] + jnp.concatenate([jnp.zeros((PANELS * rows, nb - group), jnp.float32), total], axis=1)
    scaled = times(total[:rows], first_ref[...])
    inner = total[rows:] - times(scaled, between_ref[...])
    later = times(inner, second_ref[...])
    both = jnp.concatenate(split(jnp.concatenate([scaled, later], axis=1)), axis=0)

    copies = []
    for at, columns in enumerate(column_tiles(width, UNIT_LIMIT)):
        blocks = [vector_refs[ref][:, columns] if p is None else vector_refs[ref][p, :, columns] for ref, p in pieces]
        high, low = split(jnp.concatenate(blocks, axis=0))
        main = dot(both, high, PLAIN)
        rest = dot(both[:rows], low, PLAIN)
        after[:, columns] = slab_ref[:, columns] - (main[:rows] + main[rows:] + rest)
        copies.append(pltpu.make_async_copy(after.at[:, columns], out_ref.at[:, columns], sems.at[at]))
        copies[-1].start()
    for copy in copies:
        copy.wait()


def products(kernel, arrays, *shapes):
    return pl.pallas_call(
        kernel,
        in_specs=[pl.BlockSpec(memory_space=pltpu.VMEM)] * len(arrays),
        out_specs=[pl.BlockSpec(memory_space=pltpu.VMEM)] * len(shapes),
        out_shape=[jax.ShapeDtypeStruct(shape, jnp.float32) for shape in shapes],
        compiler_params=pltpu.CompilerParams(vmem_limit_bytes=VMEM_LIMIT),
        cost_estimate=COST,
    )(*arrays)


def small(kernel, shapes, *arrays, kind=jnp.float32):
    return pl.pallas_call(
        kernel,
        out_shape=[jax.ShapeDtypeStruct(shape, kind) for shape in shapes],
        compiler_params=pltpu.CompilerParams(vmem_limit_bytes=SMALL_LIMIT),
        cost_estimate=COST,
    )(*arrays)


def update(near, terms, matrices, slab, arrays, pieces):
    width = slab.shape[1]
    whole = [near, *terms, *matrices, slab, *arrays]
    return pl.pallas_call(
        functools.partial(update_kernel, pieces, len(terms)),
        in_specs=[pl.BlockSpec(memory_space=pltpu.VMEM)] * len(whole),
        out_specs=pl.BlockSpec(memory_space=pl.ANY),
        out_shape=jax.ShapeDtypeStruct(slab.shape, jnp.float32),
        scratch_shapes=[
            pltpu.VMEM(slab.shape, jnp.float32),
            pltpu.SemaphoreType.DMA((len(column_tiles(width, UNIT_LIMIT)),)),
        ],
        compiler_params=pltpu.CompilerParams(vmem_limit_bytes=VMEM_LIMIT),
        cost_estimate=COST,
    )(*whole)


def opposite(size):
    return int(size > 4)


def exchange(array, partner, size, axis):
    return lax.ppermute(array, axis, [(i, i ^ partner(i)) for i in range(size)])


def summed_terms(value, depth, step):
    terms, reach = [value], 1
    while reach < depth:
        value = sum(terms[1:], terms[0])
        span = min(step, depth // reach)
        steps = sorted(range(1, span), key=lambda k: (k != 1, k != span - 1))
        terms = [value] + [exchange(value, lambda i, k=k: k * reach, depth, "prow") for k in steps]
        reach *= span
    return terms


def over_rest(held, low, across):
    bit = 1
    while bit < low:
        for q, array in list(held.items()):
            turned = q // low in (1, 2) and bit == 1
            held[(q ^ (3 * low) if turned else q) | bit] = across(array, lambda i, bit=bit: bit)
        bit *= 2
    return held


def body(sizes, slab, reflectors, factors):
    size, depth = sizes["pcol"], sizes["prow"]
    rows = slab.shape[0]
    block, nb = factors.shape[1:]
    high, low = size // 2, size // 4
    across = functools.partial(exchange, size=size, axis="pcol")
    first = lambda i: high if opposite(size) * (i % 2) else low
    second = lambda i: low if opposite(size) * (i % 2) else high
    both = lambda i: high | low

    by_first, by_second = across(reflectors, first), across(reflectors, second)
    corner = [across(by_second[0], first), across(by_first[1], second)]
    near = over_rest({0: reflectors, low: by_first, high: by_second}, low, across)
    near = [near[q] for q in sorted(near)]
    group = over_rest({0: factors}, low, across)
    (turned,) = small(functools.partial(turn_kernel, size), [(PANELS * nb // 4, nb)], *[group[q] for q in sorted(group)])
    near, turned = lax.optimization_barrier((near, turned))
    (total,) = products(functools.partial(near_kernel, 0), [slab, *near], (2 * rows + nb // 4, nb))
    terms = summed_terms(total, depth, 4)
    terms, corner = lax.optimization_barrier((terms, corner))
    inner, share = small(
        functools.partial(share_kernel, len(terms)), [(2 * rows, nb), ((1 + PANELS) * nb // 4, nb)], *terms, turned
    )
    shares = [share, *(across(share, way) for way in (first, second, both))]
    far = [over_rest({high | low: array}, low, across) for array in corner]
    far = [held[q] for held in far for q in sorted(held)]
    matrices = small(matrices_kernel, [(2 * nb, nb)] * (1 + PANELS), *shares, kind=jnp.bfloat16)
    (found,) = products(corner_kernel, [slab, *far], (2 * rows // 4, nb))
    count, part = len(near), len(far) // PANELS
    pieces = [piece for p in range(PANELS) for piece in (*((at, p) for at in range(count)), *((count + p * part + at, None) for at in range(part)))]
    return update(inner, summed_terms(found, depth, 4), matrices, slab, [*near, *far], pieces)


def solution(mesh):
    in_specs = (P("pcol", "prow"), P(None, "pcol", "prow"), P(None, "pcol", None))
    out_specs = P("pcol", "prow")
    return jax.shard_map(functools.partial(body, dict(mesh.shape)), mesh=mesh, in_specs=in_specs, out_specs=out_specs, check_vma=False)
```
